32 devices in a mesh: dp: 8 (over y, x, core), ctx: 4 (over z).
Axes of the slice: x: 2, y: 2, z: 4, core: 2. Of those that a mesh axis runs over, the one named last changes fastest.
Arguments:
- queries: bfloat16 [4608, 2048], P(('dp', 'ctx')), parts along dimension 0, may hold values from -40 to 40
- keys: bfloat16 [4608, 2048], P(('dp', 'ctx')), parts along dimension 0, may hold values from -40 to 40
- values: bfloat16 [4608, 2048], P(('dp', 'ctx')), parts along dimension 0, may hold values from -6 to 6
- span_starts: int32 [8], P('dp'), parts along dimension 0, may hold values from 0 to 288, as said below
Outputs:
- attended: bfloat16 [4608, 2048], P(('dp', 'ctx')), parts along dimension 0
The draws below stay inside these ranges and needn't reach their ends.
There are 8 independent parts, one for each index of `dp`. The reference program is written for one: setup_inputs(seed, part) draws one part's arguments, and reference() takes and returns one part's arrays. A program takes and returns all parts, laid end to end along the dimension named above; each array names one. Nothing has to cross between parts.
Inputs may be any that keep to these rules, and one draw needn't show every extreme that they name: `span_starts`: starts rise, and the 1 spans of 288 positions lie inside the document without intersecting.
All inputs are finite; a program needn't handle non-finite values.
Results may differ from the reference program's by a relative error of at most 0.0045.
Values may be sent and summed in bfloat16 or wider, within the bound.
A program may use at most 128 MiB of HBM per device.

```python
import jax
import jax.numpy as jnp
from jax import lax

HEADS = 16
HD = 128
LENGTH = 576
SPAN = 288
IMAGES = 1


def draw_queries(key, part):
    base = jax.random.truncated_normal(jax.random.fold_in(key, 1), -6.0, 6.0, (LENGTH, HEADS * HD), jnp.float32)
    return base.astype(jnp.bfloat16)


def draw_keys(key, part):
    base = jax.random.truncated_normal(jax.random.fold_in(key, 2), -6.0, 6.0, (LENGTH, HEADS * HD), jnp.float32)
    return base.astype(jnp.bfloat16)


def draw_span_starts(key, part):
    span_count = IMAGES
    spare = LENGTH - span_count * SPAN
    gaps = jnp.sort(jax.random.randint(jax.random.fold_in(key, 4), (span_count,), 0, spare + 1))
    return (jnp.arange(span_count, dtype=jnp.int32) * SPAN + gaps).astype(jnp.int32)


def steps_of(stream_key, extent, split, least, top_value):
    def one(axis_at, parts):
        steps = jax.random.uniform(jax.random.fold_in(jax.random.fold_in(stream_key, 6), axis_at), (parts,), jnp.float32, least / len(split), top_value / len(split))
        return jnp.repeat(jnp.exp(steps), extent[axis_at] // parts).reshape((-1,) + (1,) * (len(extent) - axis_at - 1))

    level = one(*split[0])
    for cut in split[1:]:
        level = level * one(*cut)
    return level


def gaussian(own_key, dims, scale, limit, cuts=(), kind=jnp.bfloat16):
    entries = jax.random.normal(own_key, dims, jnp.float32) * scale
    if len(cuts) > 0:
        entries = steps_of(own_key, dims, cuts, -0.22, 0.18) * entries
    return jnp.clip(entries, min=-limit, max=limit).astype(kind)


def setup_inputs(seed: int = 0, part: int = 0) -> dict:
    key_of = jax.random.split(jax.random.key(seed), 5)
    own_keys = jax.random.split(jax.random.fold_in(key_of[4], part), 5)
    return {
        "queries": draw_queries(jax.random.fold_in(jax.random.fold_in(key_of[4], part), 71), part),
        "keys": draw_keys(jax.random.fold_in(jax.random.fold_in(key_of[4], part), 71), part),
        "values": gaussian(own_keys[2], (LENGTH, HEADS * HD), 1.0, 6.0, ((0, 4),)),
        "span_starts": draw_span_starts(jax.random.fold_in(jax.random.fold_in(key_of[4], part), 71), part),
    }


def span_number(positions, span_starts):
    span_count = span_starts.shape[0]
    inside = (positions[:, None] >= span_starts[None, :]) & (positions[:, None] < span_starts[None, :] + SPAN)
    labels = (jnp.arange(span_count, dtype=jnp.int32) + 1).astype(jnp.int32)
    return jnp.sum(jnp.where(inside, labels[None, :], 0), axis=1).astype(jnp.int32)


def reference(queries, keys, values, span_starts):
    positions = jnp.arange(LENGTH, dtype=jnp.int32)
    span_id = span_number(positions, span_starts)
    visible = (positions[None, :] <= positions[:, None]) | ((span_id[:, None] == span_id[None, :]) & (span_id[:, None] > 0))
    score_scale = HD ** -0.5
    query_heads = queries.reshape(LENGTH, HEADS, HD).transpose(1, 0, 2)
    key_heads = keys.reshape(LENGTH, HEADS, HD).transpose(1, 0, 2)
    value_heads = values.reshape(LENGTH, HEADS, HD).transpose(1, 0, 2)

    def one_head(operands):
        query_h, key_h, value_h = operands
        scores = jnp.dot(query_h, key_h.T, preferred_element_type=jnp.float32) * score_scale
        masked = jnp.where(visible, scores, -jnp.inf)
        row_max = jnp.max(masked, axis=1, keepdims=True)
        weights = jnp.where(visible, jnp.exp(scores - row_max), 0.0)
        total = jnp.sum(weights, axis=1, keepdims=True)
        return jnp.dot(weights.astype(jnp.bfloat16), value_h, preferred_element_type=jnp.float32) / total

    result = lax.map(one_head, (query_heads, key_heads, value_heads))
    return result.transpose(1, 0, 2).reshape(LENGTH, HEADS * HD).astype(jnp.bfloat16)
```

```python
import functools
import math

import jax
import jax.numpy as jnp
from jax import lax
from jax.experimental import pallas as pl
from jax.experimental.pallas import tpu as pltpu
from jax.sharding import PartitionSpec as P

HEADS = 16
HD = 128
SPAN = 288


def shifted(value, axis, steps):
    count = lax.axis_size(axis)
    pairs = [(source, (source + steps) % count) for source in range(count)]
    return lax.ppermute(value, axis, pairs)


def span_number(positions, span_starts):
    span_count = span_starts.shape[0]
    inside = (positions[:, None] >= span_starts[None, :]) & (
        positions[:, None] < span_starts[None, :] + SPAN
    )
    labels = jnp.arange(span_count, dtype=jnp.int32) + 1
    return jnp.sum(jnp.where(inside, labels[None, :], 0), axis=1)


def fold_block(operands):
    state_now, visible, group_query, key_heads, value_heads = operands
    row_max, row_sum, weighted = state_now
    scores = jnp.einsum(
        "qhd,khd->hqk", group_query, key_heads, preferred_element_type=jnp.float32
    ) * HD ** (-0.5)
    scores = jnp.where(visible[None], scores, -1e30)
    new_max = jnp.maximum(row_max, jnp.max(scores, axis=2))
    rescale = jnp.exp(row_max - new_max)
    weights = jnp.where(visible[None], jnp.exp(scores - new_max[:, :, None]), 0.0)
    new_sum = row_sum * rescale + jnp.sum(weights, axis=2)
    products = jnp.einsum(
        "hqk,khd->qhd",
        weights.astype(jnp.bfloat16),
        value_heads,
        preferred_element_type=jnp.float32,
    )
    new_weighted = weighted * rescale.T[:, :, None] + products
    return (new_max, new_sum, new_weighted)


def keep_block(operands):
    return operands[0]


def ring_body(queries, keys, values, span_starts):
    tok_rows = queries.shape[0]
    row_width = queries.shape[1]
    loop_size = lax.axis_size("ctx")
    loop_index = lax.axis_index("ctx")
    local_rows = jnp.arange(tok_rows, dtype=jnp.int32)
    query_pos = loop_index * tok_rows + local_rows
    query_span = span_number(query_pos, span_starts)
    query_heads = queries.reshape(tok_rows, HEADS, HD)
    group_count = 2
    group_rows = tok_rows // group_count
    empty_state = tuple(
        (
            (
                jnp.full((HEADS, group_rows), -1e30, jnp.float32),
                jnp.zeros((HEADS, group_rows), jnp.float32),
                jnp.zeros((group_rows, HEADS, HD), jnp.float32),
            )
            for number in range(group_count)
        )
    )

    def absorb(running, block_pair, key_start):
        key_block, value_block = block_pair
        block_rows = key_block.shape[0]
        key_pos = key_start + jnp.arange(block_rows, dtype=jnp.int32)
        key_span = span_number(key_pos, span_starts)
        key_heads = key_block.reshape(block_rows, HEADS, HD)
        value_heads = value_block.reshape(block_rows, HEADS, HD)
        updated = []
        for group_index in range(group_count):
            row_start = group_index * group_rows
            group_pos = query_pos[row_start : row_start + group_rows]
            group_span = query_span[row_start : row_start + group_rows]
            group_query = query_heads[row_start : row_start + group_rows]
            visible = (key_pos[None, :] <= group_pos[:, None]) | (
                group_span[:, None] == key_span[None, :]
            ) & (group_span[:, None] > 0)
            operands = (running[group_index], visible, group_query, key_heads, value_heads)
            updated.append(lax.cond(jnp.any(visible), fold_block, keep_block, operands))
        return tuple(updated)

    stacked = jnp.stack([keys, values])
    own_state = absorb(empty_state, (keys, values), loop_index * tok_rows)

    def advance(step_index, loop_state):
        running, upward, downward = loop_state
        upward = shifted(upward, "ctx", 1)
        downward = shifted(downward, "ctx", -1)
        source_up = (loop_index - 1 - step_index) % loop_size
        source_down = (loop_index + 1 + step_index) % loop_size
        running = absorb(running, (upward[0], upward[1]), source_up * tok_rows)
        running = absorb(running, (downward[0], downward[1]), source_down * tok_rows)
        return (running, upward, downward)

    final_state, upward, downward = lax.fori_loop(
        0, (loop_size - 1) // 2, advance, (own_state, stacked, stacked)
    )
    upward = shifted(upward, "ctx", 1)
    source_last = (loop_index - loop_size // 2) % loop_size
    final_state = absorb(final_state, (upward[0], upward[1]), source_last * tok_rows)
    pieces = [weighted / row_sum.T[:, :, None] for row_max, row_sum, weighted in final_state]
    attended = jnp.concatenate(pieces, axis=0).reshape(tok_rows, row_width).astype(jnp.bfloat16)
    return attended


def exchange_kernel(
    count, images, starts_ref, q_ref, k_ref, v_ref, out_ref,
    q_all, k_all, v_all, o_all, bias,
    in_send, in_recv, in_local, out_send, out_recv, out_local,
):
    me = lax.axis_index("ctx")
    rows = q_ref.shape[0]
    length = rows * count
    own_heads = HEADS // count
    half = count // 2
    side = me // half
    far = [(1 - side) * half + (me + i) % half for i in range(half)]
    near = [side * half + (me + i) % half for i in range(1, half)]
    peers = far + near
    my_rows = pl.ds(pl.multiple_of(me * rows, rows), rows)
    sources = (q_ref, k_ref, v_ref)
    landing = (q_all, k_all, v_all)

    def columns(owner, head):
        return pl.ds(pl.multiple_of((owner * own_heads + head) * HD, HD), HD)

    def rows_of(device):
        return pl.ds(pl.multiple_of(device * rows, rows), rows)

    def operand_copy(which, head, peer):
        return pltpu.make_async_remote_copy(
            src_ref=sources[which].at[:, columns(peer, head)],
            dst_ref=landing[which].at[head, my_rows, :],
            send_sem=in_send.at[which, head, peer],
            recv_sem=in_recv.at[which, head, me],
            device_id={"ctx": peer},
            device_id_type=pl.DeviceIdType.MESH,
        )

    def operand_arrival(which, head, peer):
        return pltpu.make_async_remote_copy(
            src_ref=sources[which].at[:, columns(peer, head)],
            dst_ref=landing[which].at[head, rows_of(peer), :],
            send_sem=in_send.at[which, head, peer],
            recv_sem=in_recv.at[which, head, peer],
            device_id={"ctx": peer},
            device_id_type=pl.DeviceIdType.MESH,
        )

    def operand_local(which, head):
        return pltpu.make_async_copy(
            sources[which].at[:, columns(me, head)],
            landing[which].at[head, my_rows, :],
            in_local.at[which, head],
        )

    def result_copy(head, peer):
        return pltpu.make_async_remote_copy(
            src_ref=o_all.at[head, rows_of(peer), :],
            dst_ref=out_ref.at[:, columns(me, head)],
            send_sem=out_send.at[head, peer],
            recv_sem=out_recv.at[head, me],
            device_id={"ctx": peer},
            device_id_type=pl.DeviceIdType.MESH,
        )

    def result_arrival(head, peer):
        return pltpu.make_async_remote_copy(
            src_ref=o_all.at[head, rows_of(peer), :],
            dst_ref=out_ref.at[:, columns(peer, head)],
            send_sem=out_send.at[head, peer],
            recv_sem=out_recv.at[head, peer],
            device_id={"ctx": peer},
            device_id_type=pl.DeviceIdType.MESH,
        )

    def result_local(head):
        return pltpu.make_async_copy(
            o_all.at[head, my_rows, :], out_ref.at[:, columns(me, head)], out_local.at[head]
        )

    barrier = pltpu.get_barrier_semaphore()
    for peer in peers:
        pl.semaphore_signal(
            barrier, inc=1, device_id={"ctx": peer}, device_id_type=pl.DeviceIdType.MESH
        )
    pl.semaphore_wait(barrier, count - 1)

    def send_head(head, carry):
        for peer in peers:
            for which in range(3):
                operand_copy(which, head, peer).start()
        for which in range(3):
            operand_local(which, head).start()
        return carry

    lax.fori_loop(0, own_heads, send_head, 0)

    query_pos = lax.broadcasted_iota(jnp.int32, (length, length), 0)
    key_pos = lax.broadcasted_iota(jnp.int32, (length, length), 1)
    visible = key_pos <= query_pos
    for image in range(images):
        first = starts_ref[image]
        inside = (
            (query_pos >= first) & (query_pos < first + SPAN)
            & (key_pos >= first) & (key_pos < first + SPAN)
        )
        visible = visible | inside
    bias[...] = jnp.where(visible, 0.0, -1e30)

    def attend_head(head, carry):
        for which in range(3):
            operand_local(which, head).wait()
            for peer in peers:
                operand_arrival(which, head, peer).wait_recv()
        scores = lax.dot_general(
            q_all[head], k_all[head], (((1,), (1,)), ((), ())),
            preferred_element_type=jnp.float32,
        ) * (HD ** (-0.5) * math.log2(math.e))
        scores = scores + bias[...]
        weights = jnp.exp2(scores - jnp.max(scores, axis=1, keepdims=True))
        total = jnp.sum(weights, axis=1, keepdims=True)
        mixed = jnp.dot(
            weights.astype(jnp.bfloat16), v_all[head], preferred_element_type=jnp.float32
        )
        o_all[head] = (mixed / total).astype(jnp.bfloat16)
        for peer in peers:
            result_copy(head, peer).start()
        result_local(head).start()
        return carry

    lax.fori_loop(0, own_heads, attend_head, 0)

    def finish_head(head, carry):
        result_local(head).wait()
        for peer in peers:
            for which in range(3):
                operand_copy(which, head, peer).wait_send()
            result_copy(head, peer).wait_send()
            result_arrival(head, peer).wait_recv()
        return carry

    lax.fori_loop(0, own_heads, finish_head, 0)


def exchange_body(count, queries, keys, values, span_starts):
    rows = queries.shape[0]
    length = rows * count
    own_heads = HEADS // count
    images = span_starts.shape[0]
    everything = pl.BlockSpec(memory_space=pl.ANY)
    return pl.pallas_call(
        functools.partial(exchange_kernel, count, images),
        out_shape=jax.ShapeDtypeStruct(queries.shape, jnp.bfloat16),
        in_specs=[pl.BlockSpec(memory_space=pltpu.SMEM), everything, everything, everything],
        out_specs=everything,
        scratch_shapes=[pltpu.VMEM((own_heads, length, HD), jnp.bfloat16)] * 4
        + [
            pltpu.VMEM((length, length), jnp.float32),
            pltpu.SemaphoreType.DMA((3, own_heads, count)),
            pltpu.SemaphoreType.DMA((3, own_heads, count)),
            pltpu.SemaphoreType.DMA((3, own_heads)),
            pltpu.SemaphoreType.DMA((own_heads, count)),
            pltpu.SemaphoreType.DMA((own_heads, count)),
            pltpu.SemaphoreType.DMA((own_heads,)),
        ],
        compiler_params=pltpu.CompilerParams(
            collective_id=0, has_side_effects=True, vmem_limit_bytes=32 * 1024 * 1024
        ),
    )(span_starts, queries, keys, values)


def solution(mesh):
    count = mesh.shape["ctx"]
    fits = count % 2 == 0 and HEADS % count == 0
    body = functools.partial(exchange_body, count) if fits else ring_body
    placed = (P(("dp", "ctx"), None), P(("dp", "ctx"), None), P(("dp", "ctx"), None), P("dp"))
    return jax.shard_map(
        body, mesh=mesh, in_specs=placed, out_specs=P(("dp", "ctx"), None), check_vma=False
    )
```

```python
import functools
import math

import jax
import jax.numpy as jnp
from jax import lax
from jax.experimental import pallas as pl
from jax.experimental.pallas import tpu as pltpu
from jax.sharding import PartitionSpec as P

HEADS = 16
HD = 128
SPAN = 288


def shifted(value, axis, steps):
    count = lax.axis_size(axis)
    pairs = [(source, (source + steps) % count) for source in range(count)]
    return lax.ppermute(value, axis, pairs)


def span_number(positions, span_starts):
    span_count = span_starts.shape[0]
    inside = (positions[:, None] >= span_starts[None, :]) & (
        positions[:, None] < span_starts[None, :] + SPAN
    )
    labels = jnp.arange(span_count, dtype=jnp.int32) + 1
    return jnp.sum(jnp.where(inside, labels[None, :], 0), axis=1)


def fold_block(operands):
    state_now, visible, group_query, key_heads, value_heads = operands
    row_max, row_sum, weighted = state_now
    scores = jnp.einsum(
        "qhd,khd->hqk", group_query, key_heads, preferred_element_type=jnp.float32
    ) * HD ** (-0.5)
    scores = jnp.where(visible[None], scores, -1e30)
    new_max = jnp.maximum(row_max, jnp.max(scores, axis=2))
    rescale = jnp.exp(row_max - new_max)
    weights = jnp.where(visible[None], jnp.exp(scores - new_max[:, :, None]), 0.0)
    new_sum = row_sum * rescale + jnp.sum(weights, axis=2)
    products = jnp.einsum(
        "hqk,khd->qhd",
        weights.astype(jnp.bfloat16),
        value_heads,
        preferred_element_type=jnp.float32,
    )
    new_weighted = weighted * rescale.T[:, :, None] + products
    return (new_max, new_sum, new_weighted)


def keep_block(operands):
    return operands[0]


def ring_body(queries, keys, values, span_starts):
    tok_rows = queries.shape[0]
    row_width = queries.shape[1]
    loop_size = lax.axis_size("ctx")
    loop_index = lax.axis_index("ctx")
    local_rows = jnp.arange(tok_rows, dtype=jnp.int32)
    query_pos = loop_index * tok_rows + local_rows
    query_span = span_number(query_pos, span_starts)
    query_heads = queries.reshape(tok_rows, HEADS, HD)
    group_count = 2
    group_rows = tok_rows // group_count
    empty_state = tuple(
        (
            (
                jnp.full((HEADS, group_rows), -1e30, jnp.float32),
                jnp.zeros((HEADS, group_rows), jnp.float32),
                jnp.zeros((group_rows, HEADS, HD), jnp.float32),
            )
            for number in range(group_count)
        )
    )

    def absorb(running, block_pair, key_start):
        key_block, value_block = block_pair
        block_rows = key_block.shape[0]
        key_pos = key_start + jnp.arange(block_rows, dtype=jnp.int32)
        key_span = span_number(key_pos, span_starts)
        key_heads = key_block.reshape(block_rows, HEADS, HD)
        value_heads = value_block.reshape(block_rows, HEADS, HD)
        updated = []
        for group_index in range(group_count):
            row_start = group_index * group_rows
            group_pos = query_pos[row_start : row_start + group_rows]
            group_span = query_span[row_start : row_start + group_rows]
            group_query = query_heads[row_start : row_start + group_rows]
            visible = (key_pos[None, :] <= group_pos[:, None]) | (
                group_span[:, None] == key_span[None, :]
            ) & (group_span[:, None] > 0)
            operands = (running[group_index], visible, group_query, key_heads, value_heads)
            updated.append(lax.cond(jnp.any(visible), fold_block, keep_block, operands))
        return tuple(updated)

    stacked = jnp.stack([keys, values])
    own_state = absorb(empty_state, (keys, values), loop_index * tok_rows)

    def advance(step_index, loop_state):
        running, upward, downward = loop_state
        upward = shifted(upward, "ctx", 1)
        downward = shifted(downward, "ctx", -1)
        source_up = (loop_index - 1 - step_index) % loop_size
        source_down = (loop_index + 1 + step_index) % loop_size
        running = absorb(running, (upward[0], upward[1]), source_up * tok_rows)
        running = absorb(running, (downward[0], downward[1]), source_down * tok_rows)
        return (running, upward, downward)

    final_state, upward, downward = lax.fori_loop(
        0, (loop_size - 1) // 2, advance, (own_state, stacked, stacked)
    )
    upward = shifted(upward, "ctx", 1)
    source_last = (loop_index - loop_size // 2) % loop_size
    final_state = absorb(final_state, (upward[0], upward[1]), source_last * tok_rows)
    pieces = [weighted / row_sum.T[:, :, None] for row_max, row_sum, weighted in final_state]
    attended = jnp.concatenate(pieces, axis=0).reshape(tok_rows, row_width).astype(jnp.bfloat16)
    return attended


def exchange_kernel(
    count, images, starts_ref, q_ref, k_ref, v_ref, out_ref,
    q_all, k_all, v_all, o_all, bias,
    in_send, in_recv, in_local, out_send, out_recv, out_local,
):
    me = lax.axis_index("ctx")
    rows = q_ref.shape[0]
    length = rows * count
    own_heads = HEADS // count
    half = count // 2
    side = me // half
    far = [(1 - side) * half + (me + i) % half for i in range(half)]
    near = [side * half + (me + i) % half for i in range(1, half)]
    peers = far + near
    my_rows = pl.ds(pl.multiple_of(me * rows, rows), rows)
    sources = (q_ref, k_ref, v_ref)
    landing = (q_all, k_all, v_all)

    def columns(owner, head):
        return pl.ds(pl.multiple_of((owner * own_heads + head) * HD, HD), HD)

    def rows_of(device):
        return pl.ds(pl.multiple_of(device * rows, rows), rows)

    def operand_copy(which, head, peer):
        return pltpu.make_async_remote_copy(
            src_ref=sources[which].at[:, columns(peer, head)],
            dst_ref=landing[which].at[head, my_rows, :],
            send_sem=in_send.at[which, head, peer],
            recv_sem=in_recv.at[which, head, me],
            device_id={"ctx": peer},
            device_id_type=pl.DeviceIdType.MESH,
        )

    def operand_arrival(which, head, peer):
        return pltpu.make_async_remote_copy(
            src_ref=sources[which].at[:, columns(peer, head)],
            dst_ref=landing[which].at[head, rows_of(peer), :],
            send_sem=in_send.at[which, head, peer],
            recv_sem=in_recv.at[which, head, peer],
            device_id={"ctx": peer},
            device_id_type=pl.DeviceIdType.MESH,
        )

    def operand_local(which, head):
        return pltpu.make_async_copy(
            sources[which].at[:, columns(me, head)],
            landing[which].at[head, my_rows, :],
            in_local.at[which, head],
        )

    def result_copy(head, peer):
        return pltpu.make_async_remote_copy(
            src_ref=o_all.at[head, rows_of(peer), :],
            dst_ref=out_ref.at[:, columns(me, head)],
            send_sem=out_send.at[head, peer],
            recv_sem=out_recv.at[head, me],
            device_id={"ctx": peer},
            device_id_type=pl.DeviceIdType.MESH,
        )

    def result_arrival(head, peer):
        return pltpu.make_async_remote_copy(
            src_ref=o_all.at[head, rows_of(peer), :],
            dst_ref=out_ref.at[:, columns(peer, head)],
            send_sem=out_send.at[head, peer],
            recv_sem=out_recv.at[head, peer],
            device_id={"ctx": peer},
            device_id_type=pl.DeviceIdType.MESH,
        )

    def result_local(head):
        return pltpu.make_async_copy(
            o_all.at[head, my_rows, :], out_ref.at[:, columns(me, head)], out_local.at[head]
        )

    barrier = pltpu.get_barrier_semaphore()
    for peer in peers:
        pl.semaphore_signal(
            barrier, inc=1, device_id={"ctx": peer}, device_id_type=pl.DeviceIdType.MESH
        )
    pl.semaphore_wait(barrier, count - 1)

    def send_head(head, carry):
        for peer in peers:
            for which in range(3):
                operand_copy(which, head, peer).start()
        for which in range(3):
            operand_local(which, head).start()
        return carry

    lax.fori_loop(0, own_heads, send_head, 0)

    query_pos = lax.broadcasted_iota(jnp.int32, (length, length), 0)
    key_pos = lax.broadcasted_iota(jnp.int32, (length, length), 1)
    visible = key_pos <= query_pos
    for image in range(images):
        first = starts_ref[image]
        inside = (
            (query_pos >= first) & (query_pos < first + SPAN)
            & (key_pos >= first) & (key_pos < first + SPAN)
        )
        visible = visible | inside
    bias[...] = jnp.where(visible, 0.0, -1e30)

    def attend_head(head, carry):
        for which in range(3):
            operand_local(which, head).wait()
            for peer in peers:
                operand_arrival(which, head, peer).wait_recv()
        scores = lax.dot_general(
            q_all[head], k_all[head], (((1,), (1,)), ((), ())),
            preferred_element_type=jnp.float32,
        ) * (HD ** (-0.5) * math.log2(math.e))
        scores = scores + bias[...]
        weights = jnp.exp2(scores - jnp.max(scores, axis=1, keepdims=True))
        total = jnp.sum(weights, axis=1, keepdims=True)
        mixed = jnp.dot(
            weights.astype(jnp.bfloat16), v_all[head], preferred_element_type=jnp.float32
        )
        o_all[head] = (mixed / total).astype(jnp.bfloat16)
        for peer in peers:
            result_copy(head, peer).start()
        result_local(head).start()
        return carry

    lax.fori_loop(0, own_heads, attend_head, 0)

    def finish_head(head, carry):
        result_local(head).wait()
        for peer in peers:
            for which in range(3):
                operand_copy(which, head, peer).wait_send()
            result_copy(head, peer).wait_send()
            result_arrival(head, peer).wait_recv()
        return carry

    lax.fori_loop(0, own_heads, finish_head, 0)


def exchange_body(count, queries, keys, values, span_starts):
    rows = queries.shape[0]
    length = rows * count
    own_heads = HEADS // count
    images = span_starts.shape[0]
    everything = pl.BlockSpec(memory_space=pltpu.HBM)
    return pl.pallas_call(
        functools.partial(exchange_kernel, count, images),
        out_shape=jax.ShapeDtypeStruct(queries.shape, jnp.bfloat16),
        in_specs=[pl.BlockSpec(memory_space=pltpu.SMEM), everything, everything, everything],
        out_specs=everything,
        scratch_shapes=[pltpu.VMEM((own_heads, length, HD), jnp.bfloat16)] * 4
        + [
            pltpu.VMEM((length, length), jnp.float32),
            pltpu.SemaphoreType.DMA((3, own_heads, count)),
            pltpu.SemaphoreType.DMA((3, own_heads, count)),
            pltpu.SemaphoreType.DMA((3, own_heads)),
            pltpu.SemaphoreType.DMA((own_heads, count)),
            pltpu.SemaphoreType.DMA((own_heads, count)),
            pltpu.SemaphoreType.DMA((own_heads,)),
        ],
        compiler_params=pltpu.CompilerParams(
            collective_id=0, has_side_effects=True, vmem_limit_bytes=56 * 1024 * 1024
        ),
    )(span_starts, queries, keys, values)


def solution(mesh):
    count = mesh.shape["ctx"]
    fits = count % 2 == 0 and HEADS % count == 0
    body = functools.partial(exchange_body, count) if fits else ring_body
    placed = (P(("dp", "ctx"), None), P(("dp", "ctx"), None), P(("dp", "ctx"), None), P("dp"))
    return jax.shard_map(
        body, mesh=mesh, in_specs=placed, out_specs=P(("dp", "ctx"), None), check_vma=False
    )
```

```python
import functools
import math

import jax
import jax.numpy as jnp
from jax import lax
from jax.experimental import pallas as pl
from jax.experimental.pallas import tpu as pltpu
from jax.sharding import PartitionSpec as P

HEADS = 16
HD = 128
SPAN = 288


def shifted(value, axis, steps):
    count = lax.axis_size(axis)
    pairs = [(source, (source + steps) % count) for source in range(count)]
    return lax.ppermute(value, axis, pairs)


def span_number(positions, span_starts):
    span_count = span_starts.shape[0]
    inside = (positions[:, None] >= span_starts[None, :]) & (
        positions[:, None] < span_starts[None, :] + SPAN
    )
    labels = jnp.arange(span_count, dtype=jnp.int32) + 1
    return jnp.sum(jnp.where(inside, labels[None, :], 0), axis=1)


def fold_block(operands):
    state_now, visible, group_query, key_heads, value_heads = operands
    row_max, row_sum, weighted = state_now
    scores = jnp.einsum(
        "qhd,khd->hqk", group_query, key_heads, preferred_element_type=jnp.float32
    ) * HD ** (-0.5)
    scores = jnp.where(visible[None], scores, -1e30)
    new_max = jnp.maximum(row_max, jnp.max(scores, axis=2))
    rescale = jnp.exp(row_max - new_max)
    weights = jnp.where(visible[None], jnp.exp(scores - new_max[:, :, None]), 0.0)
    new_sum = row_sum * rescale + jnp.sum(weights, axis=2)
    products = jnp.einsum(
        "hqk,khd->qhd",
        weights.astype(jnp.bfloat16),
        value_heads,
        preferred_element_type=jnp.float32,
    )
    new_weighted = weighted * rescale.T[:, :, None] + products
    return (new_max, new_sum, new_weighted)


def keep_block(operands):
    return operands[0]


def ring_body(queries, keys, values, span_starts):
    tok_rows = queries.shape[0]
    row_width = queries.shape[1]
    loop_size = lax.axis_size("ctx")
    loop_index = lax.axis_index("ctx")
    local_rows = jnp.arange(tok_rows, dtype=jnp.int32)
    query_pos = loop_index * tok_rows + local_rows
    query_span = span_number(query_pos, span_starts)
    query_heads = queries.reshape(tok_rows, HEADS, HD)
    group_count = 2
    group_rows = tok_rows // group_count
    empty_state = tuple(
        (
            (
                jnp.full((HEADS, group_rows), -1e30, jnp.float32),
                jnp.zeros((HEADS, group_rows), jnp.float32),
                jnp.zeros((group_rows, HEADS, HD), jnp.float32),
            )
            for number in range(group_count)
        )
    )

    def absorb(running, block_pair, key_start):
        key_block, value_block = block_pair
        block_rows = key_block.shape[0]
        key_pos = key_start + jnp.arange(block_rows, dtype=jnp.int32)
        key_span = span_number(key_pos, span_starts)
        key_heads = key_block.reshape(block_rows, HEADS, HD)
        value_heads = value_block.reshape(block_rows, HEADS, HD)
        updated = []
        for group_index in range(group_count):
            row_start = group_index * group_rows
            group_pos = query_pos[row_start : row_start + group_rows]
            group_span = query_span[row_start : row_start + group_rows]
            group_query = query_heads[row_start : row_start + group_rows]
            visible = (key_pos[None, :] <= group_pos[:, None]) | (
                group_span[:, None] == key_span[None, :]
            ) & (group_span[:, None] > 0)
            operands = (running[group_index], visible, group_query, key_heads, value_heads)
            updated.append(lax.cond(jnp.any(visible), fold_block, keep_block, operands))
        return tuple(updated)

    stacked = jnp.stack([keys, values])
    own_state = absorb(empty_state, (keys, values), loop_index * tok_rows)

    def advance(step_index, loop_state):
        running, upward, downward = loop_state
        upward = shifted(upward, "ctx", 1)
        downward = shifted(downward, "ctx", -1)
        source_up = (loop_index - 1 - step_index) % loop_size
        source_down = (loop_index + 1 + step_index) % loop_size
        running = absorb(running, (upward[0], upward[1]), source_up * tok_rows)
        running = absorb(running, (downward[0], downward[1]), source_down * tok_rows)
        return (running, upward, downward)

    final_state, upward, downward = lax.fori_loop(
        0, (loop_size - 1) // 2, advance, (own_state, stacked, stacked)
    )
    upward = shifted(upward, "ctx", 1)
    source_last = (loop_index - loop_size // 2) % loop_size
    final_state = absorb(final_state, (upward[0], upward[1]), source_last * tok_rows)
    pieces = [weighted / row_sum.T[:, :, None] for row_max, row_sum, weighted in final_state]
    attended = jnp.concatenate(pieces, axis=0).reshape(tok_rows, row_width).astype(jnp.bfloat16)
    return attended


def exchange_kernel(
    count, images, starts_ref, q_ref, k_ref, v_ref, out_ref,
    q_all, k_all, v_all, o_all, bias,
    in_send, in_recv, in_local, out_send, out_recv, out_local,
):
    me = lax.axis_index("ctx")
    rows = q_ref.shape[0]
    length = rows * count
    own_heads = HEADS // count
    half = count // 2
    side = me // half
    far = [(1 - side) * half + (me + i) % half for i in range(half)]
    near = [side * half + (me + i) % half for i in range(1, half)]
    peers = far + near
    my_rows = pl.ds(pl.multiple_of(me * rows, rows), rows)
    sources = (q_ref, k_ref, v_ref)
    landing = (q_all, k_all, v_all)

    def columns(owner, head):
        return pl.ds(pl.multiple_of((owner * own_heads + head) * HD, HD), HD)

    def rows_of(device):
        return pl.ds(pl.multiple_of(device * rows, rows), rows)

    def operand_copy(which, head, peer):
        return pltpu.make_async_remote_copy(
            src_ref=sources[which].at[:, columns(peer, head)],
            dst_ref=landing[which].at[head, my_rows, :],
            send_sem=in_send.at[which, head, peer],
            recv_sem=in_recv.at[which, head, me],
            device_id={"ctx": peer},
            device_id_type=pl.DeviceIdType.MESH,
        )

    def operand_arrival(which, head, peer):
        return pltpu.make_async_remote_copy(
            src_ref=sources[which].at[:, columns(peer, head)],
            dst_ref=landing[which].at[head, rows_of(peer), :],
            send_sem=in_send.at[which, head, peer],
            recv_sem=in_recv.at[which, head, peer],
            device_id={"ctx": peer},
            device_id_type=pl.DeviceIdType.MESH,
        )

    def operand_local(which, head):
        return pltpu.make_async_copy(
            sources[which].at[:, columns(me, head)],
            landing[which].at[head, my_rows, :],
            in_local.at[which, head],
        )

    def result_copy(head, peer):
        return pltpu.make_async_remote_copy(
            src_ref=o_all.at[head, rows_of(peer), :],
            dst_ref=out_ref.at[:, columns(me, head)],
            send_sem=out_send.at[head, peer],
            recv_sem=out_recv.at[head, me],
            device_id={"ctx": peer},
            device_id_type=pl.DeviceIdType.MESH,
        )

    def result_arrival(head, peer):
        return pltpu.make_async_remote_copy(
            src_ref=o_all.at[head, rows_of(peer), :],
            dst_ref=out_ref.at[:, columns(peer, head)],
            send_sem=out_send.at[head, peer],
            recv_sem=out_recv.at[head, peer],
            device_id={"ctx": peer},
            device_id_type=pl.DeviceIdType.MESH,
        )

    def result_local(head):
        return pltpu.make_async_copy(
            o_all.at[head, my_rows, :], out_ref.at[:, columns(me, head)], out_local.at[head]
        )

    barrier = pltpu.get_barrier_semaphore()
    for peer in peers:
        pl.semaphore_signal(
            barrier, inc=1, device_id={"ctx": peer}, device_id_type=pl.DeviceIdType.MESH
        )
    pl.semaphore_wait(barrier, count - 1)

    def send_head(head, carry):
        for peer in peers:
            for which in range(3):
                operand_copy(which, head, peer).start()
        for which in range(3):
            operand_local(which, head).start()
        return carry

    lax.fori_loop(0, own_heads, send_head, 0)

    query_pos = lax.broadcasted_iota(jnp.int32, (length, length), 0)
    key_pos = lax.broadcasted_iota(jnp.int32, (length, length), 1)
    visible = key_pos <= query_pos
    for image in range(images):
        first = starts_ref[image]
        inside = (
            (query_pos >= first) & (query_pos < first + SPAN)
            & (key_pos >= first) & (key_pos < first + SPAN)
        )
        visible = visible | inside
    bias[...] = jnp.where(visible, 0.0, -1e30)

    def attend_head(head, carry):
        for which in range(3):
            operand_local(which, head).wait()
            for peer in peers:
                operand_arrival(which, head, peer).wait_recv()
        scores = lax.dot_general(
            q_all[head], k_all[head], (((1,), (1,)), ((), ())),
            preferred_element_type=jnp.float32,
        ) * (HD ** (-0.5) * math.log2(math.e))
        scores = scores + bias[...]
        weights = jnp.exp2(scores - jnp.max(scores, axis=1, keepdims=True))
        total = jnp.sum(weights, axis=1, keepdims=True)
        mixed = jnp.dot(
            weights.astype(jnp.bfloat16), v_all[head], preferred_element_type=jnp.float32
        )
        o_all[head] = (mixed / total).astype(jnp.bfloat16)
        for peer in peers:
            result_copy(head, peer).start()
        result_local(head).start()
        return carry

    lax.fori_loop(0, own_heads, attend_head, 0)

    def finish_head(head, carry):
        result_local(head).wait()
        for peer in peers:
            for which in range(3):
                operand_copy(which, head, peer).wait_send()
            result_copy(head, peer).wait_send()
            result_arrival(head, peer).wait_recv()
        return carry

    lax.fori_loop(0, own_heads, finish_head, 0)


def exchange_body(count, queries, keys, values, span_starts):
    rows = queries.shape[0]
    length = rows * count
    own_heads = HEADS // count
    images = span_starts.shape[0]
    everything = pl.BlockSpec(memory_space=pltpu.HBM)
    return pl.pallas_call(
        functools.partial(exchange_kernel, count, images),
        out_shape=jax.ShapeDtypeStruct(queries.shape, jnp.bfloat16),
        in_specs=[pl.BlockSpec(memory_space=pltpu.SMEM), everything, everything, everything],
        out_specs=everything,
        scratch_shapes=[pltpu.VMEM((own_heads, length, HD), jnp.bfloat16)] * 4
        + [
            pltpu.VMEM((length, length), jnp.float32),
            pltpu.SemaphoreType.DMA((3, own_heads, count)),
            pltpu.SemaphoreType.DMA((3, own_heads, count)),
            pltpu.SemaphoreType.DMA((3, own_heads)),
            pltpu.SemaphoreType.DMA((own_heads, count)),
            pltpu.SemaphoreType.DMA((own_heads, count)),
            pltpu.SemaphoreType.DMA((own_heads,)),
        ],
        compiler_params=pltpu.CompilerParams(
            collective_id=0, has_side_effects=True, vmem_limit_bytes=56 * 1024 * 1024
        ),
    )(span_starts, queries, keys, values)


def cut_kernel(
    starts_ref, q_ref, k_ref, v_ref, out_ref,
    q_half, k_half, v_half, o_half, cross_in, cross_out, stat_in, stat_out,
    bias_own, bias_low, bias_high,
    half_send, half_recv, half_local, cross_send, cross_recv,
    stat_send, stat_recv, out_send, out_recv, out_local,
):
    me = lax.axis_index("ctx")
    rows = q_ref.shape[0]
    pair = 2 * rows
    steps = HEADS // 2
    scale = HD ** (-0.5) * math.log2(math.e)
    sources = (q_ref, k_ref, v_ref)
    halves = (q_half, k_half, v_half)
    first = starts_ref[0]
    by_query = first >= rows
    LOW, HIGH = slice(0, rows), slice(rows, pair)

    def columns(head):
        return pl.ds(pl.multiple_of(head * HD, HD), HD)

    def remote(src, dst, send, recv, peer):
        return pltpu.make_async_remote_copy(
            src_ref=src, dst_ref=dst, send_sem=send, recv_sem=recv,
            device_id={"ctx": peer}, device_id_type=pl.DeviceIdType.MESH,
        )

    def half_copy(which, head, part, peer):
        return remote(
            sources[which].at[:, columns(head)], halves[which].at[head, part, :],
            half_send.at[which, head], half_recv.at[which, head], peer,
        )

    def own_copy(which, head, part):
        return pltpu.make_async_copy(
            sources[which].at[:, columns(head)], halves[which].at[head, part, :],
            half_local.at[which, head],
        )

    def cross_copy(slot, step, peer):
        return remote(
            cross_out.at[slot, step], cross_in.at[slot, step],
            cross_send.at[slot, step], cross_recv.at[slot, step], peer,
        )

    def query_copy(step, peer):
        return remote(
            q_half.at[step], cross_in.at[0, step],
            cross_send.at[0, step], cross_recv.at[0, step], peer,
        )

    def stat_copy(step, peer):
        return remote(
            stat_out.at[step], stat_in.at[step], stat_send.at[step], stat_recv.at[step], peer
        )

    def result_copy(head, part, peer):
        return remote(
            o_half.at[head, part, :], out_ref.at[:, columns(head)],
            out_send.at[head], out_recv.at[head], peer,
        )

    def result_local(head, part):
        return pltpu.make_async_copy(
            o_half.at[head, part, :], out_ref.at[:, columns(head)], out_local.at[head]
        )

    def scores_of(query, key):
        return lax.dot_general(
            query, key, (((1,), (1,)), ((), ())), preferred_element_type=jnp.float32
        ) * scale

    def weigh(scores, top):
        return jnp.exp2(scores - top)

    def mix(weights, value):
        return jnp.dot(weights.astype(jnp.bfloat16), value, preferred_element_type=jnp.float32)

    def attend(query, key, value, bias=None):
        scores = scores_of(query, key)
        if bias is not None:
            scores = scores + bias
        top = jnp.max(scores, axis=1, keepdims=True)
        weights = weigh(scores, top)
        return mix(weights, value), top, jnp.sum(weights, axis=1, keepdims=True)

    def as_row(column):
        return jnp.transpose(jnp.broadcast_to(column, (pair, HD)))[0:1, :]

    def as_columns(row):
        return jnp.transpose(jnp.broadcast_to(row, (HD, pair)))

    def merge(mixed, top, total, other, other_log):
        peak = jnp.maximum(top, other_log)
        mine, theirs = jnp.exp2(top - peak), jnp.exp2(other_log - peak)
        return (mixed * mine + other * theirs) / (total * mine + theirs)

    def hidden(query_start, query_rows, key_start, key_rows, causal):
        query_pos = query_start + lax.broadcasted_iota(jnp.int32, (query_rows, key_rows), 0)
        key_pos = key_start + lax.broadcasted_iota(jnp.int32, (query_rows, key_rows), 1)
        visible = (
            (query_pos >= first) & (query_pos < first + SPAN)
            & (key_pos >= first) & (key_pos < first + SPAN)
        )
        if causal:
            visible = visible | (key_pos <= query_pos)
        return jnp.where(visible, 0.0, -1e30)

    barrier = pltpu.get_barrier_semaphore()

    @pl.when(me > 0)
    def _():
        pl.semaphore_signal(
            barrier, inc=1, device_id={"ctx": me - 1}, device_id_type=pl.DeviceIdType.MESH
        )

    @pl.when(me < 3)
    def _():
        pl.semaphore_signal(
            barrier, inc=1, device_id={"ctx": me + 1}, device_id_type=pl.DeviceIdType.MESH
        )

    @pl.when((me == 0) | (me == 3))
    def _():
        pl.semaphore_wait(barrier, 1)

    @pl.when((me == 1) | (me == 2))
    def _():
        pl.semaphore_wait(barrier, 2)

    def repeat(count, one):
        lax.fori_loop(0, count, lambda step, carry: (one(step), carry)[1], 0)

    def outer_end(part, peer):
        def one(head):
            for which in range(3):
                half_copy(which, head, part, peer).wait_send()
            result_copy(head, part, peer).wait_recv()

        repeat(HEADS, one)

    @pl.when(me == 0)
    def _():
        def first_part(step):
            half_copy(1, steps + step, LOW, me + 1).start()
            half_copy(1, step, LOW, me + 1).start()
            half_copy(2, step, LOW, me + 1).start()

        repeat(steps, first_part)
        repeat(steps, lambda step: half_copy(2, steps + step, LOW, me + 1).start())
        repeat(HEADS, lambda head: half_copy(0, head, LOW, me + 1).start())
        outer_end(LOW, me + 1)

    @pl.when(me == 3)
    def _():
        repeat(HEADS, lambda head: half_copy(0, head, HIGH, me - 1).start())

        def pair_part(head):
            half_copy(1, head, HIGH, me - 1).start()
            half_copy(2, head, HIGH, me - 1).start()

        repeat(HEADS, pair_part)
        outer_end(HIGH, me - 1)

    def own_start(part):
        def one(head):
            for which in range(3):
                own_copy(which, head, part).start()

        repeat(HEADS, one)

    def own_wait(part):
        def one(head):
            for which in range(3):
                own_copy(which, head, part).wait()

        repeat(HEADS, one)

    @pl.when(me == 1)
    def _():
        peer, outer = me + 1, me - 1
        own_start(HIGH)
        bias_own[...] = hidden(0, pair, 0, pair, True)
        bias_low[...] = jnp.where(by_query, -1e30, hidden(0, pair, pair, rows, False))
        own_wait(HIGH)

        def arrived(which, head):
            half_copy(which, head, LOW, outer).wait_recv()

        def first_part(step):
            arrived(1, steps + step)
            for side, part in enumerate((LOW, HIGH)):
                cross_out[1, step, part, :] = jnp.where(
                    by_query, q_half[2 * step + side, HIGH, :], k_half[steps + step, part, :]
                )
            cross_copy(1, step, peer).start()
            arrived(1, step)
            arrived(2, step)
            query_copy(step, peer).wait_recv()
            mixed, top, total = attend(cross_in[0, step], k_half[step], v_half[step])
            cross_out[0, step] = (mixed / total).astype(jnp.bfloat16)
            stat_out[step] = as_row(top + jnp.log2(total))
            cross_copy(0, step, peer).start()
            stat_copy(step, peer).start()

        repeat(steps, first_part)

        def second_part(step):
            arrived(2, steps + step)
            cross_copy(1, step, peer).wait_recv()
            mixed, top, total = attend(
                cross_in[1, step], k_half[steps + step], v_half[steps + step]
            )
            cross_out[2, step] = jnp.where(
                by_query, (mixed / total).astype(jnp.bfloat16), v_half[steps + step]
            )
            stat_out[steps + step] = as_row(top + jnp.log2(total))
            cross_copy(2, step, peer).start()
            stat_copy(steps + step, peer).start()

        repeat(steps, second_part)

        def third_part(step):
            cross_copy(2, step, peer).wait_recv()
            stat_copy(step, peer).wait_recv()
            logs = as_columns(jnp.where(by_query, stat_in[step], -1e30))
            for side, part in enumerate((LOW, HIGH)):
                head = 2 * step + side
                arrived(0, head)
                query = q_half[head]
                near = scores_of(query, k_half[head]) + bias_own[...]
                far = scores_of(query, cross_in[1, step, part, :]) + bias_low[...]
                top = jnp.maximum(
                    jnp.max(near, axis=1, keepdims=True), jnp.max(far, axis=1, keepdims=True)
                )
                near, far = weigh(near, top), weigh(far, top)
                total = jnp.sum(near, axis=1, keepdims=True) + jnp.sum(
                    far, axis=1, keepdims=True
                )
                other = cross_in[2, step, part, :]
                mixed = mix(near, v_half[head]) + mix(far, other)
                o_half[head, LOW, :] = (mixed[LOW] / total[LOW]).astype(jnp.bfloat16)
                o_half[head, HIGH, :] = merge(
                    mixed[HIGH], top[HIGH], total[HIGH],
                    other.astype(jnp.float32), logs[part],
                ).astype(jnp.bfloat16)
                result_copy(head, LOW, outer).start()
                result_local(head, HIGH).start()

        repeat(steps, third_part)

        def finish(step):
            for slot in range(3):
                cross_copy(slot, step, peer).wait_send()
            for side in range(2):
                stat_copy(2 * step + side, peer).wait_send()
                result_copy(2 * step + side, LOW, outer).wait_send()
                result_local(2 * step + side, HIGH).wait()

        repeat(steps, finish)

    @pl.when(me == 2)
    def _():
        peer, outer = me - 1, me + 1
        own_start(LOW)
        bias_own[...] = hidden(pair, pair, pair, pair, True)
        bias_high[...] = hidden(rows, rows, pair, pair, False)
        own_wait(LOW)

        def arrived(which, head):
            half_copy(which, head, HIGH, outer).wait_recv()

        def send_query(step):
            arrived(0, step)
            query_copy(step, peer).start()

        repeat(steps, send_query)

        def send_either(step):
            arrived(0, steps + step)
            for side, part in enumerate((LOW, HIGH)):
                cross_out[1, step, part, :] = jnp.where(
                    by_query, q_half[steps + step, part, :], k_half[2 * step + side, LOW, :]
                )
            cross_copy(1, step, peer).start()

        repeat(steps, send_either)

        def send_span(step):
            cross_copy(1, step, peer).wait_recv()
            tops, totals = [], []
            for side, part in enumerate((LOW, HIGH)):
                head = 2 * step + side
                arrived(1, head)
                arrived(2, head)
                mixed, top, total = attend(
                    cross_in[1, step, part, :], k_half[head], v_half[head], bias_high[...]
                )
                cross_out[2, step, part, :] = jnp.where(
                    by_query, (mixed / total).astype(jnp.bfloat16), v_half[head, LOW, :]
                )
                tops.append(top)
                totals.append(total)
            logs = jnp.concatenate(tops, axis=0) + jnp.log2(jnp.concatenate(totals, axis=0))
            stat_out[step] = as_row(logs)
            cross_copy(2, step, peer).start()
            stat_copy(step, peer).start()

        def give(head, mixed, top, total, other, logs):
            o_half[head] = merge(mixed, top, total, other, logs).astype(jnp.bfloat16)
            result_copy(head, HIGH, outer).start()
            result_local(head, LOW).start()

        def finish_low(step):
            cross_copy(0, step, peer).wait_recv()
            stat_copy(step, peer).wait_recv()
            mixed, top, total = attend(
                q_half[step], k_half[step], v_half[step], bias_own[...]
            )
            other = cross_in[0, step].astype(jnp.float32)
            give(step, mixed, top, total, other, as_columns(stat_in[step]))

        def finish_high(step):
            head = steps + step
            cross_copy(2, step, peer).wait_recv()
            stat_copy(head, peer).wait_recv()
            mixed, top, total = attend(
                q_half[head], k_half[head], v_half[head], bias_own[...]
            )
            low_mixed, low_top, low_total = attend(
                q_half[head], cross_in[1, step], cross_in[2, step]
            )
            other = jnp.where(
                by_query, cross_in[2, step].astype(jnp.float32), low_mixed / low_total
            )
            logs = jnp.where(
                by_query, as_columns(stat_in[head]),
                jnp.broadcast_to(low_top + jnp.log2(low_total), (pair, HD)),
            )
            give(head, mixed, top, total, other, logs)

        def both(step):
            send_span(step)
            finish_low(step)

        repeat(steps // 2, both)

        def late(step):
            send_span(steps // 2 + step)
            finish_low(steps // 2 + step)
            finish_high(2 * step)
            finish_high(2 * step + 1)

        repeat(steps // 2, late)

        def finish(step):
            query_copy(step, peer).wait_send()
            for slot in (1, 2):
                cross_copy(slot, step, peer).wait_send()
            stat_copy(step, peer).wait_send()
            for side in range(2):
                result_copy(2 * step + side, HIGH, outer).wait_send()
                result_local(2 * step + side, LOW).wait()

        repeat(steps, finish)


def cut_body(queries, keys, values, span_starts):
    rows = queries.shape[0]
    pair = 2 * rows
    steps = HEADS // 2
    everything = pl.BlockSpec(memory_space=pltpu.HBM)
    dma = pltpu.SemaphoreType.DMA
    return pl.pallas_call(
        cut_kernel,
        out_shape=jax.ShapeDtypeStruct(queries.shape, jnp.bfloat16),
        in_specs=[pl.BlockSpec(memory_space=pltpu.SMEM), everything, everything, everything],
        out_specs=everything,
        scratch_shapes=[pltpu.VMEM((HEADS, pair, HD), jnp.bfloat16)] * 4
        + [pltpu.VMEM((3, steps, pair, HD), jnp.bfloat16)] * 2
        + [pltpu.VMEM((HEADS, 1, pair), jnp.float32)] * 2
        + [
            pltpu.VMEM((pair, pair), jnp.float32),
            pltpu.VMEM((pair, rows), jnp.float32),
            pltpu.VMEM((rows, pair), jnp.float32),
            dma((3, HEADS)), dma((3, HEADS)), dma((3, HEADS)),
            dma((3, steps)), dma((3, steps)),
            dma((HEADS,)), dma((HEADS,)),
            dma((HEADS,)), dma((HEADS,)), dma((HEADS,)),
        ],
        compiler_params=pltpu.CompilerParams(
            collective_id=0, has_side_effects=True, vmem_limit_bytes=56 * 1024 * 1024
        ),
    )(span_starts, queries, keys, values)


def chosen_body(count, queries, keys, values, span_starts):
    rows, images = queries.shape[0], span_starts.shape[0]
    if count == 4 and images == 1 and SPAN <= 2 * rows and rows % 16 == 0:
        return cut_body(queries, keys, values, span_starts)
    if count % 2 == 0 and HEADS % count == 0:
        return exchange_body(count, queries, keys, values, span_starts)
    return ring_body(queries, keys, values, span_starts)


def solution(mesh):
    body = functools.partial(chosen_body, mesh.shape["ctx"])
    placed = (P(("dp", "ctx"), None), P(("dp", "ctx"), None), P(("dp", "ctx"), None), P("dp"))
    return jax.shard_map(
        body, mesh=mesh, in_specs=placed, out_specs=P(("dp", "ctx"), None), check_vma=False
    )
```

```python
import functools
import math

import jax
import jax.numpy as jnp
from jax import lax
from jax.experimental import pallas as pl
from jax.experimental.pallas import tpu as pltpu
from jax.sharding import PartitionSpec as P

HEADS = 16
HD = 128
SPAN = 288


def shifted(value, axis, steps):
    count = lax.axis_size(axis)
    pairs = [(source, (source + steps) % count) for source in range(count)]
    return lax.ppermute(value, axis, pairs)


def span_number(positions, span_starts):
    span_count = span_starts.shape[0]
    inside = (positions[:, None] >= span_starts[None, :]) & (
        positions[:, None] < span_starts[None, :] + SPAN
    )
    labels = jnp.arange(span_count, dtype=jnp.int32) + 1
    return jnp.sum(jnp.where(inside, labels[None, :], 0), axis=1)


def fold_block(operands):
    state_now, visible, group_query, key_heads, value_heads = operands
    row_max, row_sum, weighted = state_now
    scores = jnp.einsum(
        "qhd,khd->hqk", group_query, key_heads, preferred_element_type=jnp.float32
    ) * HD ** (-0.5)
    scores = jnp.where(visible[None], scores, -1e30)
    new_max = jnp.maximum(row_max, jnp.max(scores, axis=2))
    rescale = jnp.exp(row_max - new_max)
    weights = jnp.where(visible[None], jnp.exp(scores - new_max[:, :, None]), 0.0)
    new_sum = row_sum * rescale + jnp.sum(weights, axis=2)
    products = jnp.einsum(
        "hqk,khd->qhd",
        weights.astype(jnp.bfloat16),
        value_heads,
        preferred_element_type=jnp.float32,
    )
    new_weighted = weighted * rescale.T[:, :, None] + products
    return (new_max, new_sum, new_weighted)


def keep_block(operands):
    return operands[0]


def ring_body(queries, keys, values, span_starts):
    tok_rows = queries.shape[0]
    row_width = queries.shape[1]
    loop_size = lax.axis_size("ctx")
    loop_index = lax.axis_index("ctx")
    local_rows = jnp.arange(tok_rows, dtype=jnp.int32)
    query_pos = loop_index * tok_rows + local_rows
    query_span = span_number(query_pos, span_starts)
    query_heads = queries.reshape(tok_rows, HEADS, HD)
    group_count = 2
    group_rows = tok_rows // group_count
    empty_state = tuple(
        (
            (
                jnp.full((HEADS, group_rows), -1e30, jnp.float32),
                jnp.zeros((HEADS, group_rows), jnp.float32),
                jnp.zeros((group_rows, HEADS, HD), jnp.float32),
            )
            for number in range(group_count)
        )
    )

    def absorb(running, block_pair, key_start):
        key_block, value_block = block_pair
        block_rows = key_block.shape[0]
        key_pos = key_start + jnp.arange(block_rows, dtype=jnp.int32)
        key_span = span_number(key_pos, span_starts)
        key_heads = key_block.reshape(block_rows, HEADS, HD)
        value_heads = value_block.reshape(block_rows, HEADS, HD)
        updated = []
        for group_index in range(group_count):
            row_start = group_index * group_rows
            group_pos = query_pos[row_start : row_start + group_rows]
            group_span = query_span[row_start : row_start + group_rows]
            group_query = query_heads[row_start : row_start + group_rows]
            visible = (key_pos[None, :] <= group_pos[:, None]) | (
                group_span[:, None] == key_span[None, :]
            ) & (group_span[:, None] > 0)
            operands = (running[group_index], visible, group_query, key_heads, value_heads)
            updated.append(lax.cond(jnp.any(visible), fold_block, keep_block, operands))
        return tuple(updated)

    stacked = jnp.stack([keys, values])
    own_state = absorb(empty_state, (keys, values), loop_index * tok_rows)

    def advance(step_index, loop_state):
        running, upward, downward = loop_state
        upward = shifted(upward, "ctx", 1)
        downward = shifted(downward, "ctx", -1)
        source_up = (loop_index - 1 - step_index) % loop_size
        source_down = (loop_index + 1 + step_index) % loop_size
        running = absorb(running, (upward[0], upward[1]), source_up * tok_rows)
        running = absorb(running, (downward[0], downward[1]), source_down * tok_rows)
        return (running, upward, downward)

    final_state, upward, downward = lax.fori_loop(
        0, (loop_size - 1) // 2, advance, (own_state, stacked, stacked)
    )
    upward = shifted(upward, "ctx", 1)
    source_last = (loop_index - loop_size // 2) % loop_size
    final_state = absorb(final_state, (upward[0], upward[1]), source_last * tok_rows)
    pieces = [weighted / row_sum.T[:, :, None] for row_max, row_sum, weighted in final_state]
    attended = jnp.concatenate(pieces, axis=0).reshape(tok_rows, row_width).astype(jnp.bfloat16)
    return attended


def exchange_kernel(
    count, images, starts_ref, q_ref, k_ref, v_ref, out_ref,
    q_all, k_all, v_all, o_all, bias,
    in_send, in_recv, in_local, out_send, out_recv, out_local,
):
    me = lax.axis_index("ctx")
    rows = q_ref.shape[0]
    length = rows * count
    own_heads = HEADS // count
    half = count // 2
    side = me // half
    far = [(1 - side) * half + (me + i) % half for i in range(half)]
    near = [side * half + (me + i) % half for i in range(1, half)]
    peers = far + near
    my_rows = pl.ds(pl.multiple_of(me * rows, rows), rows)
    sources = (q_ref, k_ref, v_ref)
    landing = (q_all, k_all, v_all)

    def columns(owner, head):
        return pl.ds(pl.multiple_of((owner * own_heads + head) * HD, HD), HD)

    def rows_of(device):
        return pl.ds(pl.multiple_of(device * rows, rows), rows)

    def operand_copy(which, head, peer):
        return pltpu.make_async_remote_copy(
            src_ref=sources[which].at[:, columns(peer, head)],
            dst_ref=landing[which].at[head, my_rows, :],
            send_sem=in_send.at[which, head, peer],
            recv_sem=in_recv.at[which, head, me],
            device_id={"ctx": peer},
            device_id_type=pl.DeviceIdType.MESH,
        )

    def operand_arrival(which, head, peer):
        return pltpu.make_async_remote_copy(
            src_ref=sources[which].at[:, columns(peer, head)],
            dst_ref=landing[which].at[head, rows_of(peer), :],
            send_sem=in_send.at[which, head, peer],
            recv_sem=in_recv.at[which, head, peer],
            device_id={"ctx": peer},
            device_id_type=pl.DeviceIdType.MESH,
        )

    def operand_local(which, head):
        return pltpu.make_async_copy(
            sources[which].at[:, columns(me, head)],
            landing[which].at[head, my_rows, :],
            in_local.at[which, head],
        )

    def result_copy(head, peer):
        return pltpu.make_async_remote_copy(
            src_ref=o_all.at[head, rows_of(peer), :],
            dst_ref=out_ref.at[:, columns(me, head)],
            send_sem=out_send.at[head, peer],
            recv_sem=out_recv.at[head, me],
            device_id={"ctx": peer},
            device_id_type=pl.DeviceIdType.MESH,
        )

    def result_arrival(head, peer):
        return pltpu.make_async_remote_copy(
            src_ref=o_all.at[head, rows_of(peer), :],
            dst_ref=out_ref.at[:, columns(peer, head)],
            send_sem=out_send.at[head, peer],
            recv_sem=out_recv.at[head, peer],
            device_id={"ctx": peer},
            device_id_type=pl.DeviceIdType.MESH,
        )

    def result_local(head):
        return pltpu.make_async_copy(
            o_all.at[head, my_rows, :], out_ref.at[:, columns(me, head)], out_local.at[head]
        )

    barrier = pltpu.get_barrier_semaphore()
    for peer in peers:
        pl.semaphore_signal(
            barrier, inc=1, device_id={"ctx": peer}, device_id_type=pl.DeviceIdType.MESH
        )
    pl.semaphore_wait(barrier, count - 1)

    def send_head(head, carry):
        for peer in peers:
            for which in range(3):
                operand_copy(which, head, peer).start()
        for which in range(3):
            operand_local(which, head).start()
        return carry

    lax.fori_loop(0, own_heads, send_head, 0)

    query_pos = lax.broadcasted_iota(jnp.int32, (length, length), 0)
    key_pos = lax.broadcasted_iota(jnp.int32, (length, length), 1)
    visible = key_pos <= query_pos
    for image in range(images):
        first = starts_ref[image]
        inside = (
            (query_pos >= first) & (query_pos < first + SPAN)
            & (key_pos >= first) & (key_pos < first + SPAN)
        )
        visible = visible | inside
    bias[...] = jnp.where(visible, 0.0, -1e30)

    def attend_head(head, carry):
        for which in range(3):
            operand_local(which, head).wait()
            for peer in peers:
                operand_arrival(which, head, peer).wait_recv()
        scores = lax.dot_general(
            q_all[head], k_all[head], (((1,), (1,)), ((), ())),
            preferred_element_type=jnp.float32,
        ) * (HD ** (-0.5) * math.log2(math.e))
        scores = scores + bias[...]
        weights = jnp.exp2(scores - jnp.max(scores, axis=1, keepdims=True))
        total = jnp.sum(weights, axis=1, keepdims=True)
        mixed = jnp.dot(
            weights.astype(jnp.bfloat16), v_all[head], preferred_element_type=jnp.float32
        )
        o_all[head] = (mixed / total).astype(jnp.bfloat16)
        for peer in peers:
            result_copy(head, peer).start()
        result_local(head).start()
        return carry

    lax.fori_loop(0, own_heads, attend_head, 0)

    def finish_head(head, carry):
        result_local(head).wait()
        for peer in peers:
            for which in range(3):
                operand_copy(which, head, peer).wait_send()
            result_copy(head, peer).wait_send()
            result_arrival(head, peer).wait_recv()
        return carry

    lax.fori_loop(0, own_heads, finish_head, 0)


def exchange_body(count, queries, keys, values, span_starts):
    rows = queries.shape[0]
    length = rows * count
    own_heads = HEADS // count
    images = span_starts.shape[0]
    everything = pl.BlockSpec(memory_space=pltpu.HBM)
    return pl.pallas_call(
        functools.partial(exchange_kernel, count, images),
        out_shape=jax.ShapeDtypeStruct(queries.shape, jnp.bfloat16),
        in_specs=[pl.BlockSpec(memory_space=pltpu.SMEM), everything, everything, everything],
        out_specs=everything,
        scratch_shapes=[pltpu.VMEM((own_heads, length, HD), jnp.bfloat16)] * 4
        + [
            pltpu.VMEM((length, length), jnp.float32),
            pltpu.SemaphoreType.DMA((3, own_heads, count)),
            pltpu.SemaphoreType.DMA((3, own_heads, count)),
            pltpu.SemaphoreType.DMA((3, own_heads)),
            pltpu.SemaphoreType.DMA((own_heads, count)),
            pltpu.SemaphoreType.DMA((own_heads, count)),
            pltpu.SemaphoreType.DMA((own_heads,)),
        ],
        compiler_params=pltpu.CompilerParams(
            collective_id=0, has_side_effects=True, vmem_limit_bytes=56 * 1024 * 1024
        ),
    )(span_starts, queries, keys, values)


def cut_kernel(
    starts_ref, q_ref, k_ref, v_ref, out_ref,
    q_half, k_half, v_half, o_half, cross_in, cross_out, stat_in, stat_out,
    bias_own, bias_low, bias_high,
    half_send, half_recv, half_local, cross_send, cross_recv,
    stat_send, stat_recv, out_send, out_recv, out_local,
):
    me = lax.axis_index("ctx")
    rows = q_ref.shape[0]
    pair = 2 * rows
    steps = HEADS // 2
    scale = HD ** (-0.5) * math.log2(math.e)
    sources = (q_ref, k_ref, v_ref)
    halves = (q_half, k_half, v_half)
    first = starts_ref[0]
    by_query = first >= rows
    LOW, HIGH = slice(0, rows), slice(rows, pair)

    def columns(head):
        return pl.ds(pl.multiple_of(head * HD, HD), HD)

    def remote(src, dst, send, recv, peer):
        return pltpu.make_async_remote_copy(
            src_ref=src, dst_ref=dst, send_sem=send, recv_sem=recv,
            device_id={"ctx": peer}, device_id_type=pl.DeviceIdType.MESH,
        )

    def half_copy(which, head, part, peer):
        return remote(
            sources[which].at[:, columns(head)], halves[which].at[head, part, :],
            half_send.at[which, head], half_recv.at[which, head], peer,
        )

    def own_copy(which, head, part):
        return pltpu.make_async_copy(
            sources[which].at[:, columns(head)], halves[which].at[head, part, :],
            half_local.at[which, head],
        )

    def cross_copy(slot, step, peer):
        return remote(
            cross_out.at[slot, step], cross_in.at[slot, step],
            cross_send.at[slot, step], cross_recv.at[slot, step], peer,
        )

    def query_copy(step, peer):
        return remote(
            q_half.at[step], cross_in.at[0, step],
            cross_send.at[0, step], cross_recv.at[0, step], peer,
        )

    def stat_copy(step, peer):
        return remote(
            stat_out.at[step], stat_in.at[step], stat_send.at[step], stat_recv.at[step], peer
        )

    def result_copy(head, part, peer):
        return remote(
            o_half.at[head, part, :], out_ref.at[:, columns(head)],
            out_send.at[head], out_recv.at[head], peer,
        )

    def result_local(head, part):
        return pltpu.make_async_copy(
            o_half.at[head, part, :], out_ref.at[:, columns(head)], out_local.at[head]
        )

    def scores_of(query, key):
        return lax.dot_general(
            query, key, (((1,), (1,)), ((), ())), preferred_element_type=jnp.float32
        ) * scale

    def weigh(scores, top):
        return jnp.exp2(scores - top)

    def mix(weights, value):
        return jnp.dot(weights.astype(jnp.bfloat16), value, preferred_element_type=jnp.float32)

    def attend(items):
        scores = [
            scores_of(query, key) if bias is None else scores_of(query, key) + bias
            for query, key, value, bias in items
        ]
        tops = [jnp.max(score, axis=1, keepdims=True) for score in scores]
        weights = [weigh(score, top) for score, top in zip(scores, tops)]
        totals = [jnp.sum(weight, axis=1, keepdims=True) for weight in weights]
        mixed = [mix(weight, item[2]) for weight, item in zip(weights, items)]
        return list(zip(mixed, tops, totals))

    def as_row(column):
        return jnp.transpose(jnp.broadcast_to(column, (pair, HD)))[0:1, :]

    def as_columns(row):
        return jnp.transpose(jnp.broadcast_to(row, (HD, pair)))

    def merge(mixed, top, total, other, other_log):
        peak = jnp.maximum(top, other_log)
        mine, theirs = jnp.exp2(top - peak), jnp.exp2(other_log - peak)
        return (mixed * mine + other * theirs) / (total * mine + theirs)

    def hidden(query_start, query_rows, key_start, key_rows, causal):
        query_pos = query_start + lax.broadcasted_iota(jnp.int32, (query_rows, key_rows), 0)
        key_pos = key_start + lax.broadcasted_iota(jnp.int32, (query_rows, key_rows), 1)
        visible = (
            (query_pos >= first) & (query_pos < first + SPAN)
            & (key_pos >= first) & (key_pos < first + SPAN)
        )
        if causal:
            visible = visible | (key_pos <= query_pos)
        return jnp.where(visible, 0.0, -1e30)

    barrier = pltpu.get_barrier_semaphore()

    @pl.when(me > 0)
    def _():
        pl.semaphore_signal(
            barrier, inc=1, device_id={"ctx": me - 1}, device_id_type=pl.DeviceIdType.MESH
        )

    @pl.when(me < 3)
    def _():
        pl.semaphore_signal(
            barrier, inc=1, device_id={"ctx": me + 1}, device_id_type=pl.DeviceIdType.MESH
        )

    @pl.when((me == 0) | (me == 3))
    def _():
        pl.semaphore_wait(barrier, 1)

    @pl.when((me == 1) | (me == 2))
    def _():
        pl.semaphore_wait(barrier, 2)

    def repeat(count, one):
        lax.fori_loop(0, count, lambda step, carry: (one(step), carry)[1], 0)

    def outer_end(part, peer):
        def one(head):
            for which in range(3):
                half_copy(which, head, part, peer).wait_send()
            result_copy(head, part, peer).wait_recv()

        repeat(HEADS, one)

    @pl.when(me == 0)
    def _():
        def first_part(step):
            half_copy(1, steps + step, LOW, me + 1).start()
            half_copy(1, step, LOW, me + 1).start()
            half_copy(2, step, LOW, me + 1).start()

        repeat(steps, first_part)
        repeat(steps, lambda step: half_copy(2, steps + step, LOW, me + 1).start())
        repeat(HEADS, lambda head: half_copy(0, head, LOW, me + 1).start())
        outer_end(LOW, me + 1)

    @pl.when(me == 3)
    def _():
        repeat(HEADS, lambda head: half_copy(0, head, HIGH, me - 1).start())

        def pair_part(head):
            half_copy(1, head, HIGH, me - 1).start()
            half_copy(2, head, HIGH, me - 1).start()

        repeat(HEADS, pair_part)
        outer_end(HIGH, me - 1)

    def own_start(part):
        def one(head):
            for which in range(3):
                own_copy(which, head, part).start()

        repeat(HEADS, one)

    def own_wait(part):
        def one(head):
            for which in range(3):
                own_copy(which, head, part).wait()

        repeat(HEADS, one)

    @pl.when(me == 1)
    def _():
        peer, outer = me + 1, me - 1
        own_start(HIGH)
        bias_own[...] = hidden(0, pair, 0, pair, True)
        bias_low[...] = jnp.where(by_query, -1e30, hidden(0, pair, pair, rows, False))
        own_wait(HIGH)

        def arrived(which, head):
            half_copy(which, head, LOW, outer).wait_recv()

        def first_part(turn):
            both = (2 * turn, 2 * turn + 1)
            for step in both:
                arrived(1, steps + step)
                for side, part in enumerate((LOW, HIGH)):
                    cross_out[1, step, part, :] = jnp.where(
                        by_query, q_half[2 * step + side, HIGH, :], k_half[steps + step, part, :]
                    )
                cross_copy(1, step, peer).start()
            for step in both:
                arrived(1, step)
                arrived(2, step)
                query_copy(step, peer).wait_recv()
            done = attend([(cross_in[0, step], k_half[step], v_half[step], None) for step in both])
            for step, (mixed, top, total) in zip(both, done):
                cross_out[0, step] = (mixed / total).astype(jnp.bfloat16)
                stat_out[step] = as_row(top + jnp.log2(total))
            for step in both:
                cross_copy(0, step, peer).start()
                stat_copy(step, peer).start()

        repeat(steps // 2, first_part)

        def second_part(turn):
            both = (2 * turn, 2 * turn + 1)
            for step in both:
                arrived(2, steps + step)
                cross_copy(1, step, peer).wait_recv()
            done = attend([
                (cross_in[1, step], k_half[steps + step], v_half[steps + step], None)
                for step in both
            ])
            for step, (mixed, top, total) in zip(both, done):
                cross_out[2, step] = jnp.where(
                    by_query, (mixed / total).astype(jnp.bfloat16), v_half[steps + step]
                )
                stat_out[steps + step] = as_row(top + jnp.log2(total))
            for step in both:
                cross_copy(2, step, peer).start()
                stat_copy(steps + step, peer).start()

        repeat(steps // 2, second_part)

        def third_part(step):
            heads = (2 * step, 2 * step + 1)
            parts = (LOW, HIGH)
            cross_copy(2, step, peer).wait_recv()
            stat_copy(step, peer).wait_recv()
            for head in heads:
                arrived(0, head)
            logs = as_columns(jnp.where(by_query, stat_in[step], -1e30))
            near = [scores_of(q_half[head], k_half[head]) + bias_own[...] for head in heads]
            far = [
                scores_of(q_half[head], cross_in[1, step, part, :]) + bias_low[...]
                for head, part in zip(heads, parts)
            ]
            tops = [
                jnp.maximum(jnp.max(a, axis=1, keepdims=True), jnp.max(b, axis=1, keepdims=True))
                for a, b in zip(near, far)
            ]
            near = [weigh(score, top) for score, top in zip(near, tops)]
            far = [weigh(score, top) for score, top in zip(far, tops)]
            totals = [
                jnp.sum(a, axis=1, keepdims=True) + jnp.sum(b, axis=1, keepdims=True)
                for a, b in zip(near, far)
            ]
            others = [cross_in[2, step, part, :] for part in parts]
            mixes = [
                mix(a, v_half[head]) + mix(b, other)
                for a, b, head, other in zip(near, far, heads, others)
            ]
            for head, part, mixed, top, total, other in zip(
                heads, parts, mixes, tops, totals, others
            ):
                o_half[head, LOW, :] = (mixed[LOW] / total[LOW]).astype(jnp.bfloat16)
                o_half[head, HIGH, :] = merge(
                    mixed[HIGH], top[HIGH], total[HIGH],
                    other.astype(jnp.float32), logs[part],
                ).astype(jnp.bfloat16)
            for head in heads:
                result_copy(head, LOW, outer).start()
                result_local(head, HIGH).start()

        repeat(steps, third_part)

        def finish(step):
            for slot in range(3):
                cross_copy(slot, step, peer).wait_send()
            for side in range(2):
                stat_copy(2 * step + side, peer).wait_send()
                result_copy(2 * step + side, LOW, outer).wait_send()
                result_local(2 * step + side, HIGH).wait()

        repeat(steps, finish)

    @pl.when(me == 2)
    def _():
        peer, outer = me - 1, me + 1
        own_start(LOW)
        bias_own[...] = hidden(pair, pair, pair, pair, True)
        bias_high[...] = hidden(rows, rows, pair, pair, False)
        own_wait(LOW)

        def arrived(which, head):
            half_copy(which, head, HIGH, outer).wait_recv()

        def send_query(step):
            arrived(0, step)
            query_copy(step, peer).start()

        repeat(steps, send_query)

        def send_either(step):
            arrived(0, steps + step)
            for side, part in enumerate((LOW, HIGH)):
                cross_out[1, step, part, :] = jnp.where(
                    by_query, q_half[steps + step, part, :], k_half[2 * step + side, LOW, :]
                )
            cross_copy(1, step, peer).start()

        repeat(steps, send_either)

        def give(heads):
            for head in heads:
                result_copy(head, HIGH, outer).start()
                result_local(head, LOW).start()

        def span_and_low(step):
            heads = (2 * step, 2 * step + 1)
            parts = (LOW, HIGH)
            cross_copy(1, step, peer).wait_recv()
            for head in heads:
                arrived(1, head)
                arrived(2, head)
            cross_copy(0, step, peer).wait_recv()
            stat_copy(step, peer).wait_recv()
            done = attend(
                [
                    (cross_in[1, step, part, :], k_half[head], v_half[head], bias_high[...])
                    for head, part in zip(heads, parts)
                ]
                + [(q_half[step], k_half[step], v_half[step], bias_own[...])]
            )
            for head, part, (mixed, top, total) in zip(heads, parts, done):
                cross_out[2, step, part, :] = jnp.where(
                    by_query, (mixed / total).astype(jnp.bfloat16), v_half[head, LOW, :]
                )
            stat_out[step] = as_row(
                jnp.concatenate([top + jnp.log2(total) for mixed, top, total in done[:2]], axis=0)
            )
            mixed, top, total = done[2]
            o_half[step] = merge(
                mixed, top, total, cross_in[0, step].astype(jnp.float32),
                as_columns(stat_in[step]),
            ).astype(jnp.bfloat16)
            cross_copy(2, step, peer).start()
            stat_copy(step, peer).start()
            give((step,))

        def high_pair(turn):
            both = (2 * turn, 2 * turn + 1)
            for step in both:
                cross_copy(2, step, peer).wait_recv()
                stat_copy(steps + step, peer).wait_recv()
            done = attend(
                [
                    (q_half[steps + step], k_half[steps + step], v_half[steps + step], bias_own[...])
                    for step in both
                ]
                + [
                    (q_half[steps + step], cross_in[1, step], cross_in[2, step], None)
                    for step in both
                ]
            )
            for step, near, low in zip(both, done[:2], done[2:]):
                other = jnp.where(
                    by_query, cross_in[2, step].astype(jnp.float32), low[0] / low[2]
                )
                logs = jnp.where(
                    by_query, as_columns(stat_in[steps + step]),
                    jnp.broadcast_to(low[1] + jnp.log2(low[2]), (pair, HD)),
                )
                o_half[steps + step] = merge(*near, other, logs).astype(jnp.bfloat16)
            give([steps + step for step in both])

        early = steps // 2 + 1
        repeat(early, span_and_low)

        def late(turn):
            span_and_low(early + turn)
            high_pair(turn)

        repeat(steps - early, late)
        high_pair(steps - early)

        def finish(step):
            query_copy(step, peer).wait_send()
            for slot in (1, 2):
                cross_copy(slot, step, peer).wait_send()
            stat_copy(step, peer).wait_send()
            for side in range(2):
                result_copy(2 * step + side, HIGH, outer).wait_send()
                result_local(2 * step + side, LOW).wait()

        repeat(steps, finish)


def cut_body(queries, keys, values, span_starts):
    rows = queries.shape[0]
    pair = 2 * rows
    steps = HEADS // 2
    everything = pl.BlockSpec(memory_space=pltpu.HBM)
    dma = pltpu.SemaphoreType.DMA
    return pl.pallas_call(
        cut_kernel,
        out_shape=jax.ShapeDtypeStruct(queries.shape, jnp.bfloat16),
        in_specs=[pl.BlockSpec(memory_space=pltpu.SMEM), everything, everything, everything],
        out_specs=pl.BlockSpec(memory_space=pl.ANY),
        scratch_shapes=[pltpu.VMEM((HEADS, pair, HD), jnp.bfloat16)] * 4
        + [pltpu.VMEM((3, steps, pair, HD), jnp.bfloat16)] * 2
        + [pltpu.VMEM((HEADS, 1, pair), jnp.float32)] * 2
        + [
            pltpu.VMEM((pair, pair), jnp.float32),
            pltpu.VMEM((pair, rows), jnp.float32),
            pltpu.VMEM((rows, pair), jnp.float32),
            dma((3, HEADS)), dma((3, HEADS)), dma((3, HEADS)),
            dma((3, steps)), dma((3, steps)),
            dma((HEADS,)), dma((HEADS,)),
            dma((HEADS,)), dma((HEADS,)), dma((HEADS,)),
        ],
        compiler_params=pltpu.CompilerParams(
            collective_id=0, has_side_effects=True, vmem_limit_bytes=32 * 1024 * 1024
        ),
    )(span_starts, queries, keys, values)


def chosen_body(count, queries, keys, values, span_starts):
    rows, images = queries.shape[0], span_starts.shape[0]
    if count == 4 and images == 1 and SPAN <= 2 * rows and rows % 16 == 0:
        return cut_body(queries, keys, values, span_starts)
    if count % 2 == 0 and HEADS % count == 0:
        return exchange_body(count, queries, keys, values, span_starts)
    return ring_body(queries, keys, values, span_starts)


def solution(mesh):
    body = functools.partial(chosen_body, mesh.shape["ctx"])
    placed = (P(("dp", "ctx"), None), P(("dp", "ctx"), None), P(("dp", "ctx"), None), P("dp"))
    return jax.shard_map(
        body, mesh=mesh, in_specs=placed, out_specs=P(("dp", "ctx"), None), check_vma=False
    )
```

```python
import functools
import math

import jax
import jax.numpy as jnp
from jax import lax
from jax.experimental import pallas as pl
from jax.experimental.pallas import tpu as pltpu
from jax.sharding import PartitionSpec as P

HEADS = 16
HD = 128
SPAN = 288


def shifted(value, axis, steps):
    count = lax.axis_size(axis)
    pairs = [(source, (source + steps) % count) for source in range(count)]
    return lax.ppermute(value, axis, pairs)


def span_number(positions, span_starts):
    span_count = span_starts.shape[0]
    inside = (positions[:, None] >= span_starts[None, :]) & (
        positions[:, None] < span_starts[None, :] + SPAN
    )
    labels = jnp.arange(span_count, dtype=jnp.int32) + 1
    return jnp.sum(jnp.where(inside, labels[None, :], 0), axis=1)


def fold_block(operands):
    state_now, visible, group_query, key_heads, value_heads = operands
    row_max, row_sum, weighted = state_now
    scores = jnp.einsum(
        "qhd,khd->hqk", group_query, key_heads, preferred_element_type=jnp.float32
    ) * HD ** (-0.5)
    scores = jnp.where(visible[None], scores, -1e30)
    new_max = jnp.maximum(row_max, jnp.max(scores, axis=2))
    rescale = jnp.exp(row_max - new_max)
    weights = jnp.where(visible[None], jnp.exp(scores - new_max[:, :, None]), 0.0)
    new_sum = row_sum * rescale + jnp.sum(weights, axis=2)
    products = jnp.einsum(
        "hqk,khd->qhd",
        weights.astype(jnp.bfloat16),
        value_heads,
        preferred_element_type=jnp.float32,
    )
    new_weighted = weighted * rescale.T[:, :, None] + products
    return (new_max, new_sum, new_weighted)


def keep_block(operands):
    return operands[0]


def ring_body(queries, keys, values, span_starts):
    tok_rows = queries.shape[0]
    row_width = queries.shape[1]
    loop_size = lax.axis_size("ctx")
    loop_index = lax.axis_index("ctx")
    local_rows = jnp.arange(tok_rows, dtype=jnp.int32)
    query_pos = loop_index * tok_rows + local_rows
    query_span = span_number(query_pos, span_starts)
    query_heads = queries.reshape(tok_rows, HEADS, HD)
    group_count = 2
    group_rows = tok_rows // group_count
    empty_state = tuple(
        (
            (
                jnp.full((HEADS, group_rows), -1e30, jnp.float32),
                jnp.zeros((HEADS, group_rows), jnp.float32),
                jnp.zeros((group_rows, HEADS, HD), jnp.float32),
            )
            for number in range(group_count)
        )
    )

    def absorb(running, block_pair, key_start):
        key_block, value_block = block_pair
        block_rows = key_block.shape[0]
        key_pos = key_start + jnp.arange(block_rows, dtype=jnp.int32)
        key_span = span_number(key_pos, span_starts)
        key_heads = key_block.reshape(block_rows, HEADS, HD)
        value_heads = value_block.reshape(block_rows, HEADS, HD)
        updated = []
        for group_index in range(group_count):
            row_start = group_index * group_rows
            group_pos = query_pos[row_start : row_start + group_rows]
            group_span = query_span[row_start : row_start + group_rows]
            group_query = query_heads[row_start : row_start + group_rows]
            visible = (key_pos[None, :] <= group_pos[:, None]) | (
                group_span[:, None] == key_span[None, :]
            ) & (group_span[:, None] > 0)
            operands = (running[group_index], visible, group_query, key_heads, value_heads)
            updated.append(lax.cond(jnp.any(visible), fold_block, keep_block, operands))
        return tuple(updated)

    stacked = jnp.stack([keys, values])
    own_state = absorb(empty_state, (keys, values), loop_index * tok_rows)

    def advance(step_index, loop_state):
        running, upward, downward = loop_state
        upward = shifted(upward, "ctx", 1)
        downward = shifted(downward, "ctx", -1)
        source_up = (loop_index - 1 - step_index) % loop_size
        source_down = (loop_index + 1 + step_index) % loop_size
        running = absorb(running, (upward[0], upward[1]), source_up * tok_rows)
        running = absorb(running, (downward[0], downward[1]), source_down * tok_rows)
        return (running, upward, downward)

    final_state, upward, downward = lax.fori_loop(
        0, (loop_size - 1) // 2, advance, (own_state, stacked, stacked)
    )
    upward = shifted(upward, "ctx", 1)
    source_last = (loop_index - loop_size // 2) % loop_size
    final_state = absorb(final_state, (upward[0], upward[1]), source_last * tok_rows)
    pieces = [weighted / row_sum.T[:, :, None] for row_max, row_sum, weighted in final_state]
    attended = jnp.concatenate(pieces, axis=0).reshape(tok_rows, row_width).astype(jnp.bfloat16)
    return attended


def exchange_kernel(
    count, images, starts_ref, q_ref, k_ref, v_ref, out_ref,
    q_all, k_all, v_all, o_all, bias,
    in_send, in_recv, in_local, out_send, out_recv, out_local,
):
    me = lax.axis_index("ctx")
    rows = q_ref.shape[0]
    length = rows * count
    own_heads = HEADS // count
    half = count // 2
    side = me // half
    far = [(1 - side) * half + (me + i) % half for i in range(half)]
    near = [side * half + (me + i) % half for i in range(1, half)]
    peers = far + near
    my_rows = pl.ds(pl.multiple_of(me * rows, rows), rows)
    sources = (q_ref, k_ref, v_ref)
    landing = (q_all, k_all, v_all)

    def columns(owner, head):
        return pl.ds(pl.multiple_of((owner * own_heads + head) * HD, HD), HD)

    def rows_of(device):
        return pl.ds(pl.multiple_of(device * rows, rows), rows)

    def operand_copy(which, head, peer):
        return pltpu.make_async_remote_copy(
            src_ref=sources[which].at[:, columns(peer, head)],
            dst_ref=landing[which].at[head, my_rows, :],
            send_sem=in_send.at[which, head, peer],
            recv_sem=in_recv.at[which, head, me],
            device_id={"ctx": peer},
            device_id_type=pl.DeviceIdType.MESH,
        )

    def operand_arrival(which, head, peer):
        return pltpu.make_async_remote_copy(
            src_ref=sources[which].at[:, columns(peer, head)],
            dst_ref=landing[which].at[head, rows_of(peer), :],
            send_sem=in_send.at[which, head, peer],
            recv_sem=in_recv.at[which, head, peer],
            device_id={"ctx": peer},
            device_id_type=pl.DeviceIdType.MESH,
        )

    def operand_local(which, head):
        return pltpu.make_async_copy(
            sources[which].at[:, columns(me, head)],
            landing[which].at[head, my_rows, :],
            in_local.at[which, head],
        )

    def result_copy(head, peer):
        return pltpu.make_async_remote_copy(
            src_ref=o_all.at[head, rows_of(peer), :],
            dst_ref=out_ref.at[:, columns(me, head)],
            send_sem=out_send.at[head, peer],
            recv_sem=out_recv.at[head, me],
            device_id={"ctx": peer},
            device_id_type=pl.DeviceIdType.MESH,
        )

    def result_arrival(head, peer):
        return pltpu.make_async_remote_copy(
            src_ref=o_all.at[head, rows_of(peer), :],
            dst_ref=out_ref.at[:, columns(peer, head)],
            send_sem=out_send.at[head, peer],
            recv_sem=out_recv.at[head, peer],
            device_id={"ctx": peer},
            device_id_type=pl.DeviceIdType.MESH,
        )

    def result_local(head):
        return pltpu.make_async_copy(
            o_all.at[head, my_rows, :], out_ref.at[:, columns(me, head)], out_local.at[head]
        )

    barrier = pltpu.get_barrier_semaphore()
    for peer in peers:
        pl.semaphore_signal(
            barrier, inc=1, device_id={"ctx": peer}, device_id_type=pl.DeviceIdType.MESH
        )
    pl.semaphore_wait(barrier, count - 1)

    def send_head(head, carry):
        for peer in peers:
            for which in range(3):
                operand_copy(which, head, peer).start()
        for which in range(3):
            operand_local(which, head).start()
        return carry

    lax.fori_loop(0, own_heads, send_head, 0)

    query_pos = lax.broadcasted_iota(jnp.int32, (length, length), 0)
    key_pos = lax.broadcasted_iota(jnp.int32, (length, length), 1)
    visible = key_pos <= query_pos
    for image in range(images):
        first = starts_ref[image]
        inside = (
            (query_pos >= first) & (query_pos < first + SPAN)
            & (key_pos >= first) & (key_pos < first + SPAN)
        )
        visible = visible | inside
    bias[...] = jnp.where(visible, 0.0, -1e30)

    def attend_head(head, carry):
        for which in range(3):
            operand_local(which, head).wait()
            for peer in peers:
                operand_arrival(which, head, peer).wait_recv()
        scores = lax.dot_general(
            q_all[head], k_all[head], (((1,), (1,)), ((), ())),
            preferred_element_type=jnp.float32,
        ) * (HD ** (-0.5) * math.log2(math.e))
        scores = scores + bias[...]
        weights = jnp.exp2(scores - jnp.max(scores, axis=1, keepdims=True))
        total = jnp.sum(weights, axis=1, keepdims=True)
        mixed = jnp.dot(
            weights.astype(jnp.bfloat16), v_all[head], preferred_element_type=jnp.float32
        )
        o_all[head] = (mixed / total).astype(jnp.bfloat16)
        for peer in peers:
            result_copy(head, peer).start()
        result_local(head).start()
        return carry

    lax.fori_loop(0, own_heads, attend_head, 0)

    def finish_head(head, carry):
        result_local(head).wait()
        for peer in peers:
            for which in range(3):
                operand_copy(which, head, peer).wait_send()
            result_copy(head, peer).wait_send()
            result_arrival(head, peer).wait_recv()
        return carry

    lax.fori_loop(0, own_heads, finish_head, 0)


def exchange_body(count, queries, keys, values, span_starts):
    rows = queries.shape[0]
    length = rows * count
    own_heads = HEADS // count
    images = span_starts.shape[0]
    everything = pl.BlockSpec(memory_space=pltpu.HBM)
    return pl.pallas_call(
        functools.partial(exchange_kernel, count, images),
        out_shape=jax.ShapeDtypeStruct(queries.shape, jnp.bfloat16),
        in_specs=[pl.BlockSpec(memory_space=pltpu.SMEM), everything, everything, everything],
        out_specs=everything,
        scratch_shapes=[pltpu.VMEM((own_heads, length, HD), jnp.bfloat16)] * 4
        + [
            pltpu.VMEM((length, length), jnp.float32),
            pltpu.SemaphoreType.DMA((3, own_heads, count)),
            pltpu.SemaphoreType.DMA((3, own_heads, count)),
            pltpu.SemaphoreType.DMA((3, own_heads)),
            pltpu.SemaphoreType.DMA((own_heads, count)),
            pltpu.SemaphoreType.DMA((own_heads, count)),
            pltpu.SemaphoreType.DMA((own_heads,)),
        ],
        compiler_params=pltpu.CompilerParams(
            collective_id=0, has_side_effects=True, vmem_limit_bytes=56 * 1024 * 1024
        ),
    )(span_starts, queries, keys, values)


def cut_kernel(
    starts_ref, q_ref, k_ref, v_ref, out_ref,
    q_half, k_half, v_half, o_half, cross_in, cross_out, stat_in, stat_out,
    bias_own, bias_low, bias_high,
    half_send, half_recv, half_local, cross_send, cross_recv,
    stat_send, stat_recv, out_send, out_recv, out_local,
):
    me = lax.axis_index("ctx")
    rows = q_ref.shape[0]
    pair = 2 * rows
    steps = HEADS // 2
    scale = HD ** (-0.5) * math.log2(math.e)
    sources = (q_ref, k_ref, v_ref)
    halves = (q_half, k_half, v_half)
    first = starts_ref[0]
    by_query = first >= rows
    LOW, HIGH = slice(0, rows), slice(rows, pair)

    def columns(head):
        return pl.ds(pl.multiple_of(head * HD, HD), HD)

    def remote(src, dst, send, recv, peer):
        return pltpu.make_async_remote_copy(
            src_ref=src, dst_ref=dst, send_sem=send, recv_sem=recv,
            device_id={"ctx": peer}, device_id_type=pl.DeviceIdType.MESH,
        )

    def half_copy(which, head, part, peer):
        return remote(
            sources[which].at[:, columns(head)], halves[which].at[head, part, :],
            half_send.at[which, head], half_recv.at[which, head], peer,
        )

    def own_copy(which, head, part):
        return pltpu.make_async_copy(
            sources[which].at[:, columns(head)], halves[which].at[head, part, :],
            half_local.at[which, head],
        )

    def cross_copy(slot, step, peer):
        return remote(
            cross_out.at[slot, step], cross_in.at[slot, step],
            cross_send.at[slot, step], cross_recv.at[slot, step], peer,
        )

    def query_copy(step, peer):
        return remote(
            q_half.at[step], cross_in.at[0, step],
            cross_send.at[0, step], cross_recv.at[0, step], peer,
        )

    def stat_copy(step, peer):
        return remote(
            stat_out.at[step], stat_in.at[step], stat_send.at[step], stat_recv.at[step], peer
        )

    def result_copy(head, part, peer):
        return remote(
            o_half.at[head, part, :], out_ref.at[:, columns(head)],
            out_send.at[head], out_recv.at[head], peer,
        )

    def result_local(head, part):
        return pltpu.make_async_copy(
            o_half.at[head, part, :], out_ref.at[:, columns(head)], out_local.at[head]
        )

    def scores_of(query, key):
        return lax.dot_general(
            query, key, (((1,), (1,)), ((), ())), preferred_element_type=jnp.float32
        ) * scale

    def weigh(scores, top):
        return jnp.exp2(scores - top)

    def mix(weights, value):
        return jnp.dot(weights.astype(jnp.bfloat16), value, preferred_element_type=jnp.float32)

    def attend(items):
        scores = [
            scores_of(query, key) if bias is None else scores_of(query, key) + bias
            for query, key, value, bias in items
        ]
        tops = [jnp.max(score, axis=1, keepdims=True) for score in scores]
        weights = [weigh(score, top) for score, top in zip(scores, tops)]
        totals = [jnp.sum(weight, axis=1, keepdims=True) for weight in weights]
        mixed = [mix(weight, item[2]) for weight, item in zip(weights, items)]
        return list(zip(mixed, tops, totals))

    def as_row(column):
        return jnp.transpose(jnp.broadcast_to(column, (pair, HD)))[0:1, :]

    def as_columns(row):
        return jnp.transpose(jnp.broadcast_to(row, (HD, pair)))

    def merge(mixed, top, total, other, other_log):
        peak = jnp.maximum(top, other_log)
        mine, theirs = jnp.exp2(top - peak), jnp.exp2(other_log - peak)
        return (mixed * mine + other * theirs) / (total * mine + theirs)

    def hidden(query_start, query_rows, key_start, key_rows, causal):
        query_pos = query_start + lax.broadcasted_iota(jnp.int32, (query_rows, key_rows), 0)
        key_pos = key_start + lax.broadcasted_iota(jnp.int32, (query_rows, key_rows), 1)
        visible = (
            (query_pos >= first) & (query_pos < first + SPAN)
            & (key_pos >= first) & (key_pos < first + SPAN)
        )
        if causal:
            visible = visible | (key_pos <= query_pos)
        return jnp.where(visible, 0.0, -1e30)

    barrier = pltpu.get_barrier_semaphore()

    @pl.when(me > 0)
    def _():
        pl.semaphore_signal(
            barrier, inc=1, device_id={"ctx": me - 1}, device_id_type=pl.DeviceIdType.MESH
        )

    @pl.when(me < 3)
    def _():
        pl.semaphore_signal(
            barrier, inc=1, device_id={"ctx": me + 1}, device_id_type=pl.DeviceIdType.MESH
        )

    @pl.when((me == 0) | (me == 3))
    def _():
        pl.semaphore_wait(barrier, 1)

    @pl.when((me == 1) | (me == 2))
    def _():
        pl.semaphore_wait(barrier, 2)

    def repeat(count, one):
        lax.fori_loop(0, count, lambda step, carry: (one(step), carry)[1], 0)

    def outer_end(part, peer):
        def one(head):
            for which in range(3):
                half_copy(which, head, part, peer).wait_send()
            result_copy(head, part, peer).wait_recv()

        repeat(HEADS, one)

    @pl.when(me == 0)
    def _():
        def first_part(step):
            half_copy(1, step, LOW, me + 1).start()
            half_copy(2, step, LOW, me + 1).start()

        repeat(steps, lambda step: half_copy(1, steps + step, LOW, me + 1).start())
        repeat(steps, first_part)
        repeat(steps, lambda step: half_copy(2, steps + step, LOW, me + 1).start())
        repeat(HEADS, lambda head: half_copy(0, head, LOW, me + 1).start())
        outer_end(LOW, me + 1)

    @pl.when(me == 3)
    def _():
        repeat(HEADS, lambda head: half_copy(0, head, HIGH, me - 1).start())

        def pair_part(head):
            half_copy(1, head, HIGH, me - 1).start()
            half_copy(2, head, HIGH, me - 1).start()

        repeat(HEADS, pair_part)
        outer_end(HIGH, me - 1)

    def own_start(part):
        def one(head):
            for which in range(3):
                own_copy(which, head, part).start()

        repeat(HEADS, one)

    def own_wait(part):
        def one(head):
            for which in range(3):
                own_copy(which, head, part).wait()

        repeat(HEADS, one)

    @pl.when(me == 1)
    def _():
        peer, outer = me + 1, me - 1
        own_start(HIGH)
        bias_own[...] = hidden(0, pair, 0, pair, True)
        bias_low[...] = jnp.where(by_query, -1e30, hidden(0, pair, pair, rows, False))
        own_wait(HIGH)

        def arrived(which, head):
            half_copy(which, head, LOW, outer).wait_recv()

        def send_either(step):
            arrived(1, steps + step)
            for side, part in enumerate((LOW, HIGH)):
                cross_out[1, step, part, :] = jnp.where(
                    by_query, q_half[2 * step + side, HIGH, :], k_half[steps + step, part, :]
                )
            cross_copy(1, step, peer).start()

        repeat(steps, send_either)

        def first_part(turn):
            both = (2 * turn, 2 * turn + 1)
            for step in both:
                arrived(1, step)
                arrived(2, step)
                query_copy(step, peer).wait_recv()
            done = attend([(cross_in[0, step], k_half[step], v_half[step], None) for step in both])
            for step, (mixed, top, total) in zip(both, done):
                cross_out[0, step] = (mixed / total).astype(jnp.bfloat16)
                stat_out[step] = as_row(top + jnp.log2(total))
            for step in both:
                cross_copy(0, step, peer).start()
                stat_copy(step, peer).start()

        repeat(steps // 2, first_part)

        def second_part(turn):
            both = (2 * turn, 2 * turn + 1)
            for step in both:
                arrived(2, steps + step)
                cross_copy(1, step, peer).wait_recv()
            done = attend([
                (cross_in[1, step], k_half[steps + step], v_half[steps + step], None)
                for step in both
            ])
            for step, (mixed, top, total) in zip(both, done):
                cross_out[2, step] = jnp.where(
                    by_query, (mixed / total).astype(jnp.bfloat16), v_half[steps + step]
                )
                stat_out[steps + step] = as_row(top + jnp.log2(total))
            for step in both:
                cross_copy(2, step, peer).start()
                stat_copy(steps + step, peer).start()

        repeat(steps // 2, second_part)

        def third_part(step):
            heads = (2 * step, 2 * step + 1)
            parts = (LOW, HIGH)
            for head in heads:
                arrived(0, head)
            near = attend([
                (q_half[head], k_half[head], v_half[head], bias_own[...]) for head in heads
            ])
            cross_copy(2, step, peer).wait_recv()
            stat_copy(step, peer).wait_recv()
            logs = as_columns(jnp.where(by_query, stat_in[step], -1e30))
            far = attend([
                (q_half[head], cross_in[1, step, part, :], cross_in[2, step, part, :], bias_low[...])
                for head, part in zip(heads, parts)
            ])
            for head, part, own, span in zip(heads, parts, near, far):
                top = jnp.maximum(own[1], span[1])
                mine, theirs = jnp.exp2(own[1] - top), jnp.exp2(span[1] - top)
                mixed = own[0] * mine + span[0] * theirs
                total = own[2] * mine + span[2] * theirs
                o_half[head, LOW, :] = (mixed[LOW] / total[LOW]).astype(jnp.bfloat16)
                o_half[head, HIGH, :] = merge(
                    mixed[HIGH], top[HIGH], total[HIGH],
                    cross_in[2, step, part, :].astype(jnp.float32), logs[part],
                ).astype(jnp.bfloat16)
            for head in heads:
                result_copy(head, LOW, outer).start()
                result_local(head, HIGH).start()

        repeat(steps, third_part)

        def finish(step):
            for slot in range(3):
                cross_copy(slot, step, peer).wait_send()
            for side in range(2):
                stat_copy(2 * step + side, peer).wait_send()
                result_copy(2 * step + side, LOW, outer).wait_send()
                result_local(2 * step + side, HIGH).wait()

        repeat(steps, finish)

    @pl.when(me == 2)
    def _():
        peer, outer = me - 1, me + 1
        own_start(LOW)
        bias_own[...] = hidden(pair, pair, pair, pair, True)
        bias_high[...] = hidden(rows, rows, pair, pair, False)
        own_wait(LOW)

        def arrived(which, head):
            half_copy(which, head, HIGH, outer).wait_recv()

        def send_query(step):
            arrived(0, step)
            query_copy(step, peer).start()

        repeat(steps, send_query)

        def send_either(step):
            arrived(0, steps + step)
            for side, part in enumerate((LOW, HIGH)):
                cross_out[1, step, part, :] = jnp.where(
                    by_query, q_half[steps + step, part, :], k_half[2 * step + side, LOW, :]
                )
            cross_copy(1, step, peer).start()

        repeat(steps, send_either)

        def give(heads):
            for head in heads:
                result_copy(head, HIGH, outer).start()
                result_local(head, LOW).start()

        def span_and_low(step):
            heads = (2 * step, 2 * step + 1)
            parts = (LOW, HIGH)
            cross_copy(1, step, peer).wait_recv()
            for head in heads:
                arrived(1, head)
                arrived(2, head)
            done = attend([
                (cross_in[1, step, part, :], k_half[head], v_half[head], bias_high[...])
                for head, part in zip(heads, parts)
            ])
            for head, part, (mixed, top, total) in zip(heads, parts, done):
                cross_out[2, step, part, :] = jnp.where(
                    by_query, (mixed / total).astype(jnp.bfloat16), v_half[head, LOW, :]
                )
            stat_out[step] = as_row(
                jnp.concatenate([top + jnp.log2(total) for mixed, top, total in done], axis=0)
            )
            cross_copy(2, step, peer).start()
            stat_copy(step, peer).start()
            near = attend([(q_half[step], k_half[step], v_half[step], bias_own[...])])[0]
            cross_copy(0, step, peer).wait_recv()
            stat_copy(step, peer).wait_recv()
            o_half[step] = merge(
                *near, cross_in[0, step].astype(jnp.float32), as_columns(stat_in[step])
            ).astype(jnp.bfloat16)
            give((step,))

        def high_pair(turn):
            both = (2 * turn, 2 * turn + 1)
            near = attend([
                (q_half[steps + step], k_half[steps + step], v_half[steps + step], bias_own[...])
                for step in both
            ])
            low = [scores_of(q_half[steps + step], cross_in[1, step]) for step in both]
            tops = [jnp.max(scores, axis=1, keepdims=True) for scores in low]
            low = [weigh(scores, top) for scores, top in zip(low, tops)]
            totals = [jnp.sum(weights, axis=1, keepdims=True) for weights in low]
            for step in both:
                cross_copy(2, step, peer).wait_recv()
                stat_copy(steps + step, peer).wait_recv()
            for step, own, weights, top, total in zip(both, near, low, tops, totals):
                other = jnp.where(
                    by_query, cross_in[2, step].astype(jnp.float32),
                    mix(weights, cross_in[2, step]) / total,
                )
                logs = jnp.where(
                    by_query, as_columns(stat_in[steps + step]),
                    jnp.broadcast_to(top + jnp.log2(total), (pair, HD)),
                )
                o_half[steps + step] = merge(*own, other, logs).astype(jnp.bfloat16)
            give([steps + step for step in both])

        early = steps // 2 + 1
        repeat(early, span_and_low)

        def late(turn):
            span_and_low(early + turn)
            high_pair(turn)

        repeat(steps - early, late)
        high_pair(steps - early)

        def finish(step):
            query_copy(step, peer).wait_send()
            for slot in (1, 2):
                cross_copy(slot, step, peer).wait_send()
            stat_copy(step, peer).wait_send()
            for side in range(2):
                result_copy(2 * step + side, HIGH, outer).wait_send()
                result_local(2 * step + side, LOW).wait()

        repeat(steps, finish)


def cut_body(queries, keys, values, span_starts):
    rows = queries.shape[0]
    pair = 2 * rows
    steps = HEADS // 2
    everything = pl.BlockSpec(memory_space=pltpu.HBM)
    dma = pltpu.SemaphoreType.DMA
    return pl.pallas_call(
        cut_kernel,
        out_shape=pltpu.VMEM(queries.shape, jnp.bfloat16),
        in_specs=[pl.BlockSpec(memory_space=pltpu.SMEM), everything, everything, everything],
        out_specs=pl.BlockSpec(memory_space=pl.ANY),
        scratch_shapes=[pltpu.VMEM((HEADS, pair, HD), jnp.bfloat16)] * 4
        + [pltpu.VMEM((3, steps, pair, HD), jnp.bfloat16)] * 2
        + [pltpu.VMEM((HEADS, 1, pair), jnp.float32)] * 2
        + [
            pltpu.VMEM((pair, pair), jnp.float32),
            pltpu.VMEM((pair, rows), jnp.float32),
            pltpu.VMEM((rows, pair), jnp.float32),
            dma((3, HEADS)), dma((3, HEADS)), dma((3, HEADS)),
            dma((3, steps)), dma((3, steps)),
            dma((HEADS,)), dma((HEADS,)),
            dma((HEADS,)), dma((HEADS,)), dma((HEADS,)),
        ],
        compiler_params=pltpu.CompilerParams(
            collective_id=0, has_side_effects=True, vmem_limit_bytes=56 * 1024 * 1024
        ),
    )(span_starts, queries, keys, values)


def chosen_body(count, queries, keys, values, span_starts):
    rows, images = queries.shape[0], span_starts.shape[0]
    if count == 4 and images == 1 and SPAN <= 2 * rows and rows % 16 == 0:
        return cut_body(queries, keys, values, span_starts)
    if count % 2 == 0 and HEADS % count == 0:
        return exchange_body(count, queries, keys, values, span_starts)
    return ring_body(queries, keys, values, span_starts)


def solution(mesh):
    body = functools.partial(chosen_body, mesh.shape["ctx"])
    placed = (P(("dp", "ctx"), None), P(("dp", "ctx"), None), P(("dp", "ctx"), None), P("dp"))
    return jax.shard_map(
        body, mesh=mesh, in_specs=placed, out_specs=P(("dp", "ctx"), None), check_vma=False
    )
```

```python
import functools
import math

import jax
import jax.numpy as jnp
from jax import lax
from jax.experimental import pallas as pl
from jax.experimental.pallas import tpu as pltpu
from jax.sharding import PartitionSpec as P

HEADS = 16
HD = 128
SPAN = 288


def shifted(value, axis, steps):
    count = lax.axis_size(axis)
    pairs = [(source, (source + steps) % count) for source in range(count)]
    return lax.ppermute(value, axis, pairs)


def span_number(positions, span_starts):
    span_count = span_starts.shape[0]
    inside = (positions[:, None] >= span_starts[None, :]) & (
        positions[:, None] < span_starts[None, :] + SPAN
    )
    labels = jnp.arange(span_count, dtype=jnp.int32) + 1
    return jnp.sum(jnp.where(inside, labels[None, :], 0), axis=1)


def fold_block(operands):
    state_now, visible, group_query, key_heads, value_heads = operands
    row_max, row_sum, weighted = state_now
    scores = jnp.einsum(
        "qhd,khd->hqk", group_query, key_heads, preferred_element_type=jnp.float32
    ) * HD ** (-0.5)
    scores = jnp.where(visible[None], scores, -1e30)
    new_max = jnp.maximum(row_max, jnp.max(scores, axis=2))
    rescale = jnp.exp(row_max - new_max)
    weights = jnp.where(visible[None], jnp.exp(scores - new_max[:, :, None]), 0.0)
    new_sum = row_sum * rescale + jnp.sum(weights, axis=2)
    products = jnp.einsum(
        "hqk,khd->qhd",
        weights.astype(jnp.bfloat16),
        value_heads,
        preferred_element_type=jnp.float32,
    )
    new_weighted = weighted * rescale.T[:, :, None] + products
    return (new_max, new_sum, new_weighted)


def keep_block(operands):
    return operands[0]


def ring_body(queries, keys, values, span_starts):
    tok_rows = queries.shape[0]
    row_width = queries.shape[1]
    loop_size = lax.axis_size("ctx")
    loop_index = lax.axis_index("ctx")
    local_rows = jnp.arange(tok_rows, dtype=jnp.int32)
    query_pos = loop_index * tok_rows + local_rows
    query_span = span_number(query_pos, span_starts)
    query_heads = queries.reshape(tok_rows, HEADS, HD)
    group_count = 2
    group_rows = tok_rows // group_count
    empty_state = tuple(
        (
            (
                jnp.full((HEADS, group_rows), -1e30, jnp.float32),
                jnp.zeros((HEADS, group_rows), jnp.float32),
                jnp.zeros((group_rows, HEADS, HD), jnp.float32),
            )
            for number in range(group_count)
        )
    )

    def absorb(running, block_pair, key_start):
        key_block, value_block = block_pair
        block_rows = key_block.shape[0]
        key_pos = key_start + jnp.arange(block_rows, dtype=jnp.int32)
        key_span = span_number(key_pos, span_starts)
        key_heads = key_block.reshape(block_rows, HEADS, HD)
        value_heads = value_block.reshape(block_rows, HEADS, HD)
        updated = []
        for group_index in range(group_count):
            row_start = group_index * group_rows
            group_pos = query_pos[row_start : row_start + group_rows]
            group_span = query_span[row_start : row_start + group_rows]
            group_query = query_heads[row_start : row_start + group_rows]
            visible = (key_pos[None, :] <= group_pos[:, None]) | (
                group_span[:, None] == key_span[None, :]
            ) & (group_span[:, None] > 0)
            operands = (running[group_index], visible, group_query, key_heads, value_heads)
            updated.append(lax.cond(jnp.any(visible), fold_block, keep_block, operands))
        return tuple(updated)

    stacked = jnp.stack([keys, values])
    own_state = absorb(empty_state, (keys, values), loop_index * tok_rows)

    def advance(step_index, loop_state):
        running, upward, downward = loop_state
        upward = shifted(upward, "ctx", 1)
        downward = shifted(downward, "ctx", -1)
        source_up = (loop_index - 1 - step_index) % loop_size
        source_down = (loop_index + 1 + step_index) % loop_size
        running = absorb(running, (upward[0], upward[1]), source_up * tok_rows)
        running = absorb(running, (downward[0], downward[1]), source_down * tok_rows)
        return (running, upward, downward)

    final_state, upward, downward = lax.fori_loop(
        0, (loop_size - 1) // 2, advance, (own_state, stacked, stacked)
    )
    upward = shifted(upward, "ctx", 1)
    source_last = (loop_index - loop_size // 2) % loop_size
    final_state = absorb(final_state, (upward[0], upward[1]), source_last * tok_rows)
    pieces = [weighted / row_sum.T[:, :, None] for row_max, row_sum, weighted in final_state]
    attended = jnp.concatenate(pieces, axis=0).reshape(tok_rows, row_width).astype(jnp.bfloat16)
    return attended


def exchange_kernel(
    count, images, starts_ref, q_ref, k_ref, v_ref, out_ref,
    q_all, k_all, v_all, o_all, bias,
    in_send, in_recv, in_local, out_send, out_recv, out_local,
):
    me = lax.axis_index("ctx")
    rows = q_ref.shape[0]
    length = rows * count
    own_heads = HEADS // count
    half = count // 2
    side = me // half
    far = [(1 - side) * half + (me + i) % half for i in range(half)]
    near = [side * half + (me + i) % half for i in range(1, half)]
    peers = far + near
    my_rows = pl.ds(pl.multiple_of(me * rows, rows), rows)
    sources = (q_ref, k_ref, v_ref)
    landing = (q_all, k_all, v_all)

    def columns(owner, head):
        return pl.ds(pl.multiple_of((owner * own_heads + head) * HD, HD), HD)

    def rows_of(device):
        return pl.ds(pl.multiple_of(device * rows, rows), rows)

    def operand_copy(which, head, peer):
        return pltpu.make_async_remote_copy(
            src_ref=sources[which].at[:, columns(peer, head)],
            dst_ref=landing[which].at[head, my_rows, :],
            send_sem=in_send.at[which, head, peer],
            recv_sem=in_recv.at[which, head, me],
            device_id={"ctx": peer},
            device_id_type=pl.DeviceIdType.MESH,
        )

    def operand_arrival(which, head, peer):
        return pltpu.make_async_remote_copy(
            src_ref=sources[which].at[:, columns(peer, head)],
            dst_ref=landing[which].at[head, rows_of(peer), :],
            send_sem=in_send.at[which, head, peer],
            recv_sem=in_recv.at[which, head, peer],
            device_id={"ctx": peer},
            device_id_type=pl.DeviceIdType.MESH,
        )

    def operand_local(which, head):
        return pltpu.make_async_copy(
            sources[which].at[:, columns(me, head)],
            landing[which].at[head, my_rows, :],
            in_local.at[which, head],
        )

    def result_copy(head, peer):
        return pltpu.make_async_remote_copy(
            src_ref=o_all.at[head, rows_of(peer), :],
            dst_ref=out_ref.at[:, columns(me, head)],
            send_sem=out_send.at[head, peer],
            recv_sem=out_recv.at[head, me],
            device_id={"ctx": peer},
            device_id_type=pl.DeviceIdType.MESH,
        )

    def result_arrival(head, peer):
        return pltpu.make_async_remote_copy(
            src_ref=o_all.at[head, rows_of(peer), :],
            dst_ref=out_ref.at[:, columns(peer, head)],
            send_sem=out_send.at[head, peer],
            recv_sem=out_recv.at[head, peer],
            device_id={"ctx": peer},
            device_id_type=pl.DeviceIdType.MESH,
        )

    def result_local(head):
        return pltpu.make_async_copy(
            o_all.at[head, my_rows, :], out_ref.at[:, columns(me, head)], out_local.at[head]
        )

    barrier = pltpu.get_barrier_semaphore()
    for peer in peers:
        pl.semaphore_signal(
            barrier, inc=1, device_id={"ctx": peer}, device_id_type=pl.DeviceIdType.MESH
        )
    pl.semaphore_wait(barrier, count - 1)

    def send_head(head, carry):
        for peer in peers:
            for which in range(3):
                operand_copy(which, head, peer).start()
        for which in range(3):
            operand_local(which, head).start()
        return carry

    lax.fori_loop(0, own_heads, send_head, 0)

    query_pos = lax.broadcasted_iota(jnp.int32, (length, length), 0)
    key_pos = lax.broadcasted_iota(jnp.int32, (length, length), 1)
    visible = key_pos <= query_pos
    for image in range(images):
        first = starts_ref[image]
        inside = (
            (query_pos >= first) & (query_pos < first + SPAN)
            & (key_pos >= first) & (key_pos < first + SPAN)
        )
        visible = visible | inside
    bias[...] = jnp.where(visible, 0.0, -1e30)

    def attend_head(head, carry):
        for which in range(3):
            operand_local(which, head).wait()
            for peer in peers:
                operand_arrival(which, head, peer).wait_recv()
        scores = lax.dot_general(
            q_all[head], k_all[head], (((1,), (1,)), ((), ())),
            preferred_element_type=jnp.float32,
        ) * (HD ** (-0.5) * math.log2(math.e))
        scores = scores + bias[...]
        weights = jnp.exp2(scores - jnp.max(scores, axis=1, keepdims=True))
        total = jnp.sum(weights, axis=1, keepdims=True)
        mixed = jnp.dot(
            weights.astype(jnp.bfloat16), v_all[head], preferred_element_type=jnp.float32
        )
        o_all[head] = (mixed / total).astype(jnp.bfloat16)
        for peer in peers:
            result_copy(head, peer).start()
        result_local(head).start()
        return carry

    lax.fori_loop(0, own_heads, attend_head, 0)

    def finish_head(head, carry):
        result_local(head).wait()
        for peer in peers:
            for which in range(3):
                operand_copy(which, head, peer).wait_send()
            result_copy(head, peer).wait_send()
            result_arrival(head, peer).wait_recv()
        return carry

    lax.fori_loop(0, own_heads, finish_head, 0)


def exchange_body(count, queries, keys, values, span_starts):
    rows = queries.shape[0]
    length = rows * count
    own_heads = HEADS // count
    images = span_starts.shape[0]
    everything = pl.BlockSpec(memory_space=pltpu.HBM)
    return pl.pallas_call(
        functools.partial(exchange_kernel, count, images),
        out_shape=jax.ShapeDtypeStruct(queries.shape, jnp.bfloat16),
        in_specs=[pl.BlockSpec(memory_space=pltpu.SMEM), everything, everything, everything],
        out_specs=everything,
        scratch_shapes=[pltpu.VMEM((own_heads, length, HD), jnp.bfloat16)] * 4
        + [
            pltpu.VMEM((length, length), jnp.float32),
            pltpu.SemaphoreType.DMA((3, own_heads, count)),
            pltpu.SemaphoreType.DMA((3, own_heads, count)),
            pltpu.SemaphoreType.DMA((3, own_heads)),
            pltpu.SemaphoreType.DMA((own_heads, count)),
            pltpu.SemaphoreType.DMA((own_heads, count)),
            pltpu.SemaphoreType.DMA((own_heads,)),
        ],
        compiler_params=pltpu.CompilerParams(
            collective_id=0, has_side_effects=True, vmem_limit_bytes=56 * 1024 * 1024
        ),
    )(span_starts, queries, keys, values)


def cut_kernel(
    starts_ref, q_ref, k_ref, v_ref, out_ref,
    q_half, k_half, v_half, o_half, cross_in, cross_out, stat_in, stat_out,
    bias_own, bias_low, bias_high, kept,
    half_send, half_recv, half_local, cross_send, cross_recv,
    stat_send, stat_recv, out_send, out_recv, out_local,
):
    me = lax.axis_index("ctx")
    rows = q_ref.shape[0]
    pair = 2 * rows
    steps = HEADS // 2
    scale = HD ** (-0.5) * math.log2(math.e)
    sources = (q_ref, k_ref, v_ref)
    halves = (q_half, k_half, v_half)
    first = starts_ref[0]
    by_query = first >= rows
    LOW, HIGH = slice(0, rows), slice(rows, pair)

    def columns(head):
        return pl.ds(pl.multiple_of(head * HD, HD), HD)

    def remote(src, dst, send, recv, peer):
        return pltpu.make_async_remote_copy(
            src_ref=src, dst_ref=dst, send_sem=send, recv_sem=recv,
            device_id={"ctx": peer}, device_id_type=pl.DeviceIdType.MESH,
        )

    def half_copy(which, head, part, peer):
        return remote(
            sources[which].at[:, columns(head)], halves[which].at[head, part, :],
            half_send.at[which, head], half_recv.at[which, head], peer,
        )

    def own_copy(which, head, part):
        return pltpu.make_async_copy(
            sources[which].at[:, columns(head)], halves[which].at[head, part, :],
            half_local.at[which, head],
        )

    def cross_copy(slot, step, peer):
        return remote(
            cross_out.at[slot, step], cross_in.at[slot, step],
            cross_send.at[slot, step], cross_recv.at[slot, step], peer,
        )

    def query_copy(step, peer):
        return remote(
            q_half.at[step], cross_in.at[0, step],
            cross_send.at[0, step], cross_recv.at[0, step], peer,
        )

    def stat_copy(step, peer):
        return remote(
            stat_out.at[step], stat_in.at[step], stat_send.at[step], stat_recv.at[step], peer
        )

    def result_copy(head, part, peer):
        return remote(
            o_half.at[head, part, :], out_ref.at[:, columns(head)],
            out_send.at[head], out_recv.at[head], peer,
        )

    def result_local(head, part):
        return pltpu.make_async_copy(
            o_half.at[head, part, :], out_ref.at[:, columns(head)], out_local.at[head]
        )

    def scores_of(query, key):
        return lax.dot_general(
            query, key, (((1,), (1,)), ((), ())), preferred_element_type=jnp.float32
        ) * scale

    def weigh(scores, top):
        return jnp.exp2(scores - top)

    def mix(weights, value):
        return jnp.dot(weights.astype(jnp.bfloat16), value, preferred_element_type=jnp.float32)

    def attend(items):
        scores = [
            scores_of(query, key) if bias is None else scores_of(query, key) + bias
            for query, key, value, bias in items
        ]
        tops = [jnp.max(score, axis=1, keepdims=True) for score in scores]
        weights = [weigh(score, top) for score, top in zip(scores, tops)]
        totals = [jnp.sum(weight, axis=1, keepdims=True) for weight in weights]
        mixed = [mix(weight, item[2]) for weight, item in zip(weights, items)]
        return list(zip(mixed, tops, totals))

    def as_row(column):
        return jnp.transpose(jnp.broadcast_to(column, (pair, HD)))[0:1, :]

    def as_columns(row):
        return jnp.transpose(jnp.broadcast_to(row, (HD, pair)))

    def merge(mixed, top, total, other, other_log):
        peak = jnp.maximum(top, other_log)
        mine, theirs = jnp.exp2(top - peak), jnp.exp2(other_log - peak)
        return (mixed * mine + other * theirs) / (total * mine + theirs)

    def hidden(query_start, query_rows, key_start, key_rows, causal):
        query_pos = query_start + lax.broadcasted_iota(jnp.int32, (query_rows, key_rows), 0)
        key_pos = key_start + lax.broadcasted_iota(jnp.int32, (query_rows, key_rows), 1)
        visible = (
            (query_pos >= first) & (query_pos < first + SPAN)
            & (key_pos >= first) & (key_pos < first + SPAN)
        )
        if causal:
            visible = visible | (key_pos <= query_pos)
        return jnp.where(visible, 0.0, -1e30)

    barrier = pltpu.get_barrier_semaphore()

    @pl.when(me > 0)
    def _():
        pl.semaphore_signal(
            barrier, inc=1, device_id={"ctx": me - 1}, device_id_type=pl.DeviceIdType.MESH
        )

    @pl.when(me < 3)
    def _():
        pl.semaphore_signal(
            barrier, inc=1, device_id={"ctx": me + 1}, device_id_type=pl.DeviceIdType.MESH
        )

    @pl.when((me == 0) | (me == 3))
    def _():
        pl.semaphore_wait(barrier, 1)

    @pl.when((me == 1) | (me == 2))
    def _():
        pl.semaphore_wait(barrier, 2)

    def repeat(count, one):
        lax.fori_loop(0, count, lambda step, carry: (one(step), carry)[1], 0)

    def outer_end(part, peer):
        def one(head):
            for which in range(3):
                half_copy(which, head, part, peer).wait_send()
            result_copy(head, part, peer).wait_recv()

        repeat(HEADS, one)

    @pl.when(me == 0)
    def _():
        def first_part(step):
            half_copy(1, step, LOW, me + 1).start()
            half_copy(2, step, LOW, me + 1).start()

        repeat(steps, lambda step: half_copy(1, steps + step, LOW, me + 1).start())
        repeat(steps, first_part)
        repeat(steps, lambda step: half_copy(2, steps + step, LOW, me + 1).start())
        repeat(HEADS, lambda head: half_copy(0, head, LOW, me + 1).start())
        outer_end(LOW, me + 1)

    @pl.when(me == 3)
    def _():
        repeat(steps, lambda head: half_copy(0, head, HIGH, me - 1).start())

        def pair_part(head):
            half_copy(1, head, HIGH, me - 1).start()
            half_copy(2, head, HIGH, me - 1).start()

        def mixed_part(head):
            half_copy(0, steps + head, HIGH, me - 1).start()
            pair_part(head)

        repeat(steps, mixed_part)
        repeat(steps, lambda head: pair_part(steps + head))
        outer_end(HIGH, me - 1)

    def own_start(part):
        def one(head):
            for which in range(3):
                own_copy(which, head, part).start()

        repeat(HEADS, one)

    def own_wait(part):
        def one(head):
            for which in range(3):
                own_copy(which, head, part).wait()

        repeat(HEADS, one)

    @pl.when(me == 1)
    def _():
        peer, outer = me + 1, me - 1
        own_start(HIGH)
        bias_own[...] = hidden(0, pair, 0, pair, True)
        bias_low[...] = jnp.where(by_query, -1e30, hidden(0, pair, pair, rows, False))
        own_wait(HIGH)

        def arrived(which, head):
            half_copy(which, head, LOW, outer).wait_recv()

        def send_either(step):
            arrived(1, steps + step)
            for side, part in enumerate((LOW, HIGH)):
                cross_out[1, step, part, :] = jnp.where(
                    by_query, q_half[2 * step + side, HIGH, :], k_half[steps + step, part, :]
                )
            cross_copy(1, step, peer).start()

        repeat(steps, send_either)

        def first_part(turn):
            both = (2 * turn, 2 * turn + 1)
            for step in both:
                arrived(1, step)
                arrived(2, step)
                query_copy(step, peer).wait_recv()
            done = attend([(cross_in[0, step], k_half[step], v_half[step], None) for step in both])
            for step, (mixed, top, total) in zip(both, done):
                cross_out[0, step] = (mixed / total).astype(jnp.bfloat16)
                stat_out[step] = as_row(top + jnp.log2(total))
            for step in both:
                cross_copy(0, step, peer).start()
                stat_copy(step, peer).start()

        repeat(steps // 2, first_part)

        def second_part(turn):
            both = (2 * turn, 2 * turn + 1)
            for step in both:
                arrived(2, steps + step)
                cross_copy(1, step, peer).wait_recv()
            done = attend([
                (cross_in[1, step], k_half[steps + step], v_half[steps + step], None)
                for step in both
            ])
            for step, (mixed, top, total) in zip(both, done):
                cross_out[2, step] = jnp.where(
                    by_query, (mixed / total).astype(jnp.bfloat16), v_half[steps + step]
                )
                stat_out[steps + step] = as_row(top + jnp.log2(total))
            for step in both:
                cross_copy(2, step, peer).start()
                stat_copy(steps + step, peer).start()

        repeat(steps // 2, second_part)

        def third_part(step):
            heads = (2 * step, 2 * step + 1)
            parts = (LOW, HIGH)
            for head in heads:
                arrived(0, head)
            near = attend([
                (q_half[head], k_half[head], v_half[head], bias_own[...]) for head in heads
            ])
            cross_copy(2, step, peer).wait_recv()
            stat_copy(step, peer).wait_recv()
            logs = as_columns(jnp.where(by_query, stat_in[step], -1e30))
            far = attend([
                (q_half[head], cross_in[1, step, part, :], cross_in[2, step, part, :], bias_low[...])
                for head, part in zip(heads, parts)
            ])
            for head, part, own, span in zip(heads, parts, near, far):
                top = jnp.maximum(own[1], span[1])
                mine, theirs = jnp.exp2(own[1] - top), jnp.exp2(span[1] - top)
                mixed = own[0] * mine + span[0] * theirs
                total = own[2] * mine + span[2] * theirs
                o_half[head, LOW, :] = (mixed[LOW] / total[LOW]).astype(jnp.bfloat16)
                o_half[head, HIGH, :] = merge(
                    mixed[HIGH], top[HIGH], total[HIGH],
                    cross_in[2, step, part, :].astype(jnp.float32), logs[part],
                ).astype(jnp.bfloat16)
            for head in heads:
                result_copy(head, LOW, outer).start()
                result_local(head, HIGH).start()

        repeat(steps, third_part)

        def finish(step):
            for slot in range(3):
                cross_copy(slot, step, peer).wait_send()
            for side in range(2):
                stat_copy(2 * step + side, peer).wait_send()
                result_copy(2 * step + side, LOW, outer).wait_send()
                result_local(2 * step + side, HIGH).wait()

        repeat(steps, finish)

    @pl.when(me == 2)
    def _():
        peer, outer = me - 1, me + 1
        own_start(LOW)
        bias_own[...] = hidden(pair, pair, pair, pair, True)
        bias_high[...] = hidden(rows, rows, pair, pair, False)
        own_wait(LOW)

        def arrived(which, head):
            half_copy(which, head, HIGH, outer).wait_recv()

        def send_query(step):
            arrived(0, step)
            query_copy(step, peer).start()

        repeat(steps, send_query)

        def send_either(step):
            arrived(0, steps + step)
            for side, part in enumerate((LOW, HIGH)):
                cross_out[1, step, part, :] = jnp.where(
                    by_query, q_half[steps + step, part, :], k_half[2 * step + side, LOW, :]
                )
            cross_copy(1, step, peer).start()


        def give(heads):
            for head in heads:
                result_copy(head, HIGH, outer).start()
                result_local(head, LOW).start()

        def span_part(step):
            heads = (2 * step, 2 * step + 1)
            parts = (LOW, HIGH)
            cross_copy(1, step, peer).wait_recv()
            for head in heads:
                arrived(1, head)
                arrived(2, head)
            done = attend([
                (cross_in[1, step, part, :], k_half[head], v_half[head], bias_high[...])
                for head, part in zip(heads, parts)
            ])
            for head, part, (mixed, top, total) in zip(heads, parts, done):
                cross_out[2, step, part, :] = jnp.where(
                    by_query, (mixed / total).astype(jnp.bfloat16), v_half[head, LOW, :]
                )
            stat_out[step] = as_row(
                jnp.concatenate([top + jnp.log2(total) for mixed, top, total in done], axis=0)
            )
            cross_copy(2, step, peer).start()
            stat_copy(step, peer).start()

        def low_pair(turn):
            both = (2 * turn, 2 * turn + 1)
            near = attend([
                (q_half[step], k_half[step], v_half[step], bias_own[...]) for step in both
            ])
            for step in both:
                cross_copy(0, step, peer).wait_recv()
                stat_copy(step, peer).wait_recv()
            for step, own in zip(both, near):
                o_half[step] = merge(
                    *own, cross_in[0, step].astype(jnp.float32), as_columns(stat_in[step])
                ).astype(jnp.bfloat16)
            give(both)

        def high_near(turn):
            both = (2 * turn, 2 * turn + 1)
            near = attend([
                (q_half[steps + step], k_half[steps + step], v_half[steps + step], bias_own[...])
                for step in both
            ])
            for step, own in zip(both, near):
                for kind in range(3):
                    kept[kind, step] = jnp.broadcast_to(own[kind], (pair, HD))

        def high_pair(turn):
            both = (2 * turn, 2 * turn + 1)
            low = [scores_of(q_half[steps + step], cross_in[1, step]) for step in both]
            tops = [jnp.max(scores, axis=1, keepdims=True) for scores in low]
            low = [weigh(scores, top) for scores, top in zip(low, tops)]
            totals = [jnp.sum(weights, axis=1, keepdims=True) for weights in low]
            for step in both:
                cross_copy(2, step, peer).wait_recv()
                stat_copy(steps + step, peer).wait_recv()
            for step, weights, top, total in zip(both, low, tops, totals):
                other = jnp.where(
                    by_query, cross_in[2, step].astype(jnp.float32),
                    mix(weights, cross_in[2, step]) / total,
                )
                logs = jnp.where(
                    by_query, as_columns(stat_in[steps + step]),
                    jnp.broadcast_to(top + jnp.log2(total), (pair, HD)),
                )
                o_half[steps + step] = merge(
                    kept[0, step], kept[1, step], kept[2, step], other, logs
                ).astype(jnp.bfloat16)
            give([steps + step for step in both])

        def send_and_span(step):
            send_either(2 * step)
            send_either(2 * step + 1)
            span_part(step)

        quarter = steps // 2
        send_and_span(0)

        def early(turn):
            send_and_span(1 + turn)
            low_pair(turn)

        repeat(quarter - 1, early)
        span_part(quarter)
        low_pair(quarter - 1)
        high_near(0)

        def late(turn):
            span_part(quarter + 1 + turn)
            high_near(1 + turn)
            high_pair(turn)

        repeat(quarter - 2, late)
        high_pair(quarter - 2)
        span_part(steps - 1)
        high_near(quarter - 1)
        high_pair(quarter - 1)

        def finish(step):
            query_copy(step, peer).wait_send()
            for slot in (1, 2):
                cross_copy(slot, step, peer).wait_send()
            stat_copy(step, peer).wait_send()
            for side in range(2):
                result_copy(2 * step + side, HIGH, outer).wait_send()
                result_local(2 * step + side, LOW).wait()

        repeat(steps, finish)


def cut_body(queries, keys, values, span_starts):
    rows = queries.shape[0]
    pair = 2 * rows
    steps = HEADS // 2
    everything = pl.BlockSpec(memory_space=pltpu.HBM)
    dma = pltpu.SemaphoreType.DMA
    return pl.pallas_call(
        cut_kernel,
        out_shape=pltpu.VMEM(queries.shape, jnp.bfloat16),
        in_specs=[pl.BlockSpec(memory_space=pltpu.SMEM), everything, everything, everything],
        out_specs=pl.BlockSpec(memory_space=pl.ANY),
        scratch_shapes=[pltpu.VMEM((HEADS, pair, HD), jnp.bfloat16)] * 4
        + [pltpu.VMEM((3, steps, pair, HD), jnp.bfloat16)] * 2
        + [pltpu.VMEM((HEADS, 1, pair), jnp.float32)] * 2
        + [
            pltpu.VMEM((pair, pair), jnp.float32),
            pltpu.VMEM((pair, rows), jnp.float32),
            pltpu.VMEM((rows, pair), jnp.float32),
            pltpu.VMEM((3, steps, pair, HD), jnp.float32),
            dma((3, HEADS)), dma((3, HEADS)), dma((3, HEADS)),
            dma((3, steps)), dma((3, steps)),
            dma((HEADS,)), dma((HEADS,)),
            dma((HEADS,)), dma((HEADS,)), dma((HEADS,)),
        ],
        compiler_params=pltpu.CompilerParams(
            collective_id=0, has_side_effects=True, vmem_limit_bytes=56 * 1024 * 1024
        ),
    )(span_starts, queries, keys, values)


def chosen_body(count, queries, keys, values, span_starts):
    rows, images = queries.shape[0], span_starts.shape[0]
    if count == 4 and images == 1 and SPAN <= 2 * rows and rows % 16 == 0:
        return cut_body(queries, keys, values, span_starts)
    if count % 2 == 0 and HEADS % count == 0:
        return exchange_body(count, queries, keys, values, span_starts)
    return ring_body(queries, keys, values, span_starts)


def solution(mesh):
    body = functools.partial(chosen_body, mesh.shape["ctx"])
    placed = (P(("dp", "ctx"), None), P(("dp", "ctx"), None), P(("dp", "ctx"), None), P("dp"))
    return jax.shard_map(
        body, mesh=mesh, in_specs=placed, out_specs=P(("dp", "ctx"), None), check_vma=False
    )
```

```python
import functools
import math

import jax
import jax.numpy as jnp
from jax import lax
from jax.experimental import pallas as pl
from jax.experimental.pallas import tpu as pltpu
from jax.sharding import PartitionSpec as P

HEADS = 16
HD = 128
SPAN = 288


def shifted(value, axis, steps):
    count = lax.axis_size(axis)
    pairs = [(source, (source + steps) % count) for source in range(count)]
    return lax.ppermute(value, axis, pairs)


def span_number(positions, span_starts):
    span_count = span_starts.shape[0]
    inside = (positions[:, None] >= span_starts[None, :]) & (
        positions[:, None] < span_starts[None, :] + SPAN
    )
    labels = jnp.arange(span_count, dtype=jnp.int32) + 1
    return jnp.sum(jnp.where(inside, labels[None, :], 0), axis=1)


def fold_block(operands):
    state_now, visible, group_query, key_heads, value_heads = operands
    row_max, row_sum, weighted = state_now
    scores = jnp.einsum(
        "qhd,khd->hqk", group_query, key_heads, preferred_element_type=jnp.float32
    ) * HD ** (-0.5)
    scores = jnp.where(visible[None], scores, -1e30)
    new_max = jnp.maximum(row_max, jnp.max(scores, axis=2))
    rescale = jnp.exp(row_max - new_max)
    weights = jnp.where(visible[None], jnp.exp(scores - new_max[:, :, None]), 0.0)
    new_sum = row_sum * rescale + jnp.sum(weights, axis=2)
    products = jnp.einsum(
        "hqk,khd->qhd",
        weights.astype(jnp.bfloat16),
        value_heads,
        preferred_element_type=jnp.float32,
    )
    new_weighted = weighted * rescale.T[:, :, None] + products
    return (new_max, new_sum, new_weighted)


def keep_block(operands):
    return operands[0]


def ring_body(queries, keys, values, span_starts):
    tok_rows = queries.shape[0]
    row_width = queries.shape[1]
    loop_size = lax.axis_size("ctx")
    loop_index = lax.axis_index("ctx")
    local_rows = jnp.arange(tok_rows, dtype=jnp.int32)
    query_pos = loop_index * tok_rows + local_rows
    query_span = span_number(query_pos, span_starts)
    query_heads = queries.reshape(tok_rows, HEADS, HD)
    group_count = 2
    group_rows = tok_rows // group_count
    empty_state = tuple(
        (
            (
                jnp.full((HEADS, group_rows), -1e30, jnp.float32),
                jnp.zeros((HEADS, group_rows), jnp.float32),
                jnp.zeros((group_rows, HEADS, HD), jnp.float32),
            )
            for number in range(group_count)
        )
    )

    def absorb(running, block_pair, key_start):
        key_block, value_block = block_pair
        block_rows = key_block.shape[0]
        key_pos = key_start + jnp.arange(block_rows, dtype=jnp.int32)
        key_span = span_number(key_pos, span_starts)
        key_heads = key_block.reshape(block_rows, HEADS, HD)
        value_heads = value_block.reshape(block_rows, HEADS, HD)
        updated = []
        for group_index in range(group_count):
            row_start = group_index * group_rows
            group_pos = query_pos[row_start : row_start + group_rows]
            group_span = query_span[row_start : row_start + group_rows]
            group_query = query_heads[row_start : row_start + group_rows]
            visible = (key_pos[None, :] <= group_pos[:, None]) | (
                group_span[:, None] == key_span[None, :]
            ) & (group_span[:, None] > 0)
            operands = (running[group_index], visible, group_query, key_heads, value_heads)
            updated.append(lax.cond(jnp.any(visible), fold_block, keep_block, operands))
        return tuple(updated)

    stacked = jnp.stack([keys, values])
    own_state = absorb(empty_state, (keys, values), loop_index * tok_rows)

    def advance(step_index, loop_state):
        running, upward, downward = loop_state
        upward = shifted(upward, "ctx", 1)
        downward = shifted(downward, "ctx", -1)
        source_up = (loop_index - 1 - step_index) % loop_size
        source_down = (loop_index + 1 + step_index) % loop_size
        running = absorb(running, (upward[0], upward[1]), source_up * tok_rows)
        running = absorb(running, (downward[0], downward[1]), source_down * tok_rows)
        return (running, upward, downward)

    final_state, upward, downward = lax.fori_loop(
        0, (loop_size - 1) // 2, advance, (own_state, stacked, stacked)
    )
    upward = shifted(upward, "ctx", 1)
    source_last = (loop_index - loop_size // 2) % loop_size
    final_state = absorb(final_state, (upward[0], upward[1]), source_last * tok_rows)
    pieces = [weighted / row_sum.T[:, :, None] for row_max, row_sum, weighted in final_state]
    attended = jnp.concatenate(pieces, axis=0).reshape(tok_rows, row_width).astype(jnp.bfloat16)
    return attended


def exchange_kernel(
    count, images, starts_ref, q_ref, k_ref, v_ref, out_ref,
    q_all, k_all, v_all, o_all, bias,
    in_send, in_recv, in_local, out_send, out_recv, out_local,
):
    me = lax.axis_index("ctx")
    rows = q_ref.shape[0]
    length = rows * count
    own_heads = HEADS // count
    half = count // 2
    side = me // half
    far = [(1 - side) * half + (me + i) % half for i in range(half)]
    near = [side * half + (me + i) % half for i in range(1, half)]
    peers = far + near
    my_rows = pl.ds(pl.multiple_of(me * rows, rows), rows)
    sources = (q_ref, k_ref, v_ref)
    landing = (q_all, k_all, v_all)

    def columns(owner, head):
        return pl.ds(pl.multiple_of((owner * own_heads + head) * HD, HD), HD)

    def rows_of(device):
        return pl.ds(pl.multiple_of(device * rows, rows), rows)

    def operand_copy(which, head, peer):
        return pltpu.make_async_remote_copy(
            src_ref=sources[which].at[:, columns(peer, head)],
            dst_ref=landing[which].at[head, my_rows, :],
            send_sem=in_send.at[which, head, peer],
            recv_sem=in_recv.at[which, head, me],
            device_id={"ctx": peer},
            device_id_type=pl.DeviceIdType.MESH,
        )

    def operand_arrival(which, head, peer):
        return pltpu.make_async_remote_copy(
            src_ref=sources[which].at[:, columns(peer, head)],
            dst_ref=landing[which].at[head, rows_of(peer), :],
            send_sem=in_send.at[which, head, peer],
            recv_sem=in_recv.at[which, head, peer],
            device_id={"ctx": peer},
            device_id_type=pl.DeviceIdType.MESH,
        )

    def operand_local(which, head):
        return pltpu.make_async_copy(
            sources[which].at[:, columns(me, head)],
            landing[which].at[head, my_rows, :],
            in_local.at[which, head],
        )

    def result_copy(head, peer):
        return pltpu.make_async_remote_copy(
            src_ref=o_all.at[head, rows_of(peer), :],
            dst_ref=out_ref.at[:, columns(me, head)],
            send_sem=out_send.at[head, peer],
            recv_sem=out_recv.at[head, me],
            device_id={"ctx": peer},
            device_id_type=pl.DeviceIdType.MESH,
        )

    def result_arrival(head, peer):
        return pltpu.make_async_remote_copy(
            src_ref=o_all.at[head, rows_of(peer), :],
            dst_ref=out_ref.at[:, columns(peer, head)],
            send_sem=out_send.at[head, peer],
            recv_sem=out_recv.at[head, peer],
            device_id={"ctx": peer},
            device_id_type=pl.DeviceIdType.MESH,
        )

    def result_local(head):
        return pltpu.make_async_copy(
            o_all.at[head, my_rows, :], out_ref.at[:, columns(me, head)], out_local.at[head]
        )

    barrier = pltpu.get_barrier_semaphore()
    for peer in peers:
        pl.semaphore_signal(
            barrier, inc=1, device_id={"ctx": peer}, device_id_type=pl.DeviceIdType.MESH
        )
    pl.semaphore_wait(barrier, count - 1)

    def send_head(head, carry):
        for peer in peers:
            for which in range(3):
                operand_copy(which, head, peer).start()
        for which in range(3):
            operand_local(which, head).start()
        return carry

    lax.fori_loop(0, own_heads, send_head, 0)

    query_pos = lax.broadcasted_iota(jnp.int32, (length, length), 0)
    key_pos = lax.broadcasted_iota(jnp.int32, (length, length), 1)
    visible = key_pos <= query_pos
    for image in range(images):
        first = starts_ref[image]
        inside = (
            (query_pos >= first) & (query_pos < first + SPAN)
            & (key_pos >= first) & (key_pos < first + SPAN)
        )
        visible = visible | inside
    bias[...] = jnp.where(visible, 0.0, -1e30)

    def attend_head(head, carry):
        for which in range(3):
            operand_local(which, head).wait()
            for peer in peers:
                operand_arrival(which, head, peer).wait_recv()
        scores = lax.dot_general(
            q_all[head], k_all[head], (((1,), (1,)), ((), ())),
            preferred_element_type=jnp.float32,
        ) * (HD ** (-0.5) * math.log2(math.e))
        scores = scores + bias[...]
        weights = jnp.exp2(scores - jnp.max(scores, axis=1, keepdims=True))
        total = jnp.sum(weights, axis=1, keepdims=True)
        mixed = jnp.dot(
            weights.astype(jnp.bfloat16), v_all[head], preferred_element_type=jnp.float32
        )
        o_all[head] = (mixed / total).astype(jnp.bfloat16)
        for peer in peers:
            result_copy(head, peer).start()
        result_local(head).start()
        return carry

    lax.fori_loop(0, own_heads, attend_head, 0)

    def finish_head(head, carry):
        result_local(head).wait()
        for peer in peers:
            for which in range(3):
                operand_copy(which, head, peer).wait_send()
            result_copy(head, peer).wait_send()
            result_arrival(head, peer).wait_recv()
        return carry

    lax.fori_loop(0, own_heads, finish_head, 0)


def exchange_body(count, queries, keys, values, span_starts):
    rows = queries.shape[0]
    length = rows * count
    own_heads = HEADS // count
    images = span_starts.shape[0]
    everything = pl.BlockSpec(memory_space=pltpu.HBM)
    return pl.pallas_call(
        functools.partial(exchange_kernel, count, images),
        out_shape=jax.ShapeDtypeStruct(queries.shape, jnp.bfloat16),
        in_specs=[pl.BlockSpec(memory_space=pltpu.SMEM), everything, everything, everything],
        out_specs=everything,
        scratch_shapes=[pltpu.VMEM((own_heads, length, HD), jnp.bfloat16)] * 4
        + [
            pltpu.VMEM((length, length), jnp.float32),
            pltpu.SemaphoreType.DMA((3, own_heads, count)),
            pltpu.SemaphoreType.DMA((3, own_heads, count)),
            pltpu.SemaphoreType.DMA((3, own_heads)),
            pltpu.SemaphoreType.DMA((own_heads, count)),
            pltpu.SemaphoreType.DMA((own_heads, count)),
            pltpu.SemaphoreType.DMA((own_heads,)),
        ],
        compiler_params=pltpu.CompilerParams(
            collective_id=0, has_side_effects=True, vmem_limit_bytes=56 * 1024 * 1024
        ),
    )(span_starts, queries, keys, values)


def cut_kernel(
    starts_ref, q_ref, k_ref, v_ref, out_ref,
    q_half, k_half, v_half, o_half, cross_in, cross_out, stat_in, stat_out,
    bias_own, bias_low, bias_high, kept,
    half_send, half_recv, half_local, cross_send, cross_recv,
    stat_send, stat_recv, out_send, out_recv, out_local,
):
    me = lax.axis_index("ctx")
    rows = q_ref.shape[0]
    pair = 2 * rows
    steps = HEADS // 2
    scale = HD ** (-0.5) * math.log2(math.e)
    sources = (q_ref, k_ref, v_ref)
    halves = (q_half, k_half, v_half)
    first = starts_ref[0]
    by_query = first >= rows
    LOW, HIGH = slice(0, rows), slice(rows, pair)

    def columns(head):
        return pl.ds(pl.multiple_of(head * HD, HD), HD)

    def remote(src, dst, send, recv, peer):
        return pltpu.make_async_remote_copy(
            src_ref=src, dst_ref=dst, send_sem=send, recv_sem=recv,
            device_id={"ctx": peer}, device_id_type=pl.DeviceIdType.MESH,
        )

    def half_copy(which, head, part, peer):
        return remote(
            sources[which].at[:, columns(head)], halves[which].at[head, part, :],
            half_send.at[which, head], half_recv.at[which, head], peer,
        )

    def own_copy(which, head, part):
        return pltpu.make_async_copy(
            sources[which].at[:, columns(head)], halves[which].at[head, part, :],
            half_local.at[which, head],
        )

    def cross_copy(slot, step, peer):
        return remote(
            cross_out.at[slot, step], cross_in.at[slot, step],
            cross_send.at[slot, step], cross_recv.at[slot, step], peer,
        )

    def query_copy(step, peer):
        return remote(
            q_half.at[step], cross_in.at[0, step],
            cross_send.at[0, step], cross_recv.at[0, step], peer,
        )

    def stat_copy(step, peer):
        return remote(
            stat_out.at[step], stat_in.at[step], stat_send.at[step], stat_recv.at[step], peer
        )

    def result_copy(head, part, peer):
        return remote(
            o_half.at[head, part, :], out_ref.at[:, columns(head)],
            out_send.at[head], out_recv.at[head], peer,
        )

    def result_local(head, part):
        return pltpu.make_async_copy(
            o_half.at[head, part, :], out_ref.at[:, columns(head)], out_local.at[head]
        )

    def scores_of(query, key):
        return lax.dot_general(
            query, key, (((1,), (1,)), ((), ())), preferred_element_type=jnp.float32
        ) * scale

    def weigh(scores, top):
        return jnp.exp2(scores - top)

    def mix(weights, value):
        return jnp.dot(weights.astype(jnp.bfloat16), value, preferred_element_type=jnp.float32)

    def attend(items):
        scores = [
            scores_of(query, key) if bias is None else scores_of(query, key) + bias
            for query, key, value, bias in items
        ]
        tops = [jnp.max(score, axis=1, keepdims=True) for score in scores]
        weights = [weigh(score, top) for score, top in zip(scores, tops)]
        totals = [jnp.sum(weight, axis=1, keepdims=True) for weight in weights]
        mixed = [mix(weight, item[2]) for weight, item in zip(weights, items)]
        return list(zip(mixed, tops, totals))

    def as_row(column):
        return jnp.transpose(jnp.broadcast_to(column, (pair, HD)))[0:1, :]

    def as_columns(row):
        return jnp.transpose(jnp.broadcast_to(row, (HD, pair)))

    def merge(mixed, top, total, other, other_log):
        peak = jnp.maximum(top, other_log)
        mine, theirs = jnp.exp2(top - peak), jnp.exp2(other_log - peak)
        return (mixed * mine + other * theirs) / (total * mine + theirs)

    def hidden(query_start, query_rows, key_start, key_rows, causal):
        query_pos = query_start + lax.broadcasted_iota(jnp.int32, (query_rows, key_rows), 0)
        key_pos = key_start + lax.broadcasted_iota(jnp.int32, (query_rows, key_rows), 1)
        visible = (
            (query_pos >= first) & (query_pos < first + SPAN)
            & (key_pos >= first) & (key_pos < first + SPAN)
        )
        if causal:
            visible = visible | (key_pos <= query_pos)
        return jnp.where(visible, 0.0, -1e30)

    barrier = pltpu.get_barrier_semaphore()

    @pl.when(me > 0)
    def _():
        pl.semaphore_signal(
            barrier, inc=1, device_id={"ctx": me - 1}, device_id_type=pl.DeviceIdType.MESH
        )

    @pl.when(me < 3)
    def _():
        pl.semaphore_signal(
            barrier, inc=1, device_id={"ctx": me + 1}, device_id_type=pl.DeviceIdType.MESH
        )

    @pl.when((me == 0) | (me == 3))
    def _():
        pl.semaphore_wait(barrier, 1)

    @pl.when((me == 1) | (me == 2))
    def _():
        pl.semaphore_wait(barrier, 2)

    def repeat(count, one):
        lax.fori_loop(0, count, lambda step, carry: (one(step), carry)[1], 0)

    def outer_end(part, peer):
        def one(head):
            for which in range(3):
                half_copy(which, head, part, peer).wait_send()
            result_copy(head, part, peer).wait_recv()

        repeat(HEADS, one)

    @pl.when(me == 0)
    def _():
        def first_part(step):
            half_copy(1, step, LOW, me + 1).start()
            half_copy(2, step, LOW, me + 1).start()

        repeat(steps, lambda step: half_copy(1, steps + step, LOW, me + 1).start())
        repeat(steps, first_part)

        def second_part(step):
            half_copy(2, steps + step, LOW, me + 1).start()
            half_copy(0, step, LOW, me + 1).start()

        repeat(steps, second_part)
        repeat(steps, lambda step: half_copy(0, steps + step, LOW, me + 1).start())
        outer_end(LOW, me + 1)

    @pl.when(me == 3)
    def _():
        repeat(steps, lambda head: half_copy(0, head, HIGH, me - 1).start())

        def pair_part(head):
            half_copy(1, head, HIGH, me - 1).start()
            half_copy(2, head, HIGH, me - 1).start()

        def mixed_part(head):
            half_copy(0, steps + head, HIGH, me - 1).start()
            pair_part(head)

        repeat(steps, mixed_part)
        repeat(steps, lambda head: pair_part(steps + head))
        outer_end(HIGH, me - 1)

    def own_start(part):
        def one(head):
            for which in range(3):
                own_copy(which, head, part).start()

        repeat(HEADS, one)

    def own_wait(part):
        def one(head):
            for which in range(3):
                own_copy(which, head, part).wait()

        repeat(HEADS, one)

    @pl.when(me == 1)
    def _():
        peer, outer = me + 1, me - 1
        own_start(HIGH)
        bias_own[...] = hidden(0, pair, 0, pair, True)
        bias_low[...] = jnp.where(by_query, -1e30, hidden(0, pair, pair, rows, False))
        own_wait(HIGH)

        def arrived(which, head):
            half_copy(which, head, LOW, outer).wait_recv()

        def send_either(step):
            arrived(1, steps + step)
            for side, part in enumerate((LOW, HIGH)):
                cross_out[1, step, part, :] = jnp.where(
                    by_query, q_half[2 * step + side, HIGH, :], k_half[steps + step, part, :]
                )
            cross_copy(1, step, peer).start()

        repeat(steps, send_either)

        def first_part(turn):
            both = (2 * turn, 2 * turn + 1)
            for step in both:
                arrived(1, step)
                arrived(2, step)
                query_copy(step, peer).wait_recv()
            done = attend([(cross_in[0, step], k_half[step], v_half[step], None) for step in both])
            for step, (mixed, top, total) in zip(both, done):
                cross_out[0, step] = (mixed / total).astype(jnp.bfloat16)
                stat_out[step] = as_row(top + jnp.log2(total))
            for step in both:
                cross_copy(0, step, peer).start()
                stat_copy(step, peer).start()

        repeat(steps // 2, first_part)

        def second_part(turn):
            both = (2 * turn, 2 * turn + 1)
            for step in both:
                arrived(2, steps + step)
                cross_copy(1, step, peer).wait_recv()
            done = attend([
                (cross_in[1, step], k_half[steps + step], v_half[steps + step], None)
                for step in both
            ])
            for step, (mixed, top, total) in zip(both, done):
                cross_out[2, step] = jnp.where(
                    by_query, (mixed / total).astype(jnp.bfloat16), v_half[steps + step]
                )
                stat_out[steps + step] = as_row(top + jnp.log2(total))
            for step in both:
                cross_copy(2, step, peer).start()
                stat_copy(steps + step, peer).start()

        def third_part(step):
            heads = (2 * step, 2 * step + 1)
            parts = (LOW, HIGH)
            for head in heads:
                arrived(0, head)
            near = attend([
                (q_half[head], k_half[head], v_half[head], bias_own[...]) for head in heads
            ])
            cross_copy(2, step, peer).wait_recv()
            stat_copy(step, peer).wait_recv()
            logs = as_columns(jnp.where(by_query, stat_in[step], -1e30))
            far = attend([
                (q_half[head], cross_in[1, step, part, :], cross_in[2, step, part, :], bias_low[...])
                for head, part in zip(heads, parts)
            ])
            for head, part, own, span in zip(heads, parts, near, far):
                top = jnp.maximum(own[1], span[1])
                mine, theirs = jnp.exp2(own[1] - top), jnp.exp2(span[1] - top)
                mixed = own[0] * mine + span[0] * theirs
                total = own[2] * mine + span[2] * theirs
                o_half[head, LOW, :] = (mixed[LOW] / total[LOW]).astype(jnp.bfloat16)
                o_half[head, HIGH, :] = merge(
                    mixed[HIGH], top[HIGH], total[HIGH],
                    cross_in[2, step, part, :].astype(jnp.float32), logs[part],
                ).astype(jnp.bfloat16)
            for head in heads:
                result_copy(head, LOW, outer).start()
                result_local(head, HIGH).start()

        def second_and_third(turn):
            second_part(turn)
            third_part(turn)

        repeat(steps // 2, second_and_third)
        repeat(steps // 2, lambda turn: third_part(steps // 2 + turn))

        def finish(step):
            for slot in range(3):
                cross_copy(slot, step, peer).wait_send()
            for side in range(2):
                stat_copy(2 * step + side, peer).wait_send()
                result_copy(2 * step + side, LOW, outer).wait_send()
                result_local(2 * step + side, HIGH).wait()

        repeat(steps, finish)

    @pl.when(me == 2)
    def _():
        peer, outer = me - 1, me + 1
        own_start(LOW)
        bias_own[...] = hidden(pair, pair, pair, pair, True)
        bias_high[...] = hidden(rows, rows, pair, pair, False)
        own_wait(LOW)

        def arrived(which, head):
            half_copy(which, head, HIGH, outer).wait_recv()

        def send_query(step):
            arrived(0, step)
            query_copy(step, peer).start()

        repeat(steps, send_query)

        def send_either(step):
            arrived(0, steps + step)
            for side, part in enumerate((LOW, HIGH)):
                cross_out[1, step, part, :] = jnp.where(
                    by_query, q_half[steps + step, part, :], k_half[2 * step + side, LOW, :]
                )
            cross_copy(1, step, peer).start()


        def give(heads):
            for head in heads:
                result_copy(head, HIGH, outer).start()
                result_local(head, LOW).start()

        def span_part(step):
            heads = (2 * step, 2 * step + 1)
            parts = (LOW, HIGH)
            cross_copy(1, step, peer).wait_recv()
            for head in heads:
                arrived(1, head)
                arrived(2, head)
            done = attend([
                (cross_in[1, step, part, :], k_half[head], v_half[head], bias_high[...])
                for head, part in zip(heads, parts)
            ])
            for head, part, (mixed, top, total) in zip(heads, parts, done):
                cross_out[2, step, part, :] = jnp.where(
                    by_query, (mixed / total).astype(jnp.bfloat16), v_half[head, LOW, :]
                )
            stat_out[step] = as_row(
                jnp.concatenate([top + jnp.log2(total) for mixed, top, total in done], axis=0)
            )
            cross_copy(2, step, peer).start()
            stat_copy(step, peer).start()

        def low_pair(turn):
            both = (2 * turn, 2 * turn + 1)
            near = attend([
                (q_half[step], k_half[step], v_half[step], bias_own[...]) for step in both
            ])
            for step in both:
                cross_copy(0, step, peer).wait_recv()
                stat_copy(step, peer).wait_recv()
            for step, own in zip(both, near):
                o_half[step] = merge(
                    *own, cross_in[0, step].astype(jnp.float32), as_columns(stat_in[step])
                ).astype(jnp.bfloat16)
            give(both)

        def high_near(turn):
            both = (2 * turn, 2 * turn + 1)
            near = attend([
                (q_half[steps + step], k_half[steps + step], v_half[steps + step], bias_own[...])
                for step in both
            ])
            for step, own in zip(both, near):
                for kind in range(3):
                    kept[kind, step] = jnp.broadcast_to(own[kind], (pair, HD))

        def high_pair(turn):
            both = (2 * turn, 2 * turn + 1)
            low = [scores_of(q_half[steps + step], cross_in[1, step]) for step in both]
            tops = [jnp.max(scores, axis=1, keepdims=True) for scores in low]
            low = [weigh(scores, top) for scores, top in zip(low, tops)]
            totals = [jnp.sum(weights, axis=1, keepdims=True) for weights in low]
            for step in both:
                cross_copy(2, step, peer).wait_recv()
                stat_copy(steps + step, peer).wait_recv()
            for step, weights, top, total in zip(both, low, tops, totals):
                other = jnp.where(
                    by_query, cross_in[2, step].astype(jnp.float32),
                    mix(weights, cross_in[2, step]) / total,
                )
                logs = jnp.where(
                    by_query, as_columns(stat_in[steps + step]),
                    jnp.broadcast_to(top + jnp.log2(total), (pair, HD)),
                )
                o_half[steps + step] = merge(
                    kept[0, step], kept[1, step], kept[2, step], other, logs
                ).astype(jnp.bfloat16)
            give([steps + step for step in both])

        def send_and_span(step):
            send_either(2 * step)
            send_either(2 * step + 1)
            span_part(step)

        quarter = steps // 2
        send_and_span(0)

        def early(turn):
            send_and_span(1 + turn)
            low_pair(turn)

        repeat(quarter - 1, early)
        span_part(quarter)
        low_pair(quarter - 1)
        high_near(0)

        def late(turn):
            span_part(quarter + 1 + turn)
            high_near(1 + turn)
            high_pair(turn)

        repeat(quarter - 2, late)
        high_pair(quarter - 2)
        span_part(steps - 1)
        high_near(quarter - 1)
        high_pair(quarter - 1)

        def finish(step):
            query_copy(step, peer).wait_send()
            for slot in (1, 2):
                cross_copy(slot, step, peer).wait_send()
            stat_copy(step, peer).wait_send()
            for side in range(2):
                result_copy(2 * step + side, HIGH, outer).wait_send()
                result_local(2 * step + side, LOW).wait()

        repeat(steps, finish)


def cut_body(queries, keys, values, span_starts):
    rows = queries.shape[0]
    pair = 2 * rows
    steps = HEADS // 2
    everything = pl.BlockSpec(memory_space=pltpu.HBM)
    dma = pltpu.SemaphoreType.DMA
    return pl.pallas_call(
        cut_kernel,
        out_shape=pltpu.VMEM(queries.shape, jnp.bfloat16),
        in_specs=[pl.BlockSpec(memory_space=pltpu.SMEM), everything, everything, everything],
        out_specs=pl.BlockSpec(memory_space=pl.ANY),
        scratch_shapes=[pltpu.VMEM((HEADS, pair, HD), jnp.bfloat16)] * 4
        + [pltpu.VMEM((3, steps, pair, HD), jnp.bfloat16)] * 2
        + [pltpu.VMEM((HEADS, 1, pair), jnp.float32)] * 2
        + [
            pltpu.VMEM((pair, pair), jnp.float32),
            pltpu.VMEM((pair, rows), jnp.float32),
            pltpu.VMEM((rows, pair), jnp.float32),
            pltpu.VMEM((3, steps, pair, HD), jnp.float32),
            dma((3, HEADS)), dma((3, HEADS)), dma((3, HEADS)),
            dma((3, steps)), dma((3, steps)),
            dma((HEADS,)), dma((HEADS,)),
            dma((HEADS,)), dma((HEADS,)), dma((HEADS,)),
        ],
        compiler_params=pltpu.CompilerParams(
            collective_id=0, has_side_effects=True, vmem_limit_bytes=56 * 1024 * 1024
        ),
    )(span_starts, queries, keys, values)


def chosen_body(count, queries, keys, values, span_starts):
    rows, images = queries.shape[0], span_starts.shape[0]
    if count == 4 and images == 1 and SPAN <= 2 * rows and rows % 16 == 0:
        return cut_body(queries, keys, values, span_starts)
    if count % 2 == 0 and HEADS % count == 0:
        return exchange_body(count, queries, keys, values, span_starts)
    return ring_body(queries, keys, values, span_starts)


def solution(mesh):
    body = functools.partial(chosen_body, mesh.shape["ctx"])
    placed = (P(("dp", "ctx"), None), P(("dp", "ctx"), None), P(("dp", "ctx"), None), P("dp"))
    return jax.shard_map(
        body, mesh=mesh, in_specs=placed, out_specs=P(("dp", "ctx"), None), check_vma=False
    )
```

```python
import functools
import math

import jax
import jax.numpy as jnp
from jax import lax
from jax.experimental import pallas as pl
from jax.experimental.pallas import tpu as pltpu
from jax.sharding import PartitionSpec as P

HEADS = 16
HD = 128
SPAN = 288


def shifted(value, axis, steps):
    count = lax.axis_size(axis)
    pairs = [(source, (source + steps) % count) for source in range(count)]
    return lax.ppermute(value, axis, pairs)


def span_number(positions, span_starts):
    span_count = span_starts.shape[0]
    inside = (positions[:, None] >= span_starts[None, :]) & (
        positions[:, None] < span_starts[None, :] + SPAN
    )
    labels = jnp.arange(span_count, dtype=jnp.int32) + 1
    return jnp.sum(jnp.where(inside, labels[None, :], 0), axis=1)


def fold_block(operands):
    state_now, visible, group_query, key_heads, value_heads = operands
    row_max, row_sum, weighted = state_now
    scores = jnp.einsum(
        "qhd,khd->hqk", group_query, key_heads, preferred_element_type=jnp.float32
    ) * HD ** (-0.5)
    scores = jnp.where(visible[None], scores, -1e30)
    new_max = jnp.maximum(row_max, jnp.max(scores, axis=2))
    rescale = jnp.exp(row_max - new_max)
    weights = jnp.where(visible[None], jnp.exp(scores - new_max[:, :, None]), 0.0)
    new_sum = row_sum * rescale + jnp.sum(weights, axis=2)
    products = jnp.einsum(
        "hqk,khd->qhd",
        weights.astype(jnp.bfloat16),
        value_heads,
        preferred_element_type=jnp.float32,
    )
    new_weighted = weighted * rescale.T[:, :, None] + products
    return (new_max, new_sum, new_weighted)


def keep_block(operands):
    return operands[0]


def ring_body(queries, keys, values, span_starts):
    tok_rows = queries.shape[0]
    row_width = queries.shape[1]
    loop_size = lax.axis_size("ctx")
    loop_index = lax.axis_index("ctx")
    local_rows = jnp.arange(tok_rows, dtype=jnp.int32)
    query_pos = loop_index * tok_rows + local_rows
    query_span = span_number(query_pos, span_starts)
    query_heads = queries.reshape(tok_rows, HEADS, HD)
    group_count = 2
    group_rows = tok_rows // group_count
    empty_state = tuple(
        (
            (
                jnp.full((HEADS, group_rows), -1e30, jnp.float32),
                jnp.zeros((HEADS, group_rows), jnp.float32),
                jnp.zeros((group_rows, HEADS, HD), jnp.float32),
            )
            for number in range(group_count)
        )
    )

    def absorb(running, block_pair, key_start):
        key_block, value_block = block_pair
        block_rows = key_block.shape[0]
        key_pos = key_start + jnp.arange(block_rows, dtype=jnp.int32)
        key_span = span_number(key_pos, span_starts)
        key_heads = key_block.reshape(block_rows, HEADS, HD)
        value_heads = value_block.reshape(block_rows, HEADS, HD)
        updated = []
        for group_index in range(group_count):
            row_start = group_index * group_rows
            group_pos = query_pos[row_start : row_start + group_rows]
            group_span = query_span[row_start : row_start + group_rows]
            group_query = query_heads[row_start : row_start + group_rows]
            visible = (key_pos[None, :] <= group_pos[:, None]) | (
                group_span[:, None] == key_span[None, :]
            ) & (group_span[:, None] > 0)
            operands = (running[group_index], visible, group_query, key_heads, value_heads)
            updated.append(lax.cond(jnp.any(visible), fold_block, keep_block, operands))
        return tuple(updated)

    stacked = jnp.stack([keys, values])
    own_state = absorb(empty_state, (keys, values), loop_index * tok_rows)

    def advance(step_index, loop_state):
        running, upward, downward = loop_state
        upward = shifted(upward, "ctx", 1)
        downward = shifted(downward, "ctx", -1)
        source_up = (loop_index - 1 - step_index) % loop_size
        source_down = (loop_index + 1 + step_index) % loop_size
        running = absorb(running, (upward[0], upward[1]), source_up * tok_rows)
        running = absorb(running, (downward[0], downward[1]), source_down * tok_rows)
        return (running, upward, downward)

    final_state, upward, downward = lax.fori_loop(
        0, (loop_size - 1) // 2, advance, (own_state, stacked, stacked)
    )
    upward = shifted(upward, "ctx", 1)
    source_last = (loop_index - loop_size // 2) % loop_size
    final_state = absorb(final_state, (upward[0], upward[1]), source_last * tok_rows)
    pieces = [weighted / row_sum.T[:, :, None] for row_max, row_sum, weighted in final_state]
    attended = jnp.concatenate(pieces, axis=0).reshape(tok_rows, row_width).astype(jnp.bfloat16)
    return attended


def exchange_kernel(
    count, images, starts_ref, q_ref, k_ref, v_ref, out_ref,
    q_all, k_all, v_all, o_all, bias,
    in_send, in_recv, in_local, out_send, out_recv, out_local,
):
    me = lax.axis_index("ctx")
    rows = q_ref.shape[0]
    length = rows * count
    own_heads = HEADS // count
    half = count // 2
    side = me // half
    far = [(1 - side) * half + (me + i) % half for i in range(half)]
    near = [side * half + (me + i) % half for i in range(1, half)]
    peers = far + near
    my_rows = pl.ds(pl.multiple_of(me * rows, rows), rows)
    sources = (q_ref, k_ref, v_ref)
    landing = (q_all, k_all, v_all)

    def columns(owner, head):
        return pl.ds(pl.multiple_of((owner * own_heads + head) * HD, HD), HD)

    def rows_of(device):
        return pl.ds(pl.multiple_of(device * rows, rows), rows)

    def operand_copy(which, head, peer):
        return pltpu.make_async_remote_copy(
            src_ref=sources[which].at[:, columns(peer, head)],
            dst_ref=landing[which].at[head, my_rows, :],
            send_sem=in_send.at[which, head, peer],
            recv_sem=in_recv.at[which, head, me],
            device_id={"ctx": peer},
            device_id_type=pl.DeviceIdType.MESH,
        )

    def operand_arrival(which, head, peer):
        return pltpu.make_async_remote_copy(
            src_ref=sources[which].at[:, columns(peer, head)],
            dst_ref=landing[which].at[head, rows_of(peer), :],
            send_sem=in_send.at[which, head, peer],
            recv_sem=in_recv.at[which, head, peer],
            device_id={"ctx": peer},
            device_id_type=pl.DeviceIdType.MESH,
        )

    def operand_local(which, head):
        return pltpu.make_async_copy(
            sources[which].at[:, columns(me, head)],
            landing[which].at[head, my_rows, :],
            in_local.at[which, head],
        )

    def result_copy(head, peer):
        return pltpu.make_async_remote_copy(
            src_ref=o_all.at[head, rows_of(peer), :],
            dst_ref=out_ref.at[:, columns(me, head)],
            send_sem=out_send.at[head, peer],
            recv_sem=out_recv.at[head, me],
            device_id={"ctx": peer},
            device_id_type=pl.DeviceIdType.MESH,
        )

    def result_arrival(head, peer):
        return pltpu.make_async_remote_copy(
            src_ref=o_all.at[head, rows_of(peer), :],
            dst_ref=out_ref.at[:, columns(peer, head)],
            send_sem=out_send.at[head, peer],
            recv_sem=out_recv.at[head, peer],
            device_id={"ctx": peer},
            device_id_type=pl.DeviceIdType.MESH,
        )

    def result_local(head):
        return pltpu.make_async_copy(
            o_all.at[head, my_rows, :], out_ref.at[:, columns(me, head)], out_local.at[head]
        )

    barrier = pltpu.get_barrier_semaphore()
    for peer in peers:
        pl.semaphore_signal(
            barrier, inc=1, device_id={"ctx": peer}, device_id_type=pl.DeviceIdType.MESH
        )
    pl.semaphore_wait(barrier, count - 1)

    def send_head(head, carry):
        for peer in peers:
            for which in range(3):
                operand_copy(which, head, peer).start()
        for which in range(3):
            operand_local(which, head).start()
        return carry

    lax.fori_loop(0, own_heads, send_head, 0)

    query_pos = lax.broadcasted_iota(jnp.int32, (length, length), 0)
    key_pos = lax.broadcasted_iota(jnp.int32, (length, length), 1)
    visible = key_pos <= query_pos
    for image in range(images):
        first = starts_ref[image]
        inside = (
            (query_pos >= first) & (query_pos < first + SPAN)
            & (key_pos >= first) & (key_pos < first + SPAN)
        )
        visible = visible | inside
    bias[...] = jnp.where(visible, 0.0, -1e30)

    def attend_head(head, carry):
        for which in range(3):
            operand_local(which, head).wait()
            for peer in peers:
                operand_arrival(which, head, peer).wait_recv()
        scores = lax.dot_general(
            q_all[head], k_all[head], (((1,), (1,)), ((), ())),
            preferred_element_type=jnp.float32,
        ) * (HD ** (-0.5) * math.log2(math.e))
        scores = scores + bias[...]
        weights = jnp.exp2(scores - jnp.max(scores, axis=1, keepdims=True))
        total = jnp.sum(weights, axis=1, keepdims=True)
        mixed = jnp.dot(
            weights.astype(jnp.bfloat16), v_all[head], preferred_element_type=jnp.float32
        )
        o_all[head] = (mixed / total).astype(jnp.bfloat16)
        for peer in peers:
            result_copy(head, peer).start()
        result_local(head).start()
        return carry

    lax.fori_loop(0, own_heads, attend_head, 0)

    def finish_head(head, carry):
        result_local(head).wait()
        for peer in peers:
            for which in range(3):
                operand_copy(which, head, peer).wait_send()
            result_copy(head, peer).wait_send()
            result_arrival(head, peer).wait_recv()
        return carry

    lax.fori_loop(0, own_heads, finish_head, 0)


def exchange_body(count, queries, keys, values, span_starts):
    rows = queries.shape[0]
    length = rows * count
    own_heads = HEADS // count
    images = span_starts.shape[0]
    everything = pl.BlockSpec(memory_space=pltpu.HBM)
    return pl.pallas_call(
        functools.partial(exchange_kernel, count, images),
        out_shape=jax.ShapeDtypeStruct(queries.shape, jnp.bfloat16),
        in_specs=[pl.BlockSpec(memory_space=pltpu.SMEM), everything, everything, everything],
        out_specs=everything,
        scratch_shapes=[pltpu.VMEM((own_heads, length, HD), jnp.bfloat16)] * 4
        + [
            pltpu.VMEM((length, length), jnp.float32),
            pltpu.SemaphoreType.DMA((3, own_heads, count)),
            pltpu.SemaphoreType.DMA((3, own_heads, count)),
            pltpu.SemaphoreType.DMA((3, own_heads)),
            pltpu.SemaphoreType.DMA((own_heads, count)),
            pltpu.SemaphoreType.DMA((own_heads, count)),
            pltpu.SemaphoreType.DMA((own_heads,)),
        ],
        compiler_params=pltpu.CompilerParams(
            collective_id=0, has_side_effects=True, vmem_limit_bytes=56 * 1024 * 1024
        ),
    )(span_starts, queries, keys, values)


def cut_kernel(
    starts_ref, q_ref, k_ref, v_ref, out_ref,
    q_half, k_half, v_half, o_half, cross_in, cross_out, stat_in, stat_out,
    bias_own, bias_low, bias_high, kept,
    half_send, half_recv, half_local, cross_send, cross_recv,
    stat_send, stat_recv, out_send, out_recv, out_local,
):
    me = lax.axis_index("ctx")
    rows = q_ref.shape[0]
    pair = 2 * rows
    steps = HEADS // 2
    scale = HD ** (-0.5) * math.log2(math.e)
    sources = (q_ref, k_ref, v_ref)
    halves = (q_half, k_half, v_half)
    first = starts_ref[0]
    by_query = first >= rows
    LOW, HIGH = slice(0, rows), slice(rows, pair)

    def columns(head):
        return pl.ds(pl.multiple_of(head * HD, HD), HD)

    def remote(src, dst, send, recv, peer):
        return pltpu.make_async_remote_copy(
            src_ref=src, dst_ref=dst, send_sem=send, recv_sem=recv,
            device_id={"ctx": peer}, device_id_type=pl.DeviceIdType.MESH,
        )

    def half_copy(which, head, part, peer):
        return remote(
            sources[which].at[:, columns(head)], halves[which].at[head, part, :],
            half_send.at[which, head], half_recv.at[which, head], peer,
        )

    def own_copy(which, head, part):
        return pltpu.make_async_copy(
            sources[which].at[:, columns(head)], halves[which].at[head, part, :],
            half_local.at[which, head],
        )

    def cross_copy(slot, step, peer):
        return remote(
            cross_out.at[slot, step], cross_in.at[slot, step],
            cross_send.at[slot, step], cross_recv.at[slot, step], peer,
        )

    def query_copy(step, peer):
        return remote(
            q_half.at[step], cross_in.at[0, step],
            cross_send.at[0, step], cross_recv.at[0, step], peer,
        )

    def stat_copy(step, peer):
        return remote(
            stat_out.at[step], stat_in.at[step], stat_send.at[step], stat_recv.at[step], peer
        )

    def result_copy(head, part, peer):
        return remote(
            o_half.at[head, part, :], out_ref.at[:, columns(head)],
            out_send.at[head], out_recv.at[head], peer,
        )

    def result_local(head, part):
        return pltpu.make_async_copy(
            o_half.at[head, part, :], out_ref.at[:, columns(head)], out_local.at[head]
        )

    def scores_of(query, key):
        return lax.dot_general(
            query, key, (((1,), (1,)), ((), ())), preferred_element_type=jnp.float32
        ) * scale

    def weigh(scores, top):
        return jnp.exp2(scores - top)

    def mix(weights, value):
        return jnp.dot(weights.astype(jnp.bfloat16), value, preferred_element_type=jnp.float32)

    def attend(items):
        scores = [
            scores_of(query, key) if bias is None else scores_of(query, key) + bias
            for query, key, value, bias in items
        ]
        tops = [jnp.max(score, axis=1, keepdims=True) for score in scores]
        weights = [weigh(score, top) for score, top in zip(scores, tops)]
        totals = [jnp.sum(weight, axis=1, keepdims=True) for weight in weights]
        mixed = [mix(weight, item[2]) for weight, item in zip(weights, items)]
        return list(zip(mixed, tops, totals))

    def as_row(column):
        return jnp.transpose(jnp.broadcast_to(column, (pair, HD)))[0:1, :]

    def as_columns(row):
        return jnp.transpose(jnp.broadcast_to(row, (HD, pair)))

    def merge(mixed, top, total, other, other_log):
        peak = jnp.maximum(top, other_log)
        mine, theirs = jnp.exp2(top - peak), jnp.exp2(other_log - peak)
        return (mixed * mine + other * theirs) / (total * mine + theirs)

    def hidden(query_start, query_rows, key_start, key_rows, causal):
        query_pos = query_start + lax.broadcasted_iota(jnp.int32, (query_rows, key_rows), 0)
        key_pos = key_start + lax.broadcasted_iota(jnp.int32, (query_rows, key_rows), 1)
        visible = (
            (query_pos >= first) & (query_pos < first + SPAN)
            & (key_pos >= first) & (key_pos < first + SPAN)
        )
        if causal:
            visible = visible | (key_pos <= query_pos)
        return jnp.where(visible, 0.0, -1e30)

    barrier = pltpu.get_barrier_semaphore()

    @pl.when(me > 0)
    def _():
        pl.semaphore_signal(
            barrier, inc=1, device_id={"ctx": me - 1}, device_id_type=pl.DeviceIdType.MESH
        )

    @pl.when(me < 3)
    def _():
        pl.semaphore_signal(
            barrier, inc=1, device_id={"ctx": me + 1}, device_id_type=pl.DeviceIdType.MESH
        )

    @pl.when((me == 0) | (me == 3))
    def _():
        pl.semaphore_wait(barrier, 1)

    @pl.when((me == 1) | (me == 2))
    def _():
        pl.semaphore_wait(barrier, 2)

    def repeat(count, one):
        lax.fori_loop(0, count, lambda step, carry: (one(step), carry)[1], 0)

    def outer_end(part, peer):
        def one(head):
            for which in range(3):
                half_copy(which, head, part, peer).wait_send()
            result_copy(head, part, peer).wait_recv()

        repeat(HEADS, one)

    @pl.when(me == 0)
    def _():
        def first_part(step):
            half_copy(1, step, LOW, me + 1).start()
            half_copy(2, step, LOW, me + 1).start()

        repeat(steps, lambda step: half_copy(1, steps + step, LOW, me + 1).start())
        repeat(steps, first_part)

        def second_part(step):
            half_copy(2, steps + step, LOW, me + 1).start()
            half_copy(0, step, LOW, me + 1).start()

        repeat(steps, second_part)
        repeat(steps, lambda step: half_copy(0, steps + step, LOW, me + 1).start())
        outer_end(LOW, me + 1)

    @pl.when(me == 3)
    def _():
        repeat(steps, lambda head: half_copy(0, head, HIGH, me - 1).start())

        def pair_part(head):
            half_copy(1, head, HIGH, me - 1).start()
            half_copy(2, head, HIGH, me - 1).start()

        def mixed_part(head):
            half_copy(0, steps + head, HIGH, me - 1).start()
            pair_part(head)

        repeat(steps, mixed_part)
        repeat(steps, lambda head: pair_part(steps + head))
        outer_end(HIGH, me - 1)

    def own_start(part):
        def one(head):
            for which in range(3):
                own_copy(which, head, part).start()

        repeat(HEADS, one)

    def own_wait(part):
        def one(head):
            for which in range(3):
                own_copy(which, head, part).wait()

        repeat(HEADS, one)

    @pl.when(me == 1)
    def _():
        peer, outer = me + 1, me - 1
        own_start(HIGH)
        bias_own[...] = hidden(0, pair, 0, pair, True)
        bias_low[...] = jnp.where(by_query, -1e30, hidden(0, pair, pair, rows, False))
        own_wait(HIGH)

        def arrived(which, head):
            half_copy(which, head, LOW, outer).wait_recv()

        def send_either(step):
            arrived(1, steps + step)
            for side, part in enumerate((LOW, HIGH)):
                cross_out[1, step, part, :] = jnp.where(
                    by_query, q_half[2 * step + side, HIGH, :], k_half[steps + step, part, :]
                )
            cross_copy(1, step, peer).start()

        repeat(steps, send_either)

        def first_part(turn):
            both = (2 * turn, 2 * turn + 1)
            for step in both:
                arrived(1, step)
                arrived(2, step)
                query_copy(step, peer).wait_recv()
            done = attend([(cross_in[0, step], k_half[step], v_half[step], None) for step in both])
            for step, (mixed, top, total) in zip(both, done):
                cross_out[0, step] = (mixed / total).astype(jnp.bfloat16)
                stat_out[step] = as_row(top + jnp.log2(total))
            for step in both:
                cross_copy(0, step, peer).start()
                stat_copy(step, peer).start()

        repeat(steps // 2, first_part)

        def near_items(step):
            return [
                (q_half[head], k_half[head], v_half[head], bias_own[...])
                for head in (2 * step, 2 * step + 1)
            ]

        def far_items(step):
            return [
                (q_half[2 * step + side], cross_in[1, step, part, :],
                 cross_in[2, step, part, :], bias_low[...])
                for side, part in enumerate((LOW, HIGH))
            ]

        def near_arrived(step):
            for head in (2 * step, 2 * step + 1):
                arrived(0, head)

        def far_arrived(step):
            cross_copy(2, step, peer).wait_recv()
            stat_copy(step, peer).wait_recv()

        def settle(step, near, far):
            logs = as_columns(jnp.where(by_query, stat_in[step], -1e30))
            heads = (2 * step, 2 * step + 1)
            for head, part, own, span in zip(heads, (LOW, HIGH), near, far):
                top = jnp.maximum(own[1], span[1])
                mine, theirs = jnp.exp2(own[1] - top), jnp.exp2(span[1] - top)
                mixed = own[0] * mine + span[0] * theirs
                total = own[2] * mine + span[2] * theirs
                o_half[head, LOW, :] = (mixed[LOW] / total[LOW]).astype(jnp.bfloat16)
                o_half[head, HIGH, :] = merge(
                    mixed[HIGH], top[HIGH], total[HIGH],
                    cross_in[2, step, part, :].astype(jnp.float32), logs[part],
                ).astype(jnp.bfloat16)
            for head in heads:
                result_copy(head, LOW, outer).start()
                result_local(head, HIGH).start()

        def second_part(turn):
            both = (2 * turn, 2 * turn + 1)
            for step in both:
                arrived(2, steps + step)
                cross_copy(1, step, peer).wait_recv()
            near_arrived(turn)
            done = attend([
                (cross_in[1, step], k_half[steps + step], v_half[steps + step], None)
                for step in both
            ] + near_items(turn))
            for step, (mixed, top, total) in zip(both, done):
                cross_out[2, step] = jnp.where(
                    by_query, (mixed / total).astype(jnp.bfloat16), v_half[steps + step]
                )
                stat_out[steps + step] = as_row(top + jnp.log2(total))
            for step in both:
                cross_copy(2, step, peer).start()
                stat_copy(steps + step, peer).start()
            far_arrived(turn)
            settle(turn, done[2:], attend(far_items(turn)))

        repeat(steps // 2, second_part)
        near_arrived(steps // 2)
        near = attend(near_items(steps // 2))
        for step in range(steps // 2, steps):
            if step + 1 < steps:
                near_arrived(step + 1)
            far_arrived(step)
            done = attend(far_items(step) + (near_items(step + 1) if step + 1 < steps else []))
            settle(step, near, done[:2])
            near = done[2:]

        def finish(step):
            for slot in range(3):
                cross_copy(slot, step, peer).wait_send()
            for side in range(2):
                stat_copy(2 * step + side, peer).wait_send()
                result_copy(2 * step + side, LOW, outer).wait_send()
                result_local(2 * step + side, HIGH).wait()

        repeat(steps, finish)

    @pl.when(me == 2)
    def _():
        peer, outer = me - 1, me + 1
        own_start(LOW)
        bias_own[...] = hidden(pair, pair, pair, pair, True)
        bias_high[...] = hidden(rows, rows, pair, pair, False)
        own_wait(LOW)

        def arrived(which, head):
            half_copy(which, head, HIGH, outer).wait_recv()

        def send_query(step):
            arrived(0, step)
            query_copy(step, peer).start()

        repeat(steps, send_query)

        def send_either(step):
            arrived(0, steps + step)
            for side, part in enumerate((LOW, HIGH)):
                cross_out[1, step, part, :] = jnp.where(
                    by_query, q_half[steps + step, part, :], k_half[2 * step + side, LOW, :]
                )
            cross_copy(1, step, peer).start()


        def give(heads):
            for head in heads:
                result_copy(head, HIGH, outer).start()
                result_local(head, LOW).start()

        def span_part(step):
            heads = (2 * step, 2 * step + 1)
            parts = (LOW, HIGH)
            cross_copy(1, step, peer).wait_recv()
            for head in heads:
                arrived(1, head)
                arrived(2, head)
            done = attend([
                (cross_in[1, step, part, :], k_half[head], v_half[head], bias_high[...])
                for head, part in zip(heads, parts)
            ])
            for head, part, (mixed, top, total) in zip(heads, parts, done):
                cross_out[2, step, part, :] = jnp.where(
                    by_query, (mixed / total).astype(jnp.bfloat16), v_half[head, LOW, :]
                )
            stat_out[step] = as_row(
                jnp.concatenate([top + jnp.log2(total) for mixed, top, total in done], axis=0)
            )
            cross_copy(2, step, peer).start()
            stat_copy(step, peer).start()

        def low_pair(turn):
            both = (2 * turn, 2 * turn + 1)
            near = attend([
                (q_half[step], k_half[step], v_half[step], bias_own[...]) for step in both
            ])
            for step in both:
                cross_copy(0, step, peer).wait_recv()
                stat_copy(step, peer).wait_recv()
            for step, own in zip(both, near):
                o_half[step] = merge(
                    *own, cross_in[0, step].astype(jnp.float32), as_columns(stat_in[step])
                ).astype(jnp.bfloat16)
            give(both)

        def high_near(turn):
            both = (2 * turn, 2 * turn + 1)
            near = attend([
                (q_half[steps + step], k_half[steps + step], v_half[steps + step], bias_own[...])
                for step in both
            ])
            for step, own in zip(both, near):
                for kind in range(3):
                    kept[kind, step] = jnp.broadcast_to(own[kind], (pair, HD))

        def high_pair(turn):
            both = (2 * turn, 2 * turn + 1)
            low = [scores_of(q_half[steps + step], cross_in[1, step]) for step in both]
            tops = [jnp.max(scores, axis=1, keepdims=True) for scores in low]
            low = [weigh(scores, top) for scores, top in zip(low, tops)]
            totals = [jnp.sum(weights, axis=1, keepdims=True) for weights in low]
            for step in both:
                cross_copy(2, step, peer).wait_recv()
                stat_copy(steps + step, peer).wait_recv()
            for step, weights, top, total in zip(both, low, tops, totals):
                other = jnp.where(
                    by_query, cross_in[2, step].astype(jnp.float32),
                    mix(weights, cross_in[2, step]) / total,
                )
                logs = jnp.where(
                    by_query, as_columns(stat_in[steps + step]),
                    jnp.broadcast_to(top + jnp.log2(total), (pair, HD)),
                )
                o_half[steps + step] = merge(
                    kept[0, step], kept[1, step], kept[2, step], other, logs
                ).astype(jnp.bfloat16)
            give([steps + step for step in both])

        def send_and_span(step):
            send_either(2 * step)
            send_either(2 * step + 1)
            span_part(step)

        quarter = steps // 2
        send_and_span(0)

        def early(turn):
            send_and_span(1 + turn)
            low_pair(turn)

        repeat(quarter - 1, early)
        span_part(quarter)
        low_pair(quarter - 1)
        high_near(0)

        def late(turn):
            span_part(quarter + 1 + turn)
            high_near(1 + turn)
            high_pair(turn)

        repeat(quarter - 2, late)
        high_pair(quarter - 2)
        span_part(steps - 1)
        high_near(quarter - 1)
        high_pair(quarter - 1)

        def finish(step):
            query_copy(step, peer).wait_send()
            for slot in (1, 2):
                cross_copy(slot, step, peer).wait_send()
            stat_copy(step, peer).wait_send()
            for side in range(2):
                result_copy(2 * step + side, HIGH, outer).wait_send()
                result_local(2 * step + side, LOW).wait()

        repeat(steps, finish)


def cut_body(queries, keys, values, span_starts):
    rows = queries.shape[0]
    pair = 2 * rows
    steps = HEADS // 2
    everything = pl.BlockSpec(memory_space=pltpu.HBM)
    dma = pltpu.SemaphoreType.DMA
    return pl.pallas_call(
        cut_kernel,
        out_shape=pltpu.VMEM(queries.shape, jnp.bfloat16),
        in_specs=[pl.BlockSpec(memory_space=pltpu.SMEM), everything, everything, everything],
        out_specs=pl.BlockSpec(memory_space=pl.ANY),
        scratch_shapes=[pltpu.VMEM((HEADS, pair, HD), jnp.bfloat16)] * 4
        + [pltpu.VMEM((3, steps, pair, HD), jnp.bfloat16)] * 2
        + [pltpu.VMEM((HEADS, 1, pair), jnp.float32)] * 2
        + [
            pltpu.VMEM((pair, pair), jnp.float32),
            pltpu.VMEM((pair, rows), jnp.float32),
            pltpu.VMEM((rows, pair), jnp.float32),
            pltpu.VMEM((3, steps, pair, HD), jnp.float32),
            dma((3, HEADS)), dma((3, HEADS)), dma((3, HEADS)),
            dma((3, steps)), dma((3, steps)),
            dma((HEADS,)), dma((HEADS,)),
            dma((HEADS,)), dma((HEADS,)), dma((HEADS,)),
        ],
        compiler_params=pltpu.CompilerParams(
            collective_id=0, has_side_effects=True, vmem_limit_bytes=56 * 1024 * 1024
        ),
    )(span_starts, queries, keys, values)


def chosen_body(count, queries, keys, values, span_starts):
    rows, images = queries.shape[0], span_starts.shape[0]
    if count == 4 and images == 1 and SPAN <= 2 * rows and rows % 16 == 0:
        return cut_body(queries, keys, values, span_starts)
    if count % 2 == 0 and HEADS % count == 0:
        return exchange_body(count, queries, keys, values, span_starts)
    return ring_body(queries, keys, values, span_starts)


def solution(mesh):
    body = functools.partial(chosen_body, mesh.shape["ctx"])
    placed = (P(("dp", "ctx"), None), P(("dp", "ctx"), None), P(("dp", "ctx"), None), P("dp"))
    return jax.shard_map(
        body, mesh=mesh, in_specs=placed, out_specs=P(("dp", "ctx"), None), check_vma=False
    )
```

```python
import functools
import math

import jax
import jax.numpy as jnp
from jax import lax
from jax.experimental import pallas as pl
from jax.experimental.pallas import tpu as pltpu
from jax.sharding import PartitionSpec as P

HEADS = 16
HD = 128
SPAN = 288


def shifted(value, axis, steps):
    count = lax.axis_size(axis)
    pairs = [(source, (source + steps) % count) for source in range(count)]
    return lax.ppermute(value, axis, pairs)


def span_number(positions, span_starts):
    span_count = span_starts.shape[0]
    inside = (positions[:, None] >= span_starts[None, :]) & (
        positions[:, None] < span_starts[None, :] + SPAN
    )
    labels = jnp.arange(span_count, dtype=jnp.int32) + 1
    return jnp.sum(jnp.where(inside, labels[None, :], 0), axis=1)


def fold_block(operands):
    state_now, visible, group_query, key_heads, value_heads = operands
    row_max, row_sum, weighted = state_now
    scores = jnp.einsum(
        "qhd,khd->hqk", group_query, key_heads, preferred_element_type=jnp.float32
    ) * HD ** (-0.5)
    scores = jnp.where(visible[None], scores, -1e30)
    new_max = jnp.maximum(row_max, jnp.max(scores, axis=2))
    rescale = jnp.exp(row_max - new_max)
    weights = jnp.where(visible[None], jnp.exp(scores - new_max[:, :, None]), 0.0)
    new_sum = row_sum * rescale + jnp.sum(weights, axis=2)
    products = jnp.einsum(
        "hqk,khd->qhd",
        weights.astype(jnp.bfloat16),
        value_heads,
        preferred_element_type=jnp.float32,
    )
    new_weighted = weighted * rescale.T[:, :, None] + products
    return (new_max, new_sum, new_weighted)


def keep_block(operands):
    return operands[0]


def ring_body(queries, keys, values, span_starts):
    tok_rows = queries.shape[0]
    row_width = queries.shape[1]
    loop_size = lax.axis_size("ctx")
    loop_index = lax.axis_index("ctx")
    local_rows = jnp.arange(tok_rows, dtype=jnp.int32)
    query_pos = loop_index * tok_rows + local_rows
    query_span = span_number(query_pos, span_starts)
    query_heads = queries.reshape(tok_rows, HEADS, HD)
    group_count = 2
    group_rows = tok_rows // group_count
    empty_state = tuple(
        (
            (
                jnp.full((HEADS, group_rows), -1e30, jnp.float32),
                jnp.zeros((HEADS, group_rows), jnp.float32),
                jnp.zeros((group_rows, HEADS, HD), jnp.float32),
            )
            for number in range(group_count)
        )
    )

    def absorb(running, block_pair, key_start):
        key_block, value_block = block_pair
        block_rows = key_block.shape[0]
        key_pos = key_start + jnp.arange(block_rows, dtype=jnp.int32)
        key_span = span_number(key_pos, span_starts)
        key_heads = key_block.reshape(block_rows, HEADS, HD)
        value_heads = value_block.reshape(block_rows, HEADS, HD)
        updated = []
        for group_index in range(group_count):
            row_start = group_index * group_rows
            group_pos = query_pos[row_start : row_start + group_rows]
            group_span = query_span[row_start : row_start + group_rows]
            group_query = query_heads[row_start : row_start + group_rows]
            visible = (key_pos[None, :] <= group_pos[:, None]) | (
                group_span[:, None] == key_span[None, :]
            ) & (group_span[:, None] > 0)
            operands = (running[group_index], visible, group_query, key_heads, value_heads)
            updated.append(lax.cond(jnp.any(visible), fold_block, keep_block, operands))
        return tuple(updated)

    stacked = jnp.stack([keys, values])
    own_state = absorb(empty_state, (keys, values), loop_index * tok_rows)

    def advance(step_index, loop_state):
        running, upward, downward = loop_state
        upward = shifted(upward, "ctx", 1)
        downward = shifted(downward, "ctx", -1)
        source_up = (loop_index - 1 - step_index) % loop_size
        source_down = (loop_index + 1 + step_index) % loop_size
        running = absorb(running, (upward[0], upward[1]), source_up * tok_rows)
        running = absorb(running, (downward[0], downward[1]), source_down * tok_rows)
        return (running, upward, downward)

    final_state, upward, downward = lax.fori_loop(
        0, (loop_size - 1) // 2, advance, (own_state, stacked, stacked)
    )
    upward = shifted(upward, "ctx", 1)
    source_last = (loop_index - loop_size // 2) % loop_size
    final_state = absorb(final_state, (upward[0], upward[1]), source_last * tok_rows)
    pieces = [weighted / row_sum.T[:, :, None] for row_max, row_sum, weighted in final_state]
    attended = jnp.concatenate(pieces, axis=0).reshape(tok_rows, row_width).astype(jnp.bfloat16)
    return attended


def exchange_kernel(
    count, images, starts_ref, q_ref, k_ref, v_ref, out_ref,
    q_all, k_all, v_all, o_all, bias,
    in_send, in_recv, in_local, out_send, out_recv, out_local,
):
    me = lax.axis_index("ctx")
    rows = q_ref.shape[0]
    length = rows * count
    own_heads = HEADS // count
    half = count // 2
    side = me // half
    far = [(1 - side) * half + (me + i) % half for i in range(half)]
    near = [side * half + (me + i) % half for i in range(1, half)]
    peers = far + near
    my_rows = pl.ds(pl.multiple_of(me * rows, rows), rows)
    sources = (q_ref, k_ref, v_ref)
    landing = (q_all, k_all, v_all)

    def columns(owner, head):
        return pl.ds(pl.multiple_of((owner * own_heads + head) * HD, HD), HD)

    def rows_of(device):
        return pl.ds(pl.multiple_of(device * rows, rows), rows)

    def operand_copy(which, head, peer):
        return pltpu.make_async_remote_copy(
            src_ref=sources[which].at[:, columns(peer, head)],
            dst_ref=landing[which].at[head, my_rows, :],
            send_sem=in_send.at[which, head, peer],
            recv_sem=in_recv.at[which, head, me],
            device_id={"ctx": peer},
            device_id_type=pl.DeviceIdType.MESH,
        )

    def operand_arrival(which, head, peer):
        return pltpu.make_async_remote_copy(
            src_ref=sources[which].at[:, columns(peer, head)],
            dst_ref=landing[which].at[head, rows_of(peer), :],
            send_sem=in_send.at[which, head, peer],
            recv_sem=in_recv.at[which, head, peer],
            device_id={"ctx": peer},
            device_id_type=pl.DeviceIdType.MESH,
        )

    def operand_local(which, head):
        return pltpu.make_async_copy(
            sources[which].at[:, columns(me, head)],
            landing[which].at[head, my_rows, :],
            in_local.at[which, head],
        )

    def result_copy(head, peer):
        return pltpu.make_async_remote_copy(
            src_ref=o_all.at[head, rows_of(peer), :],
            dst_ref=out_ref.at[:, columns(me, head)],
            send_sem=out_send.at[head, peer],
            recv_sem=out_recv.at[head, me],
            device_id={"ctx": peer},
            device_id_type=pl.DeviceIdType.MESH,
        )

    def result_arrival(head, peer):
        return pltpu.make_async_remote_copy(
            src_ref=o_all.at[head, rows_of(peer), :],
            dst_ref=out_ref.at[:, columns(peer, head)],
            send_sem=out_send.at[head, peer],
            recv_sem=out_recv.at[head, peer],
            device_id={"ctx": peer},
            device_id_type=pl.DeviceIdType.MESH,
        )

    def result_local(head):
        return pltpu.make_async_copy(
            o_all.at[head, my_rows, :], out_ref.at[:, columns(me, head)], out_local.at[head]
        )

    barrier = pltpu.get_barrier_semaphore()
    for peer in peers:
        pl.semaphore_signal(
            barrier, inc=1, device_id={"ctx": peer}, device_id_type=pl.DeviceIdType.MESH
        )
    pl.semaphore_wait(barrier, count - 1)

    def send_head(head, carry):
        for peer in peers:
            for which in range(3):
                operand_copy(which, head, peer).start()
        for which in range(3):
            operand_local(which, head).start()
        return carry

    lax.fori_loop(0, own_heads, send_head, 0)

    query_pos = lax.broadcasted_iota(jnp.int32, (length, length), 0)
    key_pos = lax.broadcasted_iota(jnp.int32, (length, length), 1)
    visible = key_pos <= query_pos
    for image in range(images):
        first = starts_ref[image]
        inside = (
            (query_pos >= first) & (query_pos < first + SPAN)
            & (key_pos >= first) & (key_pos < first + SPAN)
        )
        visible = visible | inside
    bias[...] = jnp.where(visible, 0.0, -1e30)

    def attend_head(head, carry):
        for which in range(3):
            operand_local(which, head).wait()
            for peer in peers:
                operand_arrival(which, head, peer).wait_recv()
        scores = lax.dot_general(
            q_all[head], k_all[head], (((1,), (1,)), ((), ())),
            preferred_element_type=jnp.float32,
        ) * (HD ** (-0.5) * math.log2(math.e))
        scores = scores + bias[...]
        weights = jnp.exp2(scores - jnp.max(scores, axis=1, keepdims=True))
        total = jnp.sum(weights, axis=1, keepdims=True)
        mixed = jnp.dot(
            weights.astype(jnp.bfloat16), v_all[head], preferred_element_type=jnp.float32
        )
        o_all[head] = (mixed / total).astype(jnp.bfloat16)
        for peer in peers:
            result_copy(head, peer).start()
        result_local(head).start()
        return carry

    lax.fori_loop(0, own_heads, attend_head, 0)

    def finish_head(head, carry):
        result_local(head).wait()
        for peer in peers:
            for which in range(3):
                operand_copy(which, head, peer).wait_send()
            result_copy(head, peer).wait_send()
            result_arrival(head, peer).wait_recv()
        return carry

    lax.fori_loop(0, own_heads, finish_head, 0)


def exchange_body(count, queries, keys, values, span_starts):
    rows = queries.shape[0]
    length = rows * count
    own_heads = HEADS // count
    images = span_starts.shape[0]
    everything = pl.BlockSpec(memory_space=pltpu.HBM)
    return pl.pallas_call(
        functools.partial(exchange_kernel, count, images),
        out_shape=jax.ShapeDtypeStruct(queries.shape, jnp.bfloat16),
        in_specs=[pl.BlockSpec(memory_space=pltpu.SMEM), everything, everything, everything],
        out_specs=everything,
        scratch_shapes=[pltpu.VMEM((own_heads, length, HD), jnp.bfloat16)] * 4
        + [
            pltpu.VMEM((length, length), jnp.float32),
            pltpu.SemaphoreType.DMA((3, own_heads, count)),
            pltpu.SemaphoreType.DMA((3, own_heads, count)),
            pltpu.SemaphoreType.DMA((3, own_heads)),
            pltpu.SemaphoreType.DMA((own_heads, count)),
            pltpu.SemaphoreType.DMA((own_heads, count)),
            pltpu.SemaphoreType.DMA((own_heads,)),
        ],
        compiler_params=pltpu.CompilerParams(
            collective_id=0, has_side_effects=True, vmem_limit_bytes=56 * 1024 * 1024
        ),
    )(span_starts, queries, keys, values)


def cut_kernel(
    starts_ref, q_ref, k_ref, v_ref, out_ref,
    q_half, k_half, v_half, o_half, cross_in, cross_out, stat_in, stat_out,
    bias_own, bias_low, bias_high, kept,
    half_send, half_recv, half_local, cross_send, cross_recv,
    stat_send, stat_recv, out_send, out_recv, out_local,
):
    me = lax.axis_index("ctx")
    rows = q_ref.shape[0]
    pair = 2 * rows
    steps = HEADS // 2
    scale = HD ** (-0.5) * math.log2(math.e)
    sources = (q_ref, k_ref, v_ref)
    halves = (q_half, k_half, v_half)
    first = starts_ref[0]
    by_query = first >= rows
    LOW, HIGH = slice(0, rows), slice(rows, pair)

    def columns(head):
        return pl.ds(pl.multiple_of(head * HD, HD), HD)

    def remote(src, dst, send, recv, peer):
        return pltpu.make_async_remote_copy(
            src_ref=src, dst_ref=dst, send_sem=send, recv_sem=recv,
            device_id={"ctx": peer}, device_id_type=pl.DeviceIdType.MESH,
        )

    def half_copy(which, head, part, peer):
        return remote(
            sources[which].at[:, columns(head)], halves[which].at[head, part, :],
            half_send.at[which, head], half_recv.at[which, head], peer,
        )

    def own_copy(which, head, part):
        return pltpu.make_async_copy(
            sources[which].at[:, columns(head)], halves[which].at[head, part, :],
            half_local.at[which, head],
        )

    def cross_copy(slot, step, peer):
        return remote(
            cross_out.at[slot, step], cross_in.at[slot, step],
            cross_send.at[slot, step], cross_recv.at[slot, step], peer,
        )

    def query_copy(step, peer):
        return remote(
            q_half.at[step], cross_in.at[0, step],
            cross_send.at[0, step], cross_recv.at[0, step], peer,
        )

    def stat_copy(step, peer):
        return remote(
            stat_out.at[step], stat_in.at[step], stat_send.at[step], stat_recv.at[step], peer
        )

    def result_copy(head, part, peer):
        return remote(
            o_half.at[head, part, :], out_ref.at[:, columns(head)],
            out_send.at[head], out_recv.at[head], peer,
        )

    def result_local(head, part):
        return pltpu.make_async_copy(
            o_half.at[head, part, :], out_ref.at[:, columns(head)], out_local.at[head]
        )

    def scores_of(query, key):
        return lax.dot_general(
            query, key, (((1,), (1,)), ((), ())), preferred_element_type=jnp.float32
        ) * scale

    def weigh(scores, top):
        return jnp.exp2(scores - top)

    def mix(weights, value):
        return jnp.dot(weights.astype(jnp.bfloat16), value, preferred_element_type=jnp.float32)

    def attend(items):
        scores = [
            scores_of(query, key) if bias is None else scores_of(query, key) + bias
            for query, key, value, bias in items
        ]
        tops = [jnp.max(score, axis=1, keepdims=True) for score in scores]
        weights = [weigh(score, top) for score, top in zip(scores, tops)]
        totals = [jnp.sum(weight, axis=1, keepdims=True) for weight in weights]
        mixed = [mix(weight, item[2]) for weight, item in zip(weights, items)]
        return list(zip(mixed, tops, totals))

    def as_row(column):
        return jnp.transpose(jnp.broadcast_to(column, (pair, HD)))[0:1, :]

    def as_columns(row):
        return jnp.transpose(jnp.broadcast_to(row, (HD, pair)))

    def merge(mixed, top, total, other, other_log):
        peak = jnp.maximum(top, other_log)
        mine, theirs = jnp.exp2(top - peak), jnp.exp2(other_log - peak)
        return (mixed * mine + other * theirs) / (total * mine + theirs)

    def hidden(query_start, query_rows, key_start, key_rows, causal):
        query_pos = query_start + lax.broadcasted_iota(jnp.int32, (query_rows, key_rows), 0)
        key_pos = key_start + lax.broadcasted_iota(jnp.int32, (query_rows, key_rows), 1)
        visible = (
            (query_pos >= first) & (query_pos < first + SPAN)
            & (key_pos >= first) & (key_pos < first + SPAN)
        )
        if causal:
            visible = visible | (key_pos <= query_pos)
        return jnp.where(visible, 0.0, -1e30)

    barrier = pltpu.get_barrier_semaphore()

    @pl.when(me > 0)
    def _():
        pl.semaphore_signal(
            barrier, inc=1, device_id={"ctx": me - 1}, device_id_type=pl.DeviceIdType.MESH
        )

    @pl.when(me < 3)
    def _():
        pl.semaphore_signal(
            barrier, inc=1, device_id={"ctx": me + 1}, device_id_type=pl.DeviceIdType.MESH
        )

    @pl.when((me == 0) | (me == 3))
    def _():
        pl.semaphore_wait(barrier, 1)

    @pl.when((me == 1) | (me == 2))
    def _():
        pl.semaphore_wait(barrier, 2)

    def repeat(count, one):
        lax.fori_loop(0, count, lambda step, carry: (one(step), carry)[1], 0)

    def outer_end(part, peer):
        def one(head):
            for which in range(3):
                half_copy(which, head, part, peer).wait_send()
            result_copy(head, part, peer).wait_recv()

        repeat(HEADS, one)

    @pl.when(me == 0)
    def _():
        def first_part(step):
            half_copy(1, step, LOW, me + 1).start()
            half_copy(2, step, LOW, me + 1).start()

        repeat(steps, lambda step: half_copy(1, steps + step, LOW, me + 1).start())
        repeat(steps, first_part)

        def second_part(step):
            half_copy(2, steps + step, LOW, me + 1).start()
            half_copy(0, step, LOW, me + 1).start()

        repeat(steps, second_part)
        repeat(steps, lambda step: half_copy(0, steps + step, LOW, me + 1).start())
        outer_end(LOW, me + 1)

    @pl.when(me == 3)
    def _():
        repeat(steps, lambda head: half_copy(0, head, HIGH, me - 1).start())

        def pair_part(head):
            half_copy(1, head, HIGH, me - 1).start()
            half_copy(2, head, HIGH, me - 1).start()

        def mixed_part(head):
            half_copy(0, steps + head, HIGH, me - 1).start()
            pair_part(head)

        repeat(steps, mixed_part)
        repeat(steps, lambda head: pair_part(steps + head))
        outer_end(HIGH, me - 1)

    def own_start(part):
        def one(head):
            for which in range(3):
                own_copy(which, head, part).start()

        repeat(HEADS, one)

    def own_wait(part):
        def one(head):
            for which in range(3):
                own_copy(which, head, part).wait()

        repeat(HEADS, one)

    @pl.when(me == 1)
    def _():
        peer, outer = me + 1, me - 1
        own_start(HIGH)
        bias_own[...] = hidden(0, pair, 0, pair, True)
        bias_low[...] = jnp.where(by_query, -1e30, hidden(0, pair, pair, rows, False))
        own_wait(HIGH)

        def arrived(which, head):
            half_copy(which, head, LOW, outer).wait_recv()

        def send_either(step):
            arrived(1, steps + step)
            for side, part in enumerate((LOW, HIGH)):
                cross_out[1, step, part, :] = jnp.where(
                    by_query, q_half[2 * step + side, HIGH, :], k_half[steps + step, part, :]
                )
            cross_copy(1, step, peer).start()

        repeat(steps, send_either)

        def first_part(turn):
            both = (2 * turn, 2 * turn + 1)
            for step in both:
                arrived(1, step)
                arrived(2, step)
                query_copy(step, peer).wait_recv()
            done = attend([(cross_in[0, step], k_half[step], v_half[step], None) for step in both])
            for step, (mixed, top, total) in zip(both, done):
                cross_out[0, step] = (mixed / total).astype(jnp.bfloat16)
                stat_out[step] = as_row(top + jnp.log2(total))
            for step in both:
                cross_copy(0, step, peer).start()
                stat_copy(step, peer).start()

        repeat(steps // 2, first_part)

        def near_items(step):
            return [
                (q_half[head], k_half[head], v_half[head], bias_own[...])
                for head in (2 * step, 2 * step + 1)
            ]

        def far_items(step):
            return [
                (q_half[2 * step + side], cross_in[1, step, part, :],
                 cross_in[2, step, part, :], bias_low[...])
                for side, part in enumerate((LOW, HIGH))
            ]

        def near_arrived(step):
            for head in (2 * step, 2 * step + 1):
                arrived(0, head)

        def far_arrived(step):
            cross_copy(2, step, peer).wait_recv()
            stat_copy(step, peer).wait_recv()

        def settle(step, near, far):
            logs = as_columns(jnp.where(by_query, stat_in[step], -1e30))
            heads = (2 * step, 2 * step + 1)
            for head, part, own, span in zip(heads, (LOW, HIGH), near, far):
                top = jnp.maximum(own[1], span[1])
                mine, theirs = jnp.exp2(own[1] - top), jnp.exp2(span[1] - top)
                mixed = own[0] * mine + span[0] * theirs
                total = own[2] * mine + span[2] * theirs
                o_half[head, LOW, :] = (mixed[LOW] / total[LOW]).astype(jnp.bfloat16)
                o_half[head, HIGH, :] = merge(
                    mixed[HIGH], top[HIGH], total[HIGH],
                    cross_in[2, step, part, :].astype(jnp.float32), logs[part],
                ).astype(jnp.bfloat16)
            for head in heads:
                result_copy(head, LOW, outer).start()
                result_local(head, HIGH).start()

        def second_part(turn):
            both = (2 * turn, 2 * turn + 1)
            for step in both:
                arrived(2, steps + step)
                cross_copy(1, step, peer).wait_recv()
            near_arrived(turn)
            done = attend([
                (cross_in[1, step], k_half[steps + step], v_half[steps + step], None)
                for step in both
            ] + near_items(turn))
            for step, (mixed, top, total) in zip(both, done):
                cross_out[2, step] = jnp.where(
                    by_query, (mixed / total).astype(jnp.bfloat16), v_half[steps + step]
                )
                stat_out[steps + step] = as_row(top + jnp.log2(total))
            for step in both:
                cross_copy(2, step, peer).start()
                stat_copy(steps + step, peer).start()
            far_arrived(turn)
            settle(turn, done[2:], attend(far_items(turn)))

        repeat(steps // 2, second_part)
        near_arrived(steps // 2)
        near = attend(near_items(steps // 2))
        for step in range(steps // 2, steps):
            if step + 1 < steps:
                near_arrived(step + 1)
            far_arrived(step)
            done = attend(far_items(step) + (near_items(step + 1) if step + 1 < steps else []))
            settle(step, near, done[:2])
            near = done[2:]

        def finish(step):
            for slot in range(3):
                cross_copy(slot, step, peer).wait_send()
            for side in range(2):
                stat_copy(2 * step + side, peer).wait_send()
                result_copy(2 * step + side, LOW, outer).wait_send()
                result_local(2 * step + side, HIGH).wait()

        repeat(steps, finish)

    @pl.when(me == 2)
    def _():
        peer, outer = me - 1, me + 1
        own_start(LOW)
        bias_own[...] = hidden(pair, pair, pair, pair, True)
        bias_high[...] = hidden(rows, rows, pair, pair, False)
        own_wait(LOW)

        def arrived(which, head):
            half_copy(which, head, HIGH, outer).wait_recv()

        def send_query(step):
            arrived(0, step)
            query_copy(step, peer).start()

        repeat(steps, send_query)

        def send_either(step):
            arrived(0, steps + step)
            for side, part in enumerate((LOW, HIGH)):
                cross_out[1, step, part, :] = jnp.where(
                    by_query, q_half[steps + step, part, :], k_half[2 * step + side, LOW, :]
                )
            cross_copy(1, step, peer).start()


        def give(heads):
            for head in heads:
                result_copy(head, HIGH, outer).start()
                result_local(head, LOW).start()

        def span_part(step):
            heads = (2 * step, 2 * step + 1)
            parts = (LOW, HIGH)
            cross_copy(1, step, peer).wait_recv()
            for head in heads:
                arrived(1, head)
                arrived(2, head)
            done = attend([
                (cross_in[1, step, part, :], k_half[head], v_half[head], bias_high[...])
                for head, part in zip(heads, parts)
            ])
            for head, part, (mixed, top, total) in zip(heads, parts, done):
                cross_out[2, step, part, :] = jnp.where(
                    by_query, (mixed / total).astype(jnp.bfloat16), v_half[head, LOW, :]
                )
            stat_out[step] = as_row(
                jnp.concatenate([top + jnp.log2(total) for mixed, top, total in done], axis=0)
            )
            cross_copy(2, step, peer).start()
            stat_copy(step, peer).start()

        def low_pair(turn):
            both = (2 * turn, 2 * turn + 1)
            near = attend([
                (q_half[step], k_half[step], v_half[step], bias_own[...]) for step in both
            ])
            for step in both:
                cross_copy(0, step, peer).wait_recv()
                stat_copy(step, peer).wait_recv()
            for step, own in zip(both, near):
                o_half[step] = merge(
                    *own, cross_in[0, step].astype(jnp.float32), as_columns(stat_in[step])
                ).astype(jnp.bfloat16)
            give(both)

        def high_near(turn):
            both = (2 * turn, 2 * turn + 1)
            near = attend([
                (q_half[steps + step], k_half[steps + step], v_half[steps + step], bias_own[...])
                for step in both
            ])
            for step, own in zip(both, near):
                for kind in range(3):
                    kept[kind, step] = jnp.broadcast_to(own[kind], (pair, HD))

        def high_pair(turn):
            both = (2 * turn, 2 * turn + 1)
            low = [scores_of(q_half[steps + step], cross_in[1, step]) for step in both]
            tops = [jnp.max(scores, axis=1, keepdims=True) for scores in low]
            low = [weigh(scores, top) for scores, top in zip(low, tops)]
            totals = [jnp.sum(weights, axis=1, keepdims=True) for weights in low]
            for step in both:
                cross_copy(2, step, peer).wait_recv()
                stat_copy(steps + step, peer).wait_recv()
            for step, weights, top, total in zip(both, low, tops, totals):
                other = jnp.where(
                    by_query, cross_in[2, step].astype(jnp.float32),
                    mix(weights, cross_in[2, step]) / total,
                )
                logs = jnp.where(
                    by_query, as_columns(stat_in[steps + step]),
                    jnp.broadcast_to(top + jnp.log2(total), (pair, HD)),
                )
                o_half[steps + step] = merge(
                    kept[0, step], kept[1, step], kept[2, step], other, logs
                ).astype(jnp.bfloat16)
            give([steps + step for step in both])

        def send_and_span(step):
            send_either(2 * step)
            send_either(2 * step + 1)
            span_part(step)

        quarter = steps // 2
        send_and_span(0)

        def early(turn):
            send_and_span(1 + turn)
            low_pair(turn)

        repeat(quarter - 1, early)
        span_part(quarter)
        low_pair(quarter - 1)
        high_near(0)

        def late(turn):
            span_part(quarter + 1 + turn)
            high_near(1 + turn)
            high_pair(turn)

        repeat(quarter - 2, late)
        span_part(steps - 1)
        high_pair(quarter - 2)
        high_near(quarter - 1)
        high_pair(quarter - 1)

        def finish(step):
            query_copy(step, peer).wait_send()
            for slot in (1, 2):
                cross_copy(slot, step, peer).wait_send()
            stat_copy(step, peer).wait_send()
            for side in range(2):
                result_copy(2 * step + side, HIGH, outer).wait_send()
                result_local(2 * step + side, LOW).wait()

        repeat(steps, finish)


def cut_body(queries, keys, values, span_starts):
    rows = queries.shape[0]
    pair = 2 * rows
    steps = HEADS // 2
    everything = pl.BlockSpec(memory_space=pltpu.HBM)
    dma = pltpu.SemaphoreType.DMA
    return pl.pallas_call(
        cut_kernel,
        out_shape=pltpu.VMEM(queries.shape, jnp.bfloat16),
        in_specs=[pl.BlockSpec(memory_space=pltpu.SMEM), everything, everything, everything],
        out_specs=pl.BlockSpec(memory_space=pl.ANY),
        scratch_shapes=[pltpu.VMEM((HEADS, pair, HD), jnp.bfloat16)] * 4
        + [pltpu.VMEM((3, steps, pair, HD), jnp.bfloat16)] * 2
        + [pltpu.VMEM((HEADS, 1, pair), jnp.float32)] * 2
        + [
            pltpu.VMEM((pair, pair), jnp.float32),
            pltpu.VMEM((pair, rows), jnp.float32),
            pltpu.VMEM((rows, pair), jnp.float32),
            pltpu.VMEM((3, steps, pair, HD), jnp.float32),
            dma((3, HEADS)), dma((3, HEADS)), dma((3, HEADS)),
            dma((3, steps)), dma((3, steps)),
            dma((HEADS,)), dma((HEADS,)),
            dma((HEADS,)), dma((HEADS,)), dma((HEADS,)),
        ],
        compiler_params=pltpu.CompilerParams(
            collective_id=0, has_side_effects=True, vmem_limit_bytes=56 * 1024 * 1024
        ),
    )(span_starts, queries, keys, values)


def chosen_body(count, queries, keys, values, span_starts):
    rows, images = queries.shape[0], span_starts.shape[0]
    if count == 4 and images == 1 and SPAN <= 2 * rows and rows % 16 == 0:
        return cut_body(queries, keys, values, span_starts)
    if count % 2 == 0 and HEADS % count == 0:
        return exchange_body(count, queries, keys, values, span_starts)
    return ring_body(queries, keys, values, span_starts)


def solution(mesh):
    body = functools.partial(chosen_body, mesh.shape["ctx"])
    placed = (P(("dp", "ctx"), None), P(("dp", "ctx"), None), P(("dp", "ctx"), None), P("dp"))
    return jax.shard_map(
        body, mesh=mesh, in_specs=placed, out_specs=P(("dp", "ctx"), None), check_vma=False
    )
```
